32 devices in a mesh: seq: 8 (over y, x, core), tp: 4 (over z).
Axes of the slice: x: 2, y: 2, z: 4, core: 2. Of those that a mesh axis runs over, the one named last changes fastest.
Arguments:
- tokens: bfloat16 [2, 4096, 2048], P(None, 'seq', 'tp'), may hold values from -6 to 6
- lengths: int32 [2, 3], replicated, may hold values from 1 to 3840, 4096 in all within a row
- pad_mask: int32 [2, 4096], P(None, 'seq'), may hold values 0 or 1
- gain_in: float32 [2048], replicated, may hold values from 0.5 to 1.5
- w_in: bfloat16 [2048, 3, 2048], P('seq', None, 'tp'), may hold values from -0.125 to 0.125
- conv_taps: float32 [3, 3, 2048], P(None, None, 'tp'), may hold values from -3 to 3
- log_rate: float32 [16, 2048], P(None, 'tp'), may hold values from -11 to -3.5
- pole_angle: float32 [16, 2048], P(None, 'tp'), may hold values from -0.3 to 0.3
- residues: float32 [2, 16, 2048], P(None, None, 'tp'), may hold values from -0.0625 to 0.0625
- skip_gain: float32 [2048], P('tp'), may hold values from -4 to 4
- w_out: bfloat16 [2048, 2048], P('tp', 'seq'), may hold values from -0.125 to 0.125
- gain_mlp: float32 [2048], replicated, may hold values from 0.5 to 1.5
- w_gu: bfloat16 [2048, 2, 5632], P('seq', None, 'tp'), may hold values from -0.125 to 0.125
- w_down: bfloat16 [5632, 2048], P('tp', 'seq'), may hold values from -0.078125 to 0.078125
- cotangent: bfloat16 [2, 4096, 2048], P(None, 'seq', 'tp'), may hold values from -6 to 6
Outputs:
- out: bfloat16 [2, 4096, 2048], P(None, 'seq', 'tp')
- d_tokens: bfloat16 [2, 4096, 2048], P(None, 'seq', 'tp')
- d_gain_in: float32 [2048], replicated
- d_w_in: float32 [2048, 3, 2048], P('seq', None, 'tp')
- d_conv_taps: float32 [3, 3, 2048], P(None, None, 'tp')
- d_log_rate: float32 [16, 2048], P(None, 'tp')
- d_pole_angle: float32 [16, 2048], P(None, 'tp')
- d_residues: float32 [2, 16, 2048], P(None, None, 'tp')
- d_skip_gain: float32 [2048], P('tp')
- d_w_out: float32 [2048, 2048], P('tp', 'seq')
- d_gain_mlp: float32 [2048], replicated
- d_w_gu: float32 [2048, 2, 5632], P('seq', None, 'tp')
- d_w_down: float32 [5632, 2048], P('tp', 'seq')
The draws below stay inside these ranges and needn't reach their ends.
Inputs may be any that keep to these rules, and one draw needn't show every extreme that they name: In each row the 3 lengths sum to 4096, and one of them is 3840.
All inputs are finite; a program needn't handle non-finite values. No bound on the sum of `pad_mask` on one device may be relied on, other than what follows from the above.
Results may differ from the reference program's by a relative error of at most 0.024.
Values may be sent and summed in bfloat16 or wider, within the bound.
No kernel may reach another device: no remote copies, remote signals or barrier semaphores. Data moves between devices by JAX's collectives and lax.ppermute only.
A program may use at most 256 MiB of HBM per device.

```python
import math
import jax
import jax.numpy as jnp
import numpy as np
from jax import lax

D = 2048
FF = 5632
NPOLE = 16
CH = 512
MB = 2
NDOC = 3
BLK = 64
STREAM = 4096
N_SEQ = 8


def place_ends(values, own_key, low, high):
    dims = values.shape
    index_at = [jax.random.randint(jax.random.fold_in(own_key, axis), (), 0, dims[axis]) for axis in range(len(dims))]
    values = values.at[tuple(index_at)].set(low)
    longest = dims.index(max(dims))
    index_at[longest] = (index_at[longest] + 1) % dims[longest]
    return values.at[tuple(index_at)].set(high)


def shard_levels(key, shape, cuts, smallest, largest):
    def one(dim, blocks):
        steps = jax.random.uniform(jax.random.fold_in(jax.random.fold_in(key, 6), dim), (blocks,), jnp.float32, smallest / len(cuts), largest / len(cuts))
        return jnp.repeat(jnp.exp(steps), shape[dim] // blocks).reshape((-1,) + (1,) * (len(shape) - dim - 1))

    factor_of = one(*cuts[0])
    for cut in cuts[1:]:
        factor_of = factor_of * one(*cut)
    return factor_of


def split_up(number_of, total, bound, slope):
    weights = [(1 << 20) // math.isqrt(grade ** slope) + 1 for grade in range(2, number_of + 1)]
    spare, given = total - bound - (number_of - 1), [1] * (number_of - 1)
    while spare > 0:
        movable = [i for i in range(number_of - 1) if given[i] < bound]
        mass, budget = sum([weights[i] for i in movable]), spare
        for i in movable:
            more = min(bound - given[i], max(1, budget * weights[i] // mass), spare)
            given[i] = given[i] + more
            spare = spare - more
    return np.array([bound] + given)


def uneven(rng, count, total, limit, lean):
    if count == 2:
        one = jax.random.randint(rng, (), max(1, total - limit), min(limit, total - 1) + 1)
        return jnp.stack([one, total - one])
    sizes = jnp.asarray(split_up(count, total, limit, lean), jnp.int32)
    couples = (count - 1) // 2
    source_of, sink = sizes[1:1 + 2 * couples:2], sizes[2:2 + 2 * couples:2]
    slack = jnp.minimum(source_of - 1, limit - sink)
    moved = jax.random.randint(jax.random.fold_in(rng, 1), (couples,), 0, 1 << 20) % (slack + 1)
    sizes = sizes.at[1:1 + 2 * couples:2].set(source_of - moved).at[2:2 + 2 * couples:2].set(sink + moved)
    return sizes[jax.random.permutation(jax.random.fold_in(rng, 2), count)]


def gaussian(rng, shape, scale, bound, cuts=(), kind=jnp.bfloat16):
    values = scale * jax.random.normal(rng, shape, jnp.float32)
    if cuts:
        values = values * shard_levels(rng, shape, cuts, -0.22, 0.18)
    return jnp.clip(values, -bound, bound).astype(kind)


def setup_inputs(seed: int = 0) -> dict:
    key_list = jax.random.split(jax.random.key(seed), 16)
    tokens = gaussian(key_list[0], (MB, STREAM, D), 1.0, 6.0, ((1, 8), (2, 4)))
    lengths = jax.vmap(lambda own: uneven(own, NDOC, STREAM, STREAM - CH // 2, 0))(jax.random.split(key_list[1], MB)).reshape((MB, NDOC)).astype(jnp.int32)
    pad_mask = place_ends((jax.random.randint(key_list[2], (MB, STREAM), 0, 8) < 7).astype(jnp.int32), jax.random.fold_in(key_list[2], 1), 0, 1)
    gain_in = jnp.clip(1.0 + 0.1 * jax.random.normal(key_list[3], (D,), jnp.float32), 0.5, 1.5)
    w_in = gaussian(key_list[4], (D, 3, D), D ** -0.5, 0.125, ((0, 8), (2, 4)))
    conv_taps = gaussian(key_list[5], (3, 3, D), 0.6, 3.0, ((2, 4),), jnp.float32)
    log_rate = jnp.clip(-11.0 + 7.5 * jax.random.uniform(key_list[6], (NPOLE, D), jnp.float32) ** shard_levels(key_list[6], (NPOLE, D), ((1, 4),), -0.2, 0.2), -11.0, -3.5)
    pole_angle = jnp.clip(jax.random.uniform(key_list[7], (NPOLE, D), jnp.float32, -0.3, 0.3) * shard_levels(key_list[7], (NPOLE, D), ((1, 4),), -0.4, 0.0), -0.3, 0.3)
    residues = gaussian(key_list[8], (2, NPOLE, D), (0.3 / (CH * N_SEQ) ** 0.5), 0.0625, ((2, 4),), jnp.float32)
    skip_gain = gaussian(key_list[9], (D,), 1.0, 4.0, ((0, 4),), jnp.float32)
    w_out = gaussian(key_list[10], (D, D), D ** -0.5, 0.125, ((0, 4), (1, 8)))
    gain_mlp = jnp.clip(1.0 + 0.1 * jax.random.normal(key_list[11], (D,), jnp.float32), 0.5, 1.5)
    w_gu = gaussian(key_list[12], (D, 2, FF), D ** -0.5, 0.125, ((0, 8), (2, 4)))
    w_down = gaussian(key_list[13], (FF, D), FF ** -0.5, 0.078125, ((0, 4), (1, 8)))
    cotangent = gaussian(key_list[14], (MB, STREAM, D), 1.0, 6.0, ((1, 8), (2, 4)))
    return dict(tokens=tokens, lengths=lengths, pad_mask=pad_mask, gain_in=gain_in, w_in=w_in, conv_taps=conv_taps, log_rate=log_rate, pole_angle=pole_angle, residues=residues, skip_gain=skip_gain, w_out=w_out, gain_mlp=gain_mlp, w_gu=w_gu, w_down=w_down, cotangent=cotangent)


highest = lax.Precision.HIGHEST
epsilon = 1e-06

@jax.custom_vjp
def low(v):
    return lax.optimization_barrier(v.astype(jnp.bfloat16)).astype(jnp.float32)

@jax.custom_vjp
def low_back(v):
    return v

def low_keep(v):
    return (low(v), None)

def low_pass(kept, grad):
    return (grad,)

def back_keep(v):
    return (v, None)

def back_low(kept, grad):
    return (low(grad),)
low.defvjp(low_keep, low_pass)
low_back.defvjp(back_keep, back_low)

def segment_number(position, doc_lengths):
    starts_at = (jnp.cumsum(doc_lengths) - doc_lengths).astype(jnp.int32)
    hits = (starts_at[None, :] <= position[:, None]).astype(jnp.int32)
    return lax.optimization_barrier(jnp.sum(hits, axis=1)).astype(jnp.int32)

def pole_powers(exponent, decay_rate, pole_angle):
    magnitude = jnp.exp(-exponent[:, None, None] * decay_rate[None])
    phase = exponent[:, None, None] * pole_angle[None]
    return (magnitude * jnp.cos(phase), magnitude * jnp.sin(phase))

def conv_block(carry_state, block_inputs, decay_rate, pole_angle, res_real, res_imag):
    inject, seg_block, seg_before = block_inputs
    block_len = inject.shape[0]
    exponent = jnp.arange(block_len).astype(jnp.float32)
    ker_real, ker_imag = pole_powers(exponent, decay_rate, pole_angle)
    kernel = lax.optimization_barrier(jnp.sum(res_real[None] * ker_real - res_imag[None] * ker_imag, axis=1))
    offset = jnp.arange(block_len)[:, None] - jnp.arange(block_len)[None, :]
    same_seg = jnp.logical_and(seg_block[:, None] == seg_block[None, :], offset >= 0)
    toeplitz = jnp.where(same_seg[:, :, None], kernel[jnp.clip(offset, 0, block_len - 1)], 0.0)
    y_inner = jnp.einsum('tsc,sc->tc', toeplitz, inject, precision=highest)
    carried = (seg_block == seg_before).astype(jnp.float32)
    next_real, next_imag = pole_powers(exponent + 1.0, decay_rate, pole_angle)
    state_real, state_imag = carry_state
    rs_real = res_real * state_real - res_imag * state_imag
    rs_imag = res_real * state_imag + res_imag * state_real
    y_cross = carried[:, None] * lax.optimization_barrier(jnp.sum(next_real * rs_real[None] - next_imag * rs_imag[None], axis=1))
    tail_mask = (seg_block == seg_block[block_len - 1]).astype(jnp.float32)
    end_real, end_imag = pole_powers(block_len - 1.0 - exponent, decay_rate, pole_angle)
    weighted = inject * tail_mask[:, None]
    sum_real = jnp.einsum('snc,sc->nc', end_real, weighted, precision=highest)
    sum_imag = jnp.einsum('snc,sc->nc', end_imag, weighted, precision=highest)
    full_real, full_imag = pole_powers(jnp.full((1,), block_len).astype(jnp.float32), decay_rate, pole_angle)
    keep_all = carried[block_len - 1]
    mult_real = keep_all * full_real[0]
    mult_imag = keep_all * full_imag[0]
    new_real = mult_real * state_real - mult_imag * state_imag + sum_real
    new_imag = mult_real * state_imag + mult_imag * state_real + sum_imag
    return ((new_real, new_imag), y_inner + y_cross)

def long_conv(inject, seg_all, decay_rate, pole_angle, res_real, res_imag):
    stream_len, width = inject.shape
    block_count = stream_len // BLK
    inject_blocks = inject.reshape(block_count, BLK, width)
    seg_blocks = seg_all.reshape(block_count, BLK)
    seg_befores = jnp.concatenate([jnp.zeros((1,), jnp.int32), seg_blocks[:-1, BLK - 1]])

    def advance(carry_state, block_inputs):
        return conv_block(carry_state, block_inputs, decay_rate, pole_angle, res_real, res_imag)
    zero_state = jnp.zeros((NPOLE, width), jnp.float32)
    end_state, y_blocks = lax.scan(jax.checkpoint(advance), (zero_state, zero_state), (inject_blocks, seg_blocks, seg_befores))
    return y_blocks.reshape(stream_len, width)

def short_conv(z_all, seg_all, conv_taps):
    total = conv_taps[0][None] * z_all
    for offset in (1, 2):
        shifted = jnp.concatenate([jnp.zeros((offset,) + z_all.shape[1:], jnp.float32), z_all[:-offset]])
        seg_shift = jnp.concatenate([jnp.zeros((offset,), jnp.int32), seg_all[:-offset]])
        valid = (seg_shift == seg_all).astype(jnp.float32)
        total = total + conv_taps[offset][None] * shifted * valid[:, None, None]
    return total

def rms_norm(values, gain):
    return values * lax.rsqrt(lax.optimization_barrier(jnp.mean(values * values, axis=-1, keepdims=True)) + epsilon) * gain

def block_forward(tokens, doc_lengths, pad_row, gain_in, w_in, conv_taps, log_rate, pole_angle, residues, skip_gain, w_out, gain_mlp, w_gu, w_down):
    position = jnp.arange(STREAM).astype(jnp.int32)
    seg_all = segment_number(position, doc_lengths)
    h_in = low(rms_norm(tokens, gain_in))
    z_all = jnp.dot(h_in, w_in.reshape(D, 3 * D), precision=highest).reshape(STREAM, 3, D)
    z_all = low(low_back(z_all))
    conv = short_conv(z_all, seg_all, conv_taps)
    inject = conv[:, 1] * conv[:, 2] * pad_row[:, None]
    conv_out = long_conv(inject, seg_all, jnp.exp(log_rate), pole_angle, residues[0], residues[1]) + skip_gain[None] * inject
    mixed = low(conv[:, 0] * conv_out)
    mixer = low_back(jnp.dot(mixed, w_out, precision=highest))
    x_mid = tokens + mixer
    h_mlp = low(rms_norm(x_mid, gain_mlp))
    gate_up = low_back(jnp.dot(h_mlp, w_gu.reshape(D, 2 * FF), precision=highest)).reshape(STREAM, 2, FF)
    act_low = low(jax.nn.silu(gate_up[:, 0]) * gate_up[:, 1])
    return x_mid + jnp.dot(act_low, w_down, precision=highest)

def reference(tokens, lengths, pad_mask, gain_in, w_in, conv_taps, log_rate, pole_angle, residues, skip_gain, w_out, gain_mlp, w_gu, w_down, cotangent):
    floats = [array.astype(jnp.float32) for array in (tokens, gain_in, w_in, conv_taps, log_rate, pole_angle, residues, skip_gain, w_out, gain_mlp, w_gu, w_down)]

    def forward(*params):
        tokens_f = params[0]
        rest = params[1:]
        results = [block_forward(tokens_f[micro_index], lengths[micro_index], pad_mask[micro_index].astype(jnp.float32), *rest) for micro_index in range(MB)]
        return jnp.stack(results)
    out_value, pull = jax.vjp(forward, *floats)
    grads = pull(cotangent.astype(jnp.float32))
    return (out_value.astype(jnp.bfloat16), grads[0].astype(jnp.bfloat16), grads[1], grads[2], grads[3], grads[4], grads[5], grads[6], grads[7], grads[8], grads[9], grads[10], grads[11])
```

```python
import functools

import jax
import jax.numpy as jnp
from jax import lax
from jax.experimental import pallas as pl
from jax.experimental.pallas import tpu as pltpu
from jax.sharding import PartitionSpec as P

EPS = 1e-06
SPAN = 64
STEP = 8
ROWS = 16
SUB, LANE = 8, 128
BF, F32 = jnp.bfloat16, jnp.float32
VMEM_LIMIT = 56 * 1024 * 1024


def keep_rows(z_ref, rim_ref, zs_ref):
    zs_ref[0:SUB, :] = rim_ref[...]

    def body(i, _):
        rows = pl.ds(pl.multiple_of(i * ROWS, ROWS), ROWS)
        zs_ref[pl.ds(pl.multiple_of(i * ROWS + SUB, SUB), ROWS), :] = z_ref[rows, :].astype(F32)
        return 0

    lax.fori_loop(0, z_ref.shape[0] // ROWS, body, 0)


def window(zs_ref, i, stream, width):
    rows = pl.ds(pl.multiple_of(i * ROWS, ROWS), ROWS + SUB)
    wide = zs_ref[rows, stream * width : (stream + 1) * width]
    return wide[8 : 8 + ROWS], wide[7 : 7 + ROWS], wide[6 : 6 + ROWS]


def filtered(zs_ref, taps_ref, cols, i, stream, width):
    z0, z1, z2 = window(zs_ref, i, stream, width)
    t0, t1, t2 = (taps_ref[lag * 3 + stream : lag * 3 + stream + 1, :] for lag in range(3))
    return t0 * z0 + (t1 * z1) * cols[:, 0:1] + (t2 * z2) * cols[:, 1:2]


def spread(ref, i, value):
    parts = value.shape[1] // LANE
    for c in range(parts):
        piece = value[:, c * LANE : (c + 1) * LANE]
        for half in range(SUB // parts):
            ref[pl.ds(i * (ROWS * SUB) + half * parts + c, ROWS, stride=SUB), :] = piece


def collect(ref, i, width):
    parts = width // LANE
    pieces = []
    for c in range(parts):
        piece = ref[pl.ds(i * (ROWS * SUB) + c, ROWS, stride=SUB), :]
        for half in range(1, SUB // parts):
            piece = piece + ref[pl.ds(i * (ROWS * SUB) + half * parts + c, ROWS, stride=SUB), :]
        pieces.append(piece)
    return jnp.concatenate(pieces, axis=1)


def chunk_cols(cols_ref, i):
    return cols_ref[pl.ds(pl.multiple_of(i * ROWS, ROWS), ROWS), :]


def at(group, j):
    return pl.ds(pl.multiple_of((group * STEP + j) * SUB, SUB), SUB)


def by_flag(flag, step):
    @pl.when(flag == 0)
    def _():
        step(False)

    @pl.when(flag != 0)
    def _():
        step(True)


def front_kernel(keep_ref, flag_ref, z_ref, rim_ref, taps_ref, cols_ref, lam_ref,
                 u_ref, end_ref, zs_ref):
    count, width = z_ref.shape[0], z_ref.shape[1] // 3
    poles = lam_ref.shape[0] // 2
    keep_rows(z_ref, rim_ref, zs_ref)

    def natural(i, _):
        cols = chunk_cols(cols_ref, i)
        key = filtered(zs_ref, taps_ref, cols, i, 1, width)
        value = filtered(zs_ref, taps_ref, cols, i, 2, width)
        spread(u_ref, i, key * value * cols[:, 2:3])
        return 0

    lax.fori_loop(0, count // ROWS, natural, 0)
    end_ref[...] = jnp.zeros_like(end_ref)

    def scan(group, _):
        def step(masked):
            us = [u_ref[at(group, j), :] for j in range(STEP)]
            for k in range(poles):
                lr, li = lam_ref[k], lam_ref[poles + k]
                sr, si = end_ref[k], end_ref[poles + k]
                for j in range(STEP):
                    if masked:
                        keep = keep_ref[group * STEP + j]
                        sr, si = sr * keep, si * keep
                    sr, si = lr * sr - li * si + us[j], lr * si + li * sr
                end_ref[k], end_ref[poles + k] = sr, si

        by_flag(flag_ref[group], step)
        return 0

    lax.fori_loop(0, count // STEP, scan, 0)


def joined(all_ref, full_ref, carry_ref, spans_ref, me, count, conj):
    poles = full_ref.shape[0] // 2
    carry_ref[...] = jnp.zeros_like(carry_ref)

    def hop(order, _):
        j = count - 1 - order if conj else order
        span = spans_ref[j]
        for k in range(poles):
            lr, li = full_ref[k] * span, full_ref[poles + k] * (-span if conj else span)
            sr, si = carry_ref[k], carry_ref[poles + k]
            carry_ref[k] = lr * sr - li * si + all_ref[j, k]
            carry_ref[poles + k] = lr * si + li * sr + all_ref[j, poles + k]
        return 0

    lax.fori_loop(0, count - 1 - me if conj else me, hop, 0)


def finish_kernel(keep_ref, flag_ref, spans_ref, me_ref, z_ref, rim_ref, taps_ref, cols_ref,
                  lam_ref, full_ref, res_ref, skip_ref, u_ref, ends_ref,
                  mixed_ref, conv_ref, marks_ref, zs_ref, y_ref, st_ref):
    count, width = z_ref.shape[0], z_ref.shape[1] // 3
    poles = lam_ref.shape[0] // 2
    keep_rows(z_ref, rim_ref, zs_ref)
    joined(ends_ref, full_ref, st_ref, spans_ref, me_ref[0], ends_ref.shape[0], False)

    def scan(group, _):
        @pl.when(group % (SPAN // STEP) == 0)
        def _():
            marks_ref[group // (SPAN // STEP)] = st_ref[...]

        def step(masked):
            us = [u_ref[at(group, j), :] for j in range(STEP)]
            ys = [None] * STEP
            for k in range(poles):
                lr, li = lam_ref[k], lam_ref[poles + k]
                rr, ri = res_ref[k], res_ref[poles + k]
                sr, si = st_ref[k], st_ref[poles + k]
                for j in range(STEP):
                    if masked:
                        keep = keep_ref[group * STEP + j]
                        sr, si = sr * keep, si * keep
                    sr, si = lr * sr - li * si + us[j], lr * si + li * sr
                    part = rr * sr - ri * si
                    ys[j] = part if ys[j] is None else ys[j] + part
                st_ref[k], st_ref[poles + k] = sr, si
            for j in range(STEP):
                y_ref[at(group, j), :] = ys[j]

        by_flag(flag_ref[group], step)
        return 0

    lax.fori_loop(0, count // STEP, scan, 0)

    def natural(i, _):
        rows = pl.ds(pl.multiple_of(i * ROWS, ROWS), ROWS)
        cols = chunk_cols(cols_ref, i)
        query = filtered(zs_ref, taps_ref, cols, i, 0, width)
        key = filtered(zs_ref, taps_ref, cols, i, 1, width)
        value = filtered(zs_ref, taps_ref, cols, i, 2, width)
        conv = collect(y_ref, i, width) + skip_ref[...] * (key * value * cols[:, 2:3])
        conv_ref[rows, :] = conv
        mixed_ref[rows, :] = (query * conv).astype(BF)
        return 0

    lax.fori_loop(0, count // ROWS, natural, 0)


def adjoint_kernel(keep_ref, flag_ref, z_ref, rim_ref, taps_ref, cols_ref, lam_ref, dmix_ref,
                   e_ref, end_ref, zs_ref):
    count, width = z_ref.shape[0], z_ref.shape[1] // 3
    poles = lam_ref.shape[0] // 2
    keep_rows(z_ref, rim_ref, zs_ref)

    def natural(i, _):
        rows = pl.ds(pl.multiple_of(i * ROWS, ROWS), ROWS)
        query = filtered(zs_ref, taps_ref, chunk_cols(cols_ref, i), i, 0, width)
        spread(e_ref, i, dmix_ref[rows, :].astype(F32) * query)
        return 0

    lax.fori_loop(0, count // ROWS, natural, 0)
    end_ref[...] = jnp.zeros_like(end_ref)

    def scan(order, _):
        group = count // STEP - 1 - order

        def step(masked):
            es = [e_ref[at(group, j), :] for j in range(STEP)]
            for k in range(poles):
                lr, li = lam_ref[k], lam_ref[poles + k]
                br, bi = end_ref[k], end_ref[poles + k]
                for j in reversed(range(STEP)):
                    if masked:
                        keep = keep_ref[group * STEP + j + 1]
                        br, bi = br * keep, bi * keep
                    br, bi = lr * br + li * bi + es[j], lr * bi - li * br
                end_ref[k], end_ref[poles + k] = br, bi

        by_flag(flag_ref[group] + flag_ref[group + 1], step)
        return 0

    lax.fori_loop(0, count // STEP, scan, 0)


def back_kernel(keep_ref, flag_ref, spans_ref, me_ref, z_ref, rim_ref, taps_ref, cols_ref,
                lam_ref, full_ref, res_ref, skip_ref, u_ref, e_ref, dmix_ref, conv_ref,
                marks_ref, ends_ref,
                dz_ref, rimback_ref, tail_ref, dtaps_ref, dskip_ref, dres_ref, g_ref,
                zs_ref, dc_ref, di_ref, ss_ref, bt_ref):
    count, width = z_ref.shape[0], z_ref.shape[1] // 3
    poles = lam_ref.shape[0] // 2
    state_rows = 2 * poles * SUB
    keep_rows(z_ref, rim_ref, zs_ref)
    joined(ends_ref, full_ref, bt_ref, spans_ref, me_ref[0], ends_ref.shape[0], True)
    bt_ref[...] = bt_ref[...] * keep_ref[count]
    for ref in (dtaps_ref, dskip_ref, dres_ref, g_ref):
        ref[...] = jnp.zeros_like(ref)

    def held(slot, k):
        return pl.ds(pl.multiple_of(slot * state_rows + k * SUB, SUB), SUB)

    def block(order, _):
        number = count // SPAN - 1 - order
        for k in range(2 * poles):
            ss_ref[held(0, k), :] = marks_ref[number, k]

        def forward(inner, _):
            group = number * (SPAN // STEP) + inner

            def step(masked):
                us = [u_ref[at(group, j), :] for j in range(STEP)]
                es = [e_ref[at(group, j), :] for j in range(STEP)]
                for k in range(poles):
                    lr, li = lam_ref[k], lam_ref[poles + k]
                    sr = ss_ref[held(inner * STEP, k), :]
                    si = ss_ref[held(inner * STEP, poles + k), :]
                    ar = ai = None
                    for j in range(STEP):
                        if masked:
                            keep = keep_ref[group * STEP + j]
                            sr, si = sr * keep, si * keep
                        sr, si = lr * sr - li * si + us[j], lr * si + li * sr
                        ss_ref[held(inner * STEP + j + 1, k), :] = sr
                        ss_ref[held(inner * STEP + j + 1, poles + k), :] = si
                        ar = es[j] * sr if ar is None else ar + es[j] * sr
                        ai = es[j] * si if ai is None else ai + es[j] * si
                    dres_ref[k] = dres_ref[k] + ar
                    dres_ref[poles + k] = dres_ref[poles + k] + ai

            by_flag(flag_ref[group], step)
            return 0

        lax.fori_loop(0, SPAN // STEP, forward, 0)

        def backward(outer, _):
            inner = SPAN // STEP - 1 - outer
            group = number * (SPAN // STEP) + inner

            def step(masked):
                es = [e_ref[at(group, j), :] for j in range(STEP)]
                ds = [None] * STEP
                for k in range(poles):
                    lr, li = lam_ref[k], lam_ref[poles + k]
                    rr, ri = res_ref[k], res_ref[poles + k]
                    tr, ti = bt_ref[k], bt_ref[poles + k]
                    gr, gi = g_ref[k], g_ref[poles + k]
                    for j in reversed(range(STEP)):
                        tr, ti = lr * tr + li * ti + es[j], lr * ti - li * tr
                        part = rr * tr + ri * ti
                        ds[j] = part if ds[j] is None else ds[j] + part
                        if masked:
                            keep = keep_ref[group * STEP + j]
                            tr, ti = tr * keep, ti * keep
                        sr = ss_ref[held(inner * STEP + j, k), :]
                        si = ss_ref[held(inner * STEP + j, poles + k), :]
                        gr = gr + (sr * tr + si * ti)
                        gi = gi + (sr * ti - si * tr)
                    bt_ref[k], bt_ref[poles + k] = tr, ti
                    g_ref[k], g_ref[poles + k] = gr, gi
                for j in range(STEP):
                    di_ref[at(group, j), :] = ds[j]

            by_flag(flag_ref[group], step)
            return 0

        lax.fori_loop(0, SPAN // STEP, backward, 0)
        return 0

    lax.fori_loop(0, count // SPAN, block, 0)

    def eighths(value):
        total = value[0:SUB]
        for start in range(SUB, ROWS, SUB):
            total = total + value[start : start + SUB]
        return total

    def natural(i, _):
        rows = pl.ds(pl.multiple_of(i * ROWS, ROWS), ROWS)
        cols = chunk_cols(cols_ref, i)
        query = filtered(zs_ref, taps_ref, cols, i, 0, width)
        key = filtered(zs_ref, taps_ref, cols, i, 1, width)
        value = filtered(zs_ref, taps_ref, cols, i, 2, width)
        mask = cols[:, 2:3]
        d_mixed = dmix_ref[rows, :].astype(F32)
        e = d_mixed * query
        dskip_ref[...] = dskip_ref[...] + eighths(e * (key * value * mask))
        d_inject = (collect(di_ref, i, width) + skip_ref[...] * e) * mask
        for stream, grad in enumerate((d_mixed * conv_ref[rows, :], d_inject * value, d_inject * key)):
            lanes = slice(stream * width, (stream + 1) * width)
            dc_ref[rows, lanes] = grad
            shifted = window(zs_ref, i, stream, width)
            for lag in range(3):
                product = grad * shifted[lag]
                if lag:
                    product = product * cols[:, lag - 1 : lag]
                slot = slice((lag * 3 + stream) * SUB, (lag * 3 + stream + 1) * SUB)
                dtaps_ref[slot, :] = dtaps_ref[slot, :] + eighths(product)
        return 0

    lax.fori_loop(0, count // ROWS, natural, 0)
    dc_ref[count : count + SUB, :] = jnp.zeros((SUB, 3 * width), F32)

    def spread_back(i, _):
        rows = pl.ds(pl.multiple_of(i * ROWS, ROWS), ROWS)
        beyond = pl.ds(pl.multiple_of(i * ROWS, ROWS), ROWS + SUB)
        cols = cols_ref[beyond, :]
        v1, v2 = cols[1 : 1 + ROWS, 0:1], cols[2 : 2 + ROWS, 1:2]
        for stream in range(3):
            lanes = slice(stream * width, (stream + 1) * width)
            wide = dc_ref[beyond, lanes]
            t0, t1, t2 = (taps_ref[lag * 3 + stream : lag * 3 + stream + 1, :] for lag in range(3))
            total = t0 * wide[0:ROWS] + (t1 * wide[1 : 1 + ROWS]) * v1 + (t2 * wide[2 : 2 + ROWS]) * v2
            dz_ref[rows, lanes] = total.astype(BF)

            @pl.when(i == count // ROWS - 1)
            def _():
                tail_ref[:, lanes] = total

        return 0

    lax.fori_loop(0, count // ROWS, spread_back, 0)
    first = cols_ref[0:SUB, :]
    for stream in range(3):
        lanes = slice(stream * width, (stream + 1) * width)
        dc = dc_ref[0:SUB, lanes]
        t1, t2 = (taps_ref[lag * 3 + stream : lag * 3 + stream + 1, :] for lag in (1, 2))
        one, two = t1 * (dc * first[:, 0:1]), t2 * (dc * first[:, 1:2])
        rimback_ref[...] = rimback_ref[...] if stream else jnp.zeros_like(rimback_ref)
        rimback_ref[0:1, lanes] = two[0:1]
        rimback_ref[1:2, lanes] = one[0:1] + two[1:2]


def call(kernel, ins, outs, scratch, smem, name, flops):
    vmem = pl.BlockSpec(memory_space=pltpu.VMEM)
    scalar = pl.BlockSpec(memory_space=pltpu.SMEM)
    moved = sum(a.size * a.dtype.itemsize for a in ins) + sum(
        functools.reduce(lambda x, y: x * y, s) * jnp.dtype(d).itemsize for s, d in outs
    )
    return pl.pallas_call(
        kernel,
        out_shape=[jax.ShapeDtypeStruct(s, d) for s, d in outs],
        in_specs=[scalar] * smem + [vmem] * (len(ins) - smem),
        out_specs=[vmem] * len(outs),
        scratch_shapes=[pltpu.VMEM(s, d) for s, d in scratch],
        compiler_params=pltpu.CompilerParams(vmem_limit_bytes=VMEM_LIMIT),
        cost_estimate=pl.CostEstimate(flops=flops, bytes_accessed=moved, transcendentals=0),
        name=name,
    )(*ins)


def segment_number(position, doc_lengths):
    starts_at = jnp.cumsum(doc_lengths) - doc_lengths
    hits = (starts_at[None, :] <= position[:, None]).astype(jnp.int32)
    return jnp.sum(hits, axis=1)


def norm_scale(values):
    return lax.rsqrt(jnp.mean(values * values, axis=-1, keepdims=True) + EPS)


def norm_back(values, scale, gain, grad):
    weighted = gain[None] * grad
    d_values = scale * weighted - values * scale**3 * jnp.mean(
        weighted * values, axis=-1, keepdims=True
    )
    return d_values, jnp.sum(grad * values * scale, axis=0)


def polar(exponent, decay_rate, pole_angle):
    magnitude = jnp.exp(-exponent * decay_rate)
    phase = exponent * pole_angle
    return magnitude * jnp.cos(phase), magnitude * jnp.sin(phase)


def packed(real, imag):
    rows = real.size // (SUB * LANE)
    return jnp.concatenate([real.reshape(rows, SUB, LANE), imag.reshape(rows, SUB, LANE)])


def unpacked(pair, shape):
    half = pair.shape[0] // 2
    return pair[:half].reshape(shape), pair[half:].reshape(shape)


def gather(block, axis, dim):
    return lax.all_gather(block, axis, axis=dim, tiled=True)


def scatter(block, axis, dim):
    return lax.psum_scatter(block, axis, scatter_dimension=dim, tiled=True)


def dot(a, b, dims):
    return lax.dot_general(a, b, (dims, ((), ())), preferred_element_type=F32)


def shards(tokens, lengths, pad_mask, gain_in, w_in, conv_taps, log_rate, pole_angle, residues,
           skip_gain, w_out, gain_mlp, w_gu, w_down, cotangent):
    micros, count, width = tokens.shape
    n_seq, n_tp = lax.axis_size("seq"), lax.axis_size("tp")
    me = lax.axis_index("seq")
    hidden = w_gu.shape[2]
    x_own = [tokens[m] for m in range(micros)]
    x_full = [gather(x, "tp", 1) for x in x_own]
    in_full = gather(w_in.reshape(w_in.shape[0], -1), "seq", 0)
    out_full = gather(gather(w_out, "seq", 1), "tp", 0)
    gu_full = gather(w_gu.reshape(w_gu.shape[0], -1), "seq", 0)
    down_full = gather(w_down, "seq", 1)
    cot_full = gather(cotangent, "tp", 2)

    rate = jnp.exp(log_rate)
    lam_real, lam_imag = polar(1.0, rate, pole_angle)
    lam = packed(lam_real, lam_imag)
    lam_all = packed(*polar(float(count), rate, pole_angle))
    res = packed(residues[0], residues[1])
    taps = conv_taps.reshape(9, width)
    skip = skip_gain.reshape(1, width)
    me_word = me.astype(jnp.int32).reshape(1)
    edges = jnp.arange(n_seq + 1) * count
    seq_shape = (count * SUB, LANE)
    st_shape = lam.shape
    work = lam.shape[0] * SUB * LANE * count

    kept = []
    outputs = []
    for m in range(micros):
        position = me * count + jnp.arange(-2, count + 1)
        seg = segment_number(position, lengths[m])
        valid1 = (seg[2:] == seg[1:-1]).astype(F32)
        valid1 = valid1.at[count].multiply((me < n_seq - 1).astype(F32))
        valid2 = (seg[2:-1] == seg[:-3]).astype(F32)
        mask = pad_mask[m].astype(F32)
        cols = jnp.zeros((count + SUB, SUB), F32)
        cols = cols.at[:count, 0].set(valid1[:count]).at[:count, 1].set(valid2).at[:count, 2].set(mask)
        keep = jnp.concatenate([valid1, jnp.zeros((SUB - 1,), F32)])
        flags = jnp.any(keep.reshape(-1, STEP) == 0, axis=1).astype(jnp.int32)
        last, first = segment_number(edges - 1, lengths[m]), segment_number(edges, lengths[m])
        spans = (last[1:] == last[:-1]).astype(F32)
        spans_back = (first[1:] == first[:-1]).astype(F32)

        x_wide = x_full[m].astype(F32)
        h_in = (x_wide * norm_scale(x_wide) * gain_in[None]).astype(BF)
        z_low = dot(h_in, in_full, ((1,), (0,))).astype(BF)
        rim = lax.ppermute(z_low[count - 2 :], "seq", [(i, i + 1) for i in range(n_seq - 1)])
        rim = jnp.concatenate([jnp.zeros((SUB - 2, 3 * width), F32), rim.astype(F32)])
        base = (z_low, rim, taps, cols, lam)
        zs = ((count + SUB, 3 * width), F32)
        u, end = call(front_kernel, (keep, flags, *base), [(seq_shape, F32), (st_shape, F32)],
                      [zs], 2, "mixer_front", 4 * work)
        ends = lax.all_gather(end, "seq")
        mixed, conv_out, marks = call(
            finish_kernel,
            (keep, flags, spans, me_word, *base, lam_all, res, skip, u, ends),
            [((count, width), BF), ((count, width), F32), ((count // SPAN, *st_shape), F32)],
            [zs, (seq_shape, F32), (st_shape, F32)], 4, "mixer_finish", 6 * work,
        )
        mixed_full = gather(mixed, "tp", 1)
        x_mid = x_wide + dot(mixed_full, out_full, ((1,), (0,)))
        scale_mid = norm_scale(x_mid)
        h_mlp = (x_mid * scale_mid * gain_mlp[None]).astype(BF)
        gate_up = dot(h_mlp, gu_full, ((1,), (0,)))
        gate, up = gate_up[:, :hidden], gate_up[:, hidden:]
        sig = jax.nn.sigmoid(gate)
        act = (gate * sig * up).astype(BF)
        down_own = scatter(dot(act, down_full, ((1,), (0,))).astype(BF), "tp", 1)
        mid_own = lax.dynamic_slice_in_dim(x_mid, lax.axis_index("tp") * width, width, 1)
        outputs.append((mid_own + down_own.astype(F32)).astype(BF))

        cot = cot_full[m]
        d_act = dot(cot, down_full, ((1,), (1,)))
        d_gu = jnp.concatenate(
            [d_act * up * sig * (1.0 + gate * (1.0 - sig)), d_act * gate * sig], axis=1
        ).astype(BF)
        d_h = dot(d_gu, gu_full, ((1,), (1,)))
        d_norm, d_gain_mlp = norm_back(x_mid, scale_mid, gain_mlp, d_h)
        d_mid = d_norm + cot.astype(F32) * (1.0 / n_tp)
        d_low = d_mid.astype(BF)
        d_mixed = scatter(dot(d_low, out_full, ((1,), (1,))).astype(BF), "tp", 1)
        kept.append(dict(
            base=base, zs=zs, keep=keep, flags=flags, spans=spans_back, u=u, conv=conv_out,
            marks=marks, mixed=mixed_full, h_mlp=h_mlp, act=act, d_gu=d_gu, d_mid=d_mid,
            d_low=d_low, d_mixed=d_mixed, x_wide=x_wide, h_in=h_in, d_gain_mlp=d_gain_mlp,
        ))

    token_grads = []
    smalls = []
    for m in range(micros):
        c = kept[m]
        base, zs, u, d_mixed = c["base"], c["zs"], c["u"], c["d_mixed"]
        e, end = call(adjoint_kernel, (c["keep"], c["flags"], *base, d_mixed),
                      [(seq_shape, F32), (st_shape, F32)], [zs], 2, "mixer_adjoint", 4 * work)
        ends = lax.all_gather(end, "seq")
        d_z, rim_back, tail, d_taps, d_skip, d_res, d_lam = call(
            back_kernel,
            (c["keep"], c["flags"], c["spans"], me_word, *base, lam_all, res, skip, u, e, d_mixed,
             c["conv"], c["marks"], ends),
            [((count, 3 * width), BF), ((SUB, 3 * width), F32), ((ROWS, 3 * width), F32),
             ((9 * SUB, width), F32), ((SUB, width), F32), (st_shape, F32), (st_shape, F32)],
            [zs, ((count + SUB, 3 * width), F32), (seq_shape, F32),
             (((SPAN + 1) * st_shape[0] * SUB, LANE), F32), (st_shape, F32)],
            4, "mixer_back", 16 * work,
        )
        rim_back = lax.ppermute(rim_back[:2], "seq", [(i + 1, i) for i in range(n_seq - 1)])
        tail = (tail + jnp.concatenate([jnp.zeros((ROWS - 2, 3 * width), F32), rim_back])).astype(BF)
        d_z = lax.dynamic_update_slice(d_z, tail, (count - ROWS, 0))
        d_h_in = dot(d_z, in_full, ((1,), (1,)))
        d_norm, d_gain_in = norm_back(c["x_wide"], norm_scale(c["x_wide"]), gain_in, d_h_in)
        token_grads.append(scatter((c["d_mid"] + d_norm).astype(BF), "tp", 1))
        g_real, g_imag = unpacked(d_lam, log_rate.shape)
        s_real, s_imag = unpacked(d_res, log_rate.shape)
        h_real = residues[0] * g_real + residues[1] * g_imag
        h_imag = residues[0] * g_imag - residues[1] * g_real
        c["d_z"] = d_z
        smalls.append(jnp.concatenate([
            jnp.sum(d_taps.reshape(9, SUB, width), axis=1),
            -rate * (lam_real * h_real + lam_imag * h_imag),
            lam_real * h_imag - lam_imag * h_real,
            s_real, -s_imag,
            jnp.sum(d_skip, axis=0, keepdims=True),
            d_gain_in.reshape(-1, width), c["d_gain_mlp"].reshape(-1, width),
        ]))

    def both(name):
        return jnp.concatenate([c[name] for c in kept])

    rows = ((0,), (0,))
    g_down = scatter(dot(both("act"), cot_full.reshape(micros * count, -1), rows).astype(BF), "seq", 1)
    g_gu = scatter(dot(both("h_mlp"), both("d_gu"), rows).astype(BF), "seq", 0)
    g_out = scatter(dot(both("mixed"), both("d_low"), rows).astype(BF), "seq", 1)
    g_out = scatter(g_out, "tp", 0)
    g_in = scatter(dot(both("h_in"), both("d_z"), rows).astype(BF), "seq", 0)

    small = sum(smalls)
    small = jnp.sum(lax.all_gather(small.astype(BF), "seq").astype(F32), axis=0)
    n_gain = 2 * (gain_in.shape[0] // width)
    n_pole = log_rate.shape[0]
    gains = jnp.sum(lax.all_gather(small[-n_gain:].astype(BF), "tp").astype(F32), axis=0)
    cuts = [9, 9 + n_pole, 9 + 2 * n_pole, 9 + 3 * n_pole, 9 + 4 * n_pole]
    return (
        jnp.stack(outputs),
        jnp.stack(token_grads),
        gains[: n_gain // 2].reshape(-1),
        g_in.astype(F32).reshape(w_in.shape),
        small[: cuts[0]].reshape(conv_taps.shape),
        small[cuts[0] : cuts[1]],
        small[cuts[1] : cuts[2]],
        small[cuts[2] : cuts[4]].reshape(residues.shape),
        small[cuts[4]],
        g_out.astype(F32),
        gains[n_gain // 2 :].reshape(-1),
        g_gu.astype(F32).reshape(w_gu.shape),
        g_down.astype(F32),
    )


def solution(mesh):
    wide, deep, flat = P(None, "seq", "tp"), P("seq", None, "tp"), P("tp", "seq")
    poles, taps = P(None, "tp"), P(None, None, "tp")
    return jax.shard_map(
        shards,
        mesh=mesh,
        in_specs=(wide, P(), P(None, "seq"), P(), deep, taps, poles, poles, taps, P("tp"), flat,
                  P(), deep, flat, wide),
        out_specs=(wide, wide, P(), deep, taps, poles, poles, taps, P("tp"), flat, P(), deep, flat),
        check_vma=False,
    )
```

```python
import functools

import jax
import jax.numpy as jnp
from jax import lax
from jax.experimental import pallas as pl
from jax.experimental.pallas import tpu as pltpu
from jax.sharding import PartitionSpec as P

EPS = 1e-06
SPAN = 64
STEP = 8
ROWS = 16
SUB, LANE = 8, 128
BF, F32 = jnp.bfloat16, jnp.float32
VMEM_LIMIT = 56 * 1024 * 1024


def keep_rows(z_ref, rim_ref, zs_ref):
    zs_ref[0:SUB, :] = rim_ref[...]

    def body(i, _):
        rows = pl.ds(pl.multiple_of(i * ROWS, ROWS), ROWS)
        zs_ref[pl.ds(pl.multiple_of(i * ROWS + SUB, SUB), ROWS), :] = z_ref[rows, :].astype(F32)
        return 0

    lax.fori_loop(0, z_ref.shape[0] // ROWS, body, 0)


def window(zs_ref, i, stream, width):
    rows = pl.ds(pl.multiple_of(i * ROWS, ROWS), ROWS + SUB)
    wide = zs_ref[rows, stream * width : (stream + 1) * width]
    return wide[8 : 8 + ROWS], wide[7 : 7 + ROWS], wide[6 : 6 + ROWS]


def filtered(zs_ref, taps_ref, cols, i, stream, width):
    z0, z1, z2 = window(zs_ref, i, stream, width)
    t0, t1, t2 = (taps_ref[lag * 3 + stream : lag * 3 + stream + 1, :] for lag in range(3))
    return t0 * z0 + (t1 * z1) * cols[:, 0:1] + (t2 * z2) * cols[:, 1:2]


def spread(ref, i, value):
    parts = value.shape[1] // LANE
    for c in range(parts):
        piece = value[:, c * LANE : (c + 1) * LANE]
        for half in range(SUB // parts):
            ref[pl.ds(i * (ROWS * SUB) + half * parts + c, ROWS, stride=SUB), :] = piece


def collect(ref, i, width):
    parts = width // LANE
    pieces = []
    for c in range(parts):
        piece = ref[pl.ds(i * (ROWS * SUB) + c, ROWS, stride=SUB), :]
        for half in range(1, SUB // parts):
            piece = piece + ref[pl.ds(i * (ROWS * SUB) + half * parts + c, ROWS, stride=SUB), :]
        pieces.append(piece)
    return jnp.concatenate(pieces, axis=1)


def chunk_cols(cols_ref, i):
    return cols_ref[pl.ds(pl.multiple_of(i * ROWS, ROWS), ROWS), :]


def at(group, j):
    return pl.ds(pl.multiple_of((group * STEP + j) * SUB, SUB), SUB)


def by_flag(flag, step):
    @pl.when(flag == 0)
    def _():
        step(False)

    @pl.when(flag != 0)
    def _():
        step(True)


def front_kernel(keep_ref, flag_ref, z_ref, rim_ref, taps_ref, cols_ref, lam_ref,
                 u_ref, end_ref, zs_ref):
    count, width = z_ref.shape[0], z_ref.shape[1] // 3
    poles = lam_ref.shape[0] // 2
    keep_rows(z_ref, rim_ref, zs_ref)

    def natural(i, _):
        cols = chunk_cols(cols_ref, i)
        key = filtered(zs_ref, taps_ref, cols, i, 1, width)
        value = filtered(zs_ref, taps_ref, cols, i, 2, width)
        spread(u_ref, i, key * value * cols[:, 2:3])
        return 0

    lax.fori_loop(0, count // ROWS, natural, 0)
    end_ref[...] = jnp.zeros_like(end_ref)

    def scan(group, _):
        def step(masked):
            us = [u_ref[at(group, j), :] for j in range(STEP)]
            for k in range(poles):
                lr, li = lam_ref[k], lam_ref[poles + k]
                sr, si = end_ref[k], end_ref[poles + k]
                for j in range(STEP):
                    if masked:
                        keep = keep_ref[group * STEP + j]
                        sr, si = sr * keep, si * keep
                    sr, si = lr * sr - li * si + us[j], lr * si + li * sr
                end_ref[k], end_ref[poles + k] = sr, si

        by_flag(flag_ref[group], step)
        return 0

    lax.fori_loop(0, count // STEP, scan, 0)


def joined(all_ref, micro, full_ref, carry_ref, spans_ref, me, count, conj):
    poles = full_ref.shape[0] // 2
    carry_ref[...] = jnp.zeros_like(carry_ref)

    def hop(order, _):
        j = count - 1 - order if conj else order
        span = spans_ref[j]
        for k in range(poles):
            lr, li = full_ref[k] * span, full_ref[poles + k] * (-span if conj else span)
            sr, si = carry_ref[k], carry_ref[poles + k]
            carry_ref[k] = lr * sr - li * si + all_ref[j, micro, k]
            carry_ref[poles + k] = lr * si + li * sr + all_ref[j, micro, poles + k]
        return 0

    lax.fori_loop(0, count - 1 - me if conj else me, hop, 0)


def finish_kernel(micro, keep_ref, flag_ref, spans_ref, me_ref, z_ref, rim_ref, taps_ref, cols_ref,
                  lam_ref, full_ref, res_ref, skip_ref, u_ref, ends_ref,
                  mixed_ref, conv_ref, marks_ref, zs_ref, y_ref, st_ref):
    count, width = z_ref.shape[0], z_ref.shape[1] // 3
    poles = lam_ref.shape[0] // 2
    keep_rows(z_ref, rim_ref, zs_ref)
    joined(ends_ref, micro, full_ref, st_ref, spans_ref, me_ref[0], ends_ref.shape[0], False)

    def scan(group, _):
        @pl.when(group % (SPAN // STEP) == 0)
        def _():
            marks_ref[group // (SPAN // STEP)] = st_ref[...]

        def step(masked):
            us = [u_ref[at(group, j), :] for j in range(STEP)]
            ys = [None] * STEP
            for k in range(poles):
                lr, li = lam_ref[k], lam_ref[poles + k]
                rr, ri = res_ref[k], res_ref[poles + k]
                sr, si = st_ref[k], st_ref[poles + k]
                for j in range(STEP):
                    if masked:
                        keep = keep_ref[group * STEP + j]
                        sr, si = sr * keep, si * keep
                    sr, si = lr * sr - li * si + us[j], lr * si + li * sr
                    part = rr * sr - ri * si
                    ys[j] = part if ys[j] is None else ys[j] + part
                st_ref[k], st_ref[poles + k] = sr, si
            for j in range(STEP):
                y_ref[at(group, j), :] = ys[j]

        by_flag(flag_ref[group], step)
        return 0

    lax.fori_loop(0, count // STEP, scan, 0)

    def natural(i, _):
        rows = pl.ds(pl.multiple_of(i * ROWS, ROWS), ROWS)
        cols = chunk_cols(cols_ref, i)
        query = filtered(zs_ref, taps_ref, cols, i, 0, width)
        key = filtered(zs_ref, taps_ref, cols, i, 1, width)
        value = filtered(zs_ref, taps_ref, cols, i, 2, width)
        conv = collect(y_ref, i, width) + skip_ref[...] * (key * value * cols[:, 2:3])
        conv_ref[rows, :] = conv
        mixed_ref[rows, :] = (query * conv).astype(BF)
        return 0

    lax.fori_loop(0, count // ROWS, natural, 0)


def adjoint_kernel(keep_ref, flag_ref, z_ref, rim_ref, taps_ref, cols_ref, lam_ref, dmix_ref,
                   e_ref, end_ref, zs_ref):
    count, width = z_ref.shape[0], z_ref.shape[1] // 3
    poles = lam_ref.shape[0] // 2
    keep_rows(z_ref, rim_ref, zs_ref)

    def natural(i, _):
        rows = pl.ds(pl.multiple_of(i * ROWS, ROWS), ROWS)
        query = filtered(zs_ref, taps_ref, chunk_cols(cols_ref, i), i, 0, width)
        spread(e_ref, i, dmix_ref[rows, :].astype(F32) * query)
        return 0

    lax.fori_loop(0, count // ROWS, natural, 0)
    end_ref[...] = jnp.zeros_like(end_ref)

    def scan(order, _):
        group = count // STEP - 1 - order

        def step(masked):
            es = [e_ref[at(group, j), :] for j in range(STEP)]
            for k in range(poles):
                lr, li = lam_ref[k], lam_ref[poles + k]
                br, bi = end_ref[k], end_ref[poles + k]
                for j in reversed(range(STEP)):
                    if masked:
                        keep = keep_ref[group * STEP + j + 1]
                        br, bi = br * keep, bi * keep
                    br, bi = lr * br + li * bi + es[j], lr * bi - li * br
                end_ref[k], end_ref[poles + k] = br, bi

        by_flag(flag_ref[group] + flag_ref[group + 1], step)
        return 0

    lax.fori_loop(0, count // STEP, scan, 0)


def back_kernel(micro, keep_ref, flag_ref, spans_ref, me_ref, z_ref, rim_ref, taps_ref, cols_ref,
                lam_ref, full_ref, res_ref, skip_ref, u_ref, e_ref, dmix_ref, conv_ref,
                marks_ref, ends_ref,
                dz_ref, rimback_ref, tail_ref, dtaps_ref, dskip_ref, dres_ref, g_ref,
                zs_ref, dc_ref, di_ref, ss_ref, bt_ref):
    count, width = z_ref.shape[0], z_ref.shape[1] // 3
    poles = lam_ref.shape[0] // 2
    state_rows = 2 * poles * SUB
    keep_rows(z_ref, rim_ref, zs_ref)
    joined(ends_ref, micro, full_ref, bt_ref, spans_ref, me_ref[0], ends_ref.shape[0], True)
    bt_ref[...] = bt_ref[...] * keep_ref[count]
    for ref in (dtaps_ref, dskip_ref, dres_ref, g_ref):
        ref[...] = jnp.zeros_like(ref)

    def held(slot, k):
        return pl.ds(pl.multiple_of(slot * state_rows + k * SUB, SUB), SUB)

    def block(order, _):
        number = count // SPAN - 1 - order
        for k in range(2 * poles):
            ss_ref[held(0, k), :] = marks_ref[number, k]

        def forward(inner, _):
            group = number * (SPAN // STEP) + inner

            def step(masked):
                us = [u_ref[at(group, j), :] for j in range(STEP)]
                es = [e_ref[at(group, j), :] for j in range(STEP)]
                for k in range(poles):
                    lr, li = lam_ref[k], lam_ref[poles + k]
                    sr = ss_ref[held(inner * STEP, k), :]
                    si = ss_ref[held(inner * STEP, poles + k), :]
                    ar = ai = None
                    for j in range(STEP):
                        if masked:
                            keep = keep_ref[group * STEP + j]
                            sr, si = sr * keep, si * keep
                        sr, si = lr * sr - li * si + us[j], lr * si + li * sr
                        ss_ref[held(inner * STEP + j + 1, k), :] = sr
                        ss_ref[held(inner * STEP + j + 1, poles + k), :] = si
                        ar = es[j] * sr if ar is None else ar + es[j] * sr
                        ai = es[j] * si if ai is None else ai + es[j] * si
                    dres_ref[k] = dres_ref[k] + ar
                    dres_ref[poles + k] = dres_ref[poles + k] + ai

            by_flag(flag_ref[group], step)
            return 0

        lax.fori_loop(0, SPAN // STEP, forward, 0)

        def backward(outer, _):
            inner = SPAN // STEP - 1 - outer
            group = number * (SPAN // STEP) + inner

            def step(masked):
                es = [e_ref[at(group, j), :] for j in range(STEP)]
                ds = [None] * STEP
                for k in range(poles):
                    lr, li = lam_ref[k], lam_ref[poles + k]
                    rr, ri = res_ref[k], res_ref[poles + k]
                    tr, ti = bt_ref[k], bt_ref[poles + k]
                    gr, gi = g_ref[k], g_ref[poles + k]
                    for j in reversed(range(STEP)):
                        tr, ti = lr * tr + li * ti + es[j], lr * ti - li * tr
                        part = rr * tr + ri * ti
                        ds[j] = part if ds[j] is None else ds[j] + part
                        if masked:
                            keep = keep_ref[group * STEP + j]
                            tr, ti = tr * keep, ti * keep
                        sr = ss_ref[held(inner * STEP + j, k), :]
                        si = ss_ref[held(inner * STEP + j, poles + k), :]
                        gr = gr + (sr * tr + si * ti)
                        gi = gi + (sr * ti - si * tr)
                    bt_ref[k], bt_ref[poles + k] = tr, ti
                    g_ref[k], g_ref[poles + k] = gr, gi
                for j in range(STEP):
                    di_ref[at(group, j), :] = ds[j]

            by_flag(flag_ref[group], step)
            return 0

        lax.fori_loop(0, SPAN // STEP, backward, 0)
        return 0

    lax.fori_loop(0, count // SPAN, block, 0)

    def eighths(value):
        total = value[0:SUB]
        for start in range(SUB, ROWS, SUB):
            total = total + value[start : start + SUB]
        return total

    def natural(i, _):
        rows = pl.ds(pl.multiple_of(i * ROWS, ROWS), ROWS)
        cols = chunk_cols(cols_ref, i)
        query = filtered(zs_ref, taps_ref, cols, i, 0, width)
        key = filtered(zs_ref, taps_ref, cols, i, 1, width)
        value = filtered(zs_ref, taps_ref, cols, i, 2, width)
        mask = cols[:, 2:3]
        d_mixed = dmix_ref[rows, :].astype(F32)
        e = d_mixed * query
        dskip_ref[...] = dskip_ref[...] + eighths(e * (key * value * mask))
        d_inject = (collect(di_ref, i, width) + skip_ref[...] * e) * mask
        for stream, grad in enumerate((d_mixed * conv_ref[rows, :], d_inject * value, d_inject * key)):
            lanes = slice(stream * width, (stream + 1) * width)
            dc_ref[rows, lanes] = grad
            shifted = window(zs_ref, i, stream, width)
            for lag in range(3):
                product = grad * shifted[lag]
                if lag:
                    product = product * cols[:, lag - 1 : lag]
                slot = slice((lag * 3 + stream) * SUB, (lag * 3 + stream + 1) * SUB)
                dtaps_ref[slot, :] = dtaps_ref[slot, :] + eighths(product)
        return 0

    lax.fori_loop(0, count // ROWS, natural, 0)
    dc_ref[count : count + SUB, :] = jnp.zeros((SUB, 3 * width), F32)

    def spread_back(i, _):
        rows = pl.ds(pl.multiple_of(i * ROWS, ROWS), ROWS)
        beyond = pl.ds(pl.multiple_of(i * ROWS, ROWS), ROWS + SUB)
        cols = cols_ref[beyond, :]
        v1, v2 = cols[1 : 1 + ROWS, 0:1], cols[2 : 2 + ROWS, 1:2]
        for stream in range(3):
            lanes = slice(stream * width, (stream + 1) * width)
            wide = dc_ref[beyond, lanes]
            t0, t1, t2 = (taps_ref[lag * 3 + stream : lag * 3 + stream + 1, :] for lag in range(3))
            total = t0 * wide[0:ROWS] + (t1 * wide[1 : 1 + ROWS]) * v1 + (t2 * wide[2 : 2 + ROWS]) * v2
            dz_ref[rows, lanes] = total.astype(BF)

            @pl.when(i == count // ROWS - 1)
            def _():
                tail_ref[:, lanes] = total

        return 0

    lax.fori_loop(0, count // ROWS, spread_back, 0)
    first = cols_ref[0:SUB, :]
    for stream in range(3):
        lanes = slice(stream * width, (stream + 1) * width)
        dc = dc_ref[0:SUB, lanes]
        t1, t2 = (taps_ref[lag * 3 + stream : lag * 3 + stream + 1, :] for lag in (1, 2))
        one, two = t1 * (dc * first[:, 0:1]), t2 * (dc * first[:, 1:2])
        rimback_ref[...] = rimback_ref[...] if stream else jnp.zeros_like(rimback_ref)
        rimback_ref[0:1, lanes] = two[0:1]
        rimback_ref[1:2, lanes] = one[0:1] + two[1:2]


def call(kernel, ins, outs, scratch, smem, name, flops, after=()):
    count = len(ins)

    def without(*refs):
        kernel(*refs[:count], *refs[count + len(after) :])

    vmem = pl.BlockSpec(memory_space=pltpu.VMEM)
    scalar = pl.BlockSpec(memory_space=pltpu.SMEM)
    moved = sum(a.size * a.dtype.itemsize for a in ins) + sum(
        functools.reduce(lambda x, y: x * y, s) * jnp.dtype(d).itemsize for s, d in outs
    )
    return pl.pallas_call(
        without,
        out_shape=[jax.ShapeDtypeStruct(s, d) for s, d in outs],
        in_specs=[scalar] * smem + [vmem] * (count - smem)
        + [pl.BlockSpec(memory_space=pl.ANY)] * len(after),
        out_specs=[vmem] * len(outs),
        scratch_shapes=[pltpu.VMEM(s, d) for s, d in scratch],
        compiler_params=pltpu.CompilerParams(vmem_limit_bytes=VMEM_LIMIT),
        cost_estimate=pl.CostEstimate(flops=flops, bytes_accessed=moved, transcendentals=0),
        name=name,
    )(*ins, *after)


def segment_number(position, doc_lengths):
    starts_at = jnp.cumsum(doc_lengths) - doc_lengths
    hits = (starts_at[None, :] <= position[:, None]).astype(jnp.int32)
    return jnp.sum(hits, axis=1)


def norm_scale(values):
    return lax.rsqrt(jnp.mean(values * values, axis=-1, keepdims=True) + EPS)


def norm_back(values, scale, gain, grad):
    weighted = gain[None] * grad
    d_values = scale * weighted - values * scale**3 * jnp.mean(
        weighted * values, axis=-1, keepdims=True
    )
    return d_values, jnp.sum(grad * values * scale, axis=0)


def polar(exponent, decay_rate, pole_angle):
    magnitude = jnp.exp(-exponent * decay_rate)
    phase = exponent * pole_angle
    return magnitude * jnp.cos(phase), magnitude * jnp.sin(phase)


def packed(real, imag):
    rows = real.size // (SUB * LANE)
    return jnp.concatenate([real.reshape(rows, SUB, LANE), imag.reshape(rows, SUB, LANE)])


def unpacked(pair, shape):
    half = pair.shape[0] // 2
    return pair[:half].reshape(shape), pair[half:].reshape(shape)


def gather(block, axis, dim):
    return lax.all_gather(block, axis, axis=dim, tiled=True)


def scatter(block, axis, dim):
    return lax.psum_scatter(block, axis, scatter_dimension=dim, tiled=True)


CORE, X, Y = 1, 2, 4


def over(value, bit):
    return lax.ppermute(value, "seq", [(i, i ^ bit) for i in range(8)])


def place_kernel(spots, me_ref, *refs):
    count = len(spots)
    pieces, out_ref, held, sems = refs[:count], refs[count], refs[count + 1 : -1], refs[-1]
    arrive = [pltpu.make_async_copy(pieces[i], held[i], sems.at[0, i]) for i in range(count)]
    leave = [
        pltpu.make_async_copy(held[i], out_ref.at[spots[i](me_ref[0])], sems.at[1, i])
        for i in range(count)
    ]
    for copy in arrive:
        copy.start()
    for i in range(count):
        arrive[i].wait()
        leave[i].start()
    for copy in leave:
        copy.wait()


def place(me, pieces, spots, shape, name):
    anywhere = pl.BlockSpec(memory_space=pl.ANY)
    moved = 4 * shape[0] * shape[1]
    return pl.pallas_call(
        functools.partial(place_kernel, spots),
        out_shape=jax.ShapeDtypeStruct(shape, pieces[0].dtype),
        in_specs=[pl.BlockSpec(memory_space=pltpu.SMEM)] + [anywhere] * len(pieces),
        out_specs=anywhere,
        scratch_shapes=[pltpu.VMEM(piece.shape, piece.dtype) for piece in pieces]
        + [pltpu.SemaphoreType.DMA((2, len(pieces)))],
        compiler_params=pltpu.CompilerParams(vmem_limit_bytes=VMEM_LIMIT),
        cost_estimate=pl.CostEstimate(flops=0, bytes_accessed=moved, transcendentals=0),
        name=name,
    )(me.astype(jnp.int32).reshape(1), *pieces)


def rows_of(bits, rows):
    return lambda me: pl.ds(pl.multiple_of((me ^ bits) * rows, 16), rows)


def seq_links(block, relay):
    if lax.axis_size("seq") != 8:
        return (block,)
    from_x, from_y = over(block, X), over(block, Y)
    return block, from_x, from_y, over(from_x if relay == Y else from_y, relay)


def seq_gather(blocks):
    if lax.axis_size("seq") != 8:
        return gather(blocks[0], "seq", 0)
    rows, width = blocks[0].shape
    others = [over(block, CORE) for block in blocks]
    spots = [rows_of(bits + core, rows) for core in (0, CORE) for bits in (0, X, Y, X + Y)]
    return place(lax.axis_index("seq"), [*blocks, *others], spots, (8 * rows, width), "place_rows")


def plus(*terms):
    total = terms[0].astype(F32)
    for term in terms[1:]:
        total = total + term.astype(F32)
    return total


def half_kernel(micros, me_ref, *refs):
    lefts, rights, out_ref = refs[:micros], refs[micros : 2 * micros], refs[-1]
    total = None
    for left, right in zip(lefts, rights):
        part = lax.dot_general(left[...], right[...], (((0,), (0,)), ((), ())), preferred_element_type=F32)
        total = part if total is None else total + part
    out_ref[...] = total.astype(BF)


def grad_half(lefts, rights, own, name, after):
    count, wide = lefts[0].shape
    rows, width = wide // 8, rights[0].shape[1]
    core = (lax.axis_index("seq") & CORE).astype(jnp.int32)
    core = (core if own else 1 - core).reshape(1)
    steps, pick = (8, lambda i, c: (0, i)) if own is None else (4, lambda i, c: (0, 2 * i + c[0]))
    n = len(lefts)
    return pl.pallas_call(
        functools.partial(half_kernel, n),
        out_shape=jax.ShapeDtypeStruct((steps * rows, width), BF),
        grid_spec=pltpu.PrefetchScalarGridSpec(
            num_scalar_prefetch=1,
            grid=(steps,),
            in_specs=[pl.BlockSpec((count, rows), pick)] * n
            + [pl.BlockSpec((count, width), lambda i, c: (0, 0))] * n
            + [pl.BlockSpec(memory_space=pl.ANY)] * len(after),
            out_specs=pl.BlockSpec((rows, width), lambda i, c: (i, 0)),
        ),
        compiler_params=pltpu.CompilerParams(vmem_limit_bytes=VMEM_LIMIT),
        cost_estimate=pl.CostEstimate(
            flops=2 * n * count * rows * steps * width,
            bytes_accessed=n * count * (wide + 2 * width) + wide * width,
            transcendentals=0,
        ),
        name=name,
    )(core, *lefts, *rights, *after)


def grad_halves(lefts, rights, name, after=()):
    if lax.axis_size("seq") != 8:
        return (dot(jnp.concatenate(lefts), jnp.concatenate(rights), ((0,), (0,))).astype(BF),)
    return tuple(grad_half(lefts, rights, own, name, after) for own in (False, True))


def grad_chip(halves):
    if len(halves) == 1:
        return halves[0]
    send, keep = halves
    four = plus(keep, over(send, CORE)).astype(BF)
    return four.reshape(4, keep.shape[0] // 4, keep.shape[1])


def owner(four, bits):
    return lax.dynamic_index_in_dim(four, (lax.axis_index("seq") // 2) ^ (bits // 2), 0, keepdims=False)


def grad_far(four, relay):
    if four.ndim == 2:
        return four
    return over(owner(four, X + Y), relay)


def grad_own(four, far, relay):
    if four.ndim == 2:
        return scatter(four, "seq", 0).astype(F32)
    to_x, to_y = owner(four, X), owner(four, Y)
    if relay == Y:
        to_x = plus(to_x, far).astype(BF)
    else:
        to_y = plus(to_y, far).astype(BF)
    return plus(owner(four, 0), over(to_x, X), over(to_y, Y))


def grad_sum(halves, relay):
    four = grad_chip(halves)
    return grad_own(four, grad_far(four, relay), relay)


def tp_sum(block):
    count = lax.axis_size("tp")
    return plus(block, *[
        lax.ppermute(block, "tp", [(i, (i + hop) % count) for i in range(count)])
        for hop in range(1, count)
    ])


def tied(value, *others):
    if not others:
        return value
    nothing = sum(other[(0,) * other.ndim].astype(F32) * 0.0 for other in others)
    return value + nothing.astype(value.dtype)


def dot(a, b, dims):
    return lax.dot_general(a, b, (dims, ((), ())), preferred_element_type=F32)


def shards(tokens, lengths, pad_mask, gain_in, w_in, conv_taps, log_rate, pole_angle, residues,
           skip_gain, w_out, gain_mlp, w_gu, w_down, cotangent):
    micros, count, width = tokens.shape
    n_seq, n_tp = lax.axis_size("seq"), lax.axis_size("tp")
    me = lax.axis_index("seq")
    hidden = w_gu.shape[2]
    joint = jnp.concatenate([tokens.reshape(micros * count, width), w_out.T])
    joint = gather(joint, "tp", 1)
    x_full = joint[: micros * count].reshape(micros, count, -1)
    out_lanes = joint[micros * count :]
    in_links = seq_links(w_in.reshape(w_in.shape[0], -1), Y)
    gu_links = seq_links(tied(w_gu.reshape(w_gu.shape[0], -1), *in_links[1:2]), X)
    down_links = seq_links(tied(w_down.T, gu_links[-1]), Y)
    in_full, gu_full, down_full = seq_gather(in_links), seq_gather(gu_links), seq_gather(down_links)
    cot_full = [gather(cotangent[0], "tp", 1)]
    out_links = seq_links(out_lanes, X)
    out_full = seq_gather(out_links)

    rate = jnp.exp(log_rate)
    lam_real, lam_imag = polar(1.0, rate, pole_angle)
    lam = packed(lam_real, lam_imag)
    lam_all = packed(*polar(float(count), rate, pole_angle))
    res = packed(residues[0], residues[1])
    taps = conv_taps.reshape(9, width)
    skip = skip_gain.reshape(1, width)
    me_word = me.astype(jnp.int32).reshape(1)
    edges = jnp.arange(n_seq + 1) * count
    seq_shape = (count * SUB, LANE)
    st_shape = lam.shape
    work = lam.shape[0] * SUB * LANE * count

    position = me * count + jnp.arange(-2, count + 1)
    seg = jnp.stack([segment_number(position, lengths[m]) for m in range(micros)])
    valid1 = (seg[:, 2:] == seg[:, 1:-1]).astype(F32)
    valid2 = (seg[:, 2:] == seg[:, :-2]).astype(F32)
    inside = (jnp.arange(count + 1) < count) | (me < n_seq - 1)
    keeps = jnp.pad(valid1 * inside[None].astype(F32), ((0, 0), (0, SUB - 1)))
    group_flags = jnp.any(keeps.reshape(micros, -1, STEP) == 0, axis=2).astype(jnp.int32)
    columns = jnp.stack([valid1[:, :count], valid2[:, :count], pad_mask.astype(F32)], axis=2)
    columns = jnp.pad(columns, ((0, 0), (0, SUB), (0, SUB - 3)))

    x_wide = x_full.astype(F32)
    scale_in = norm_scale(x_wide)
    h_in = (x_wide * scale_in * tied(gain_in, gu_full)).astype(BF)
    z_low = dot(h_in, in_full, ((2,), (0,))).astype(BF)
    rims = lax.ppermute(z_low[:, count - 2 :], "seq", [(i, i + 1) for i in range(n_seq - 1)])
    rims = jnp.pad(rims.astype(F32), ((0, 0), (SUB - 2, 0), (0, 0)))
    zs = ((count + SUB, 3 * width), F32)
    bases = [(z_low[m], rims[m], taps, columns[m], lam) for m in range(micros)]
    masks = [(keeps[m], group_flags[m]) for m in range(micros)]
    last = [segment_number(edges - 1, lengths[m]) for m in range(micros)]
    first = [segment_number(edges, lengths[m]) for m in range(micros)]
    spans = [(v[1:] == v[:-1]).astype(F32) for v in last]
    spans_back = [(v[1:] == v[:-1]).astype(F32) for v in first]
    injects, ends = zip(*[
        call(front_kernel, (*masks[m], *bases[m]), [(seq_shape, F32), (st_shape, F32)],
             [zs], 2, "mixer_front", 4 * work)
        for m in range(micros)
    ])
    ends = lax.all_gather(jnp.stack(ends).astype(BF), "seq").astype(F32)

    kept = []
    outputs = []
    for m in range(micros):
        mixed, conv_out, marks = call(
            functools.partial(finish_kernel, m),
            (*masks[m], spans[m], me_word, *bases[m], lam_all, res, skip, injects[m], ends),
            [((count, width), BF), ((count, width), F32), ((count // SPAN, *st_shape), F32)],
            [zs, (seq_shape, F32), (st_shape, F32)], 4, "mixer_finish", 6 * work,
            (out_links[-1], *down_links[1:3]) if m else (*cot_full, *out_links[1:3]),
        )
        kept.append(dict(mixed=mixed, conv=conv_out, marks=marks))

    for m in range(micros):
        mixed_full = gather(kept[m]["mixed"], "tp", 1)
        if m + 1 < micros:
            cot_full.append(gather(tied(cotangent[m + 1], mixed_full), "tp", 1))
        x_mid = x_full[m].astype(F32) + dot(mixed_full, out_full, ((1,), (1,)))
        scale_mid = norm_scale(x_mid)
        h_mlp = (x_mid * scale_mid * gain_mlp[None]).astype(BF)
        gate_up = dot(h_mlp, gu_full, ((1,), (0,)))
        gate, up = gate_up[:, :hidden], gate_up[:, hidden:]
        sig = jax.nn.sigmoid(gate)
        act = (gate * sig * up).astype(BF)
        down_own = scatter(dot(act, down_full, ((1,), (1,))).astype(BF), "tp", 1)
        mid_own = lax.dynamic_slice_in_dim(x_mid, lax.axis_index("tp") * width, width, 1)
        outputs.append((mid_own + down_own.astype(F32)).astype(BF))

        cot = cot_full[m]
        d_act = dot(cot, down_full, ((1,), (0,)))
        d_gu = jnp.concatenate(
            [d_act * up * sig * (1.0 + gate * (1.0 - sig)), d_act * gate * sig], axis=1
        ).astype(BF)
        d_h = dot(d_gu, gu_full, ((1,), (1,)))
        d_norm, d_gain_mlp = norm_back(x_mid, scale_mid, gain_mlp, d_h)
        d_mid = d_norm + cot.astype(F32) * (1.0 / n_tp)
        d_low = d_mid.astype(BF)
        d_mixed = scatter(dot(d_low, out_full, ((1,), (0,))).astype(BF), "tp", 1)
        kept[m].update(
            mixed=mixed_full, h_mlp=h_mlp, act=act, d_gu=d_gu, d_mid=d_mid, d_low=d_low,
            d_mixed=d_mixed, d_gain_mlp=d_gain_mlp,
        )

    def each(name):
        return [c[name] for c in kept]

    down_halves = grad_halves(cot_full, each("act"), "grad_down")
    out_halves = grad_halves(each("d_low"), each("mixed"), "grad_out")
    g_down = grad_sum(down_halves, Y)
    g_out = scatter(grad_sum(out_halves, X).astype(BF), "tp", 1)
    adjoints, ends = zip(*[
        call(adjoint_kernel, (*masks[m], *bases[m], kept[m]["d_mixed"]),
             [(seq_shape, F32), (st_shape, F32)], [zs], 2, "mixer_adjoint", 4 * work,
             (*down_halves, *out_halves))
        for m in range(micros)
    ])
    ends = lax.all_gather(jnp.stack(ends).astype(BF), "seq").astype(F32)
    gu_halves = grad_halves(each("h_mlp"), each("d_gu"), "grad_gu", (ends,))
    gu_chip = grad_chip(gu_halves)
    gu_far = grad_far(gu_chip, X)
    g_gu = grad_own(gu_chip, gu_far, X)

    token_grads = []
    partial_grads = []
    smalls = []
    for m in range(micros):
        c = kept[m]
        d_z, rim_back, tail, d_taps, d_skip, d_res, d_lam = call(
            functools.partial(back_kernel, m),
            (*masks[m], spans_back[m], me_word, *bases[m], lam_all, res, skip, injects[m],
             adjoints[m], c["d_mixed"], c["conv"], c["marks"], ends),
            [((count, 3 * width), BF), ((SUB, 3 * width), F32), ((ROWS, 3 * width), F32),
             ((9 * SUB, width), F32), ((SUB, width), F32), (st_shape, F32), (st_shape, F32)],
            [zs, ((count + SUB, 3 * width), F32), (seq_shape, F32),
             (((SPAN + 1) * st_shape[0] * SUB, LANE), F32), (st_shape, F32)],
            4, "mixer_back", 16 * work, (*partial_grads, g_down, gu_far) if m else (*gu_halves, gu_chip),
        )
        rim_back = lax.ppermute(rim_back[:2], "seq", [(i + 1, i) for i in range(n_seq - 1)])
        tail = (tail + jnp.concatenate([jnp.zeros((ROWS - 2, 3 * width), F32), rim_back])).astype(BF)
        d_z = lax.dynamic_update_slice(d_z, tail, (count - ROWS, 0))
        c["d_z"] = d_z
        gain = gain_in
        if m == micros - 1:
            in_halves = grad_halves([h_in[i] for i in range(micros)], each("d_z"), "grad_in")
            gain = tied(gain_in, in_halves[0])
        d_h_in = dot(d_z, in_full, ((1,), (1,)))
        d_norm, d_gain_in = norm_back(x_full[m].astype(F32), scale_in[m], gain, d_h_in)
        partial_grads.append((c["d_mid"] + d_norm).astype(BF))
        token_grads.append(scatter(partial_grads[m], "tp", 1))
        g_real, g_imag = unpacked(d_lam, log_rate.shape)
        s_real, s_imag = unpacked(d_res, log_rate.shape)
        h_real = residues[0] * g_real + residues[1] * g_imag
        h_imag = residues[0] * g_imag - residues[1] * g_real
        smalls.append(jnp.concatenate([
            jnp.sum(d_taps.reshape(9, SUB, width), axis=1),
            -rate * (lam_real * h_real + lam_imag * h_imag),
            lam_real * h_imag - lam_imag * h_real,
            s_real, -s_imag,
            jnp.sum(d_skip, axis=0, keepdims=True),
            d_gain_in.reshape(-1, width), c["d_gain_mlp"].reshape(-1, width),
        ]))

    g_in = grad_sum(in_halves, Y)
    n_gain = 2 * (gain_in.shape[0] // width)
    small = sum(smalls)
    gains = tp_sum(small[-n_gain:].astype(BF))
    small = jnp.sum(lax.all_gather(tied(small[:-n_gain], partial_grads[-1]).astype(BF), "seq").astype(F32), axis=0)
    gains = jnp.sum(lax.all_gather(tied(gains, g_in).astype(BF), "seq").astype(F32), axis=0)
    n_pole = log_rate.shape[0]
    cuts = [9, 9 + n_pole, 9 + 2 * n_pole, 9 + 3 * n_pole, 9 + 4 * n_pole]
    return (
        jnp.stack(outputs),
        jnp.stack(token_grads),
        gains[: n_gain // 2].reshape(-1),
        g_in.reshape(w_in.shape),
        small[: cuts[0]].reshape(conv_taps.shape),
        small[cuts[0] : cuts[1]],
        small[cuts[1] : cuts[2]],
        small[cuts[2] : cuts[4]].reshape(residues.shape),
        small[cuts[4]],
        g_out.T.astype(F32),
        gains[n_gain // 2 :].reshape(-1),
        g_gu.reshape(w_gu.shape),
        g_down.T,
    )


def solution(mesh):
    wide, deep, flat = P(None, "seq", "tp"), P("seq", None, "tp"), P("tp", "seq")
    poles, taps = P(None, "tp"), P(None, None, "tp")
    return jax.shard_map(
        shards,
        mesh=mesh,
        in_specs=(wide, P(), P(None, "seq"), P(), deep, taps, poles, poles, taps, P("tp"), flat,
                  P(), deep, flat, wide),
        out_specs=(wide, wide, P(), deep, taps, poles, poles, taps, P("tp"), flat, P(), deep, flat),
        check_vma=False,
    )
```

```python
import functools

import jax
import jax.numpy as jnp
from jax import lax
from jax.experimental import pallas as pl
from jax.experimental.pallas import tpu as pltpu
from jax.sharding import PartitionSpec as P

EPS = 1e-06
SPAN = 64
STEP = 8
ROWS = 16
SUB, LANE = 8, 128
BF, F32 = jnp.bfloat16, jnp.float32
VMEM_LIMIT = 56 * 1024 * 1024


def keep_rows(z_ref, rim_ref, zs_ref):
    zs_ref[0:SUB, :] = rim_ref[...]

    def body(i, _):
        rows = pl.ds(pl.multiple_of(i * ROWS, ROWS), ROWS)
        zs_ref[pl.ds(pl.multiple_of(i * ROWS + SUB, SUB), ROWS), :] = z_ref[rows, :].astype(F32)
        return 0

    lax.fori_loop(0, z_ref.shape[0] // ROWS, body, 0)


def window(zs_ref, i, stream, width):
    rows = pl.ds(pl.multiple_of(i * ROWS, ROWS), ROWS + SUB)
    wide = zs_ref[rows, stream * width : (stream + 1) * width]
    return wide[8 : 8 + ROWS], wide[7 : 7 + ROWS], wide[6 : 6 + ROWS]


def filtered(zs_ref, taps_ref, cols, i, stream, width):
    z0, z1, z2 = window(zs_ref, i, stream, width)
    t0, t1, t2 = (taps_ref[lag * 3 + stream : lag * 3 + stream + 1, :] for lag in range(3))
    return t0 * z0 + (t1 * z1) * cols[:, 0:1] + (t2 * z2) * cols[:, 1:2]


def spread(ref, i, value):
    parts = value.shape[1] // LANE
    for c in range(parts):
        piece = value[:, c * LANE : (c + 1) * LANE]
        for half in range(SUB // parts):
            ref[pl.ds(i * (ROWS * SUB) + half * parts + c, ROWS, stride=SUB), :] = piece


def collect(ref, i, width):
    parts = width // LANE
    pieces = []
    for c in range(parts):
        piece = ref[pl.ds(i * (ROWS * SUB) + c, ROWS, stride=SUB), :]
        for half in range(1, SUB // parts):
            piece = piece + ref[pl.ds(i * (ROWS * SUB) + half * parts + c, ROWS, stride=SUB), :]
        pieces.append(piece)
    return jnp.concatenate(pieces, axis=1)


def chunk_cols(cols_ref, i):
    return cols_ref[pl.ds(pl.multiple_of(i * ROWS, ROWS), ROWS), :]


def at(group, j):
    return pl.ds(pl.multiple_of((group * STEP + j) * SUB, SUB), SUB)


def by_flag(flag, step):
    @pl.when(flag == 0)
    def _():
        step(False)

    @pl.when(flag != 0)
    def _():
        step(True)


def front_kernel(keep_ref, flag_ref, z_ref, rim_ref, taps_ref, cols_ref, lam_ref,
                 u_ref, end_ref, zs_ref):
    count, width = z_ref.shape[0], z_ref.shape[1] // 3
    poles = lam_ref.shape[0] // 2
    keep_rows(z_ref, rim_ref, zs_ref)

    def natural(i, _):
        cols = chunk_cols(cols_ref, i)
        key = filtered(zs_ref, taps_ref, cols, i, 1, width)
        value = filtered(zs_ref, taps_ref, cols, i, 2, width)
        spread(u_ref, i, key * value * cols[:, 2:3])
        return 0

    lax.fori_loop(0, count // ROWS, natural, 0)
    end_ref[...] = jnp.zeros_like(end_ref)

    def scan(group, _):
        def step(masked):
            us = [u_ref[at(group, j), :] for j in range(STEP)]
            for k in range(poles):
                lr, li = lam_ref[k], lam_ref[poles + k]
                sr, si = end_ref[k], end_ref[poles + k]
                for j in range(STEP):
                    if masked:
                        keep = keep_ref[group * STEP + j]
                        sr, si = sr * keep, si * keep
                    sr, si = lr * sr - li * si + us[j], lr * si + li * sr
                end_ref[k], end_ref[poles + k] = sr, si

        by_flag(flag_ref[group], step)
        return 0

    lax.fori_loop(0, count // STEP, scan, 0)


def joined(all_ref, micro, full_ref, carry_ref, spans_ref, me, count, conj):
    poles = full_ref.shape[0] // 2
    carry_ref[...] = jnp.zeros_like(carry_ref)

    def hop(order, _):
        j = count - 1 - order if conj else order
        span = spans_ref[j]
        for k in range(poles):
            lr, li = full_ref[k] * span, full_ref[poles + k] * (-span if conj else span)
            sr, si = carry_ref[k], carry_ref[poles + k]
            carry_ref[k] = lr * sr - li * si + all_ref[j, micro, k]
            carry_ref[poles + k] = lr * si + li * sr + all_ref[j, micro, poles + k]
        return 0

    lax.fori_loop(0, count - 1 - me if conj else me, hop, 0)


def finish_kernel(micro, keep_ref, flag_ref, spans_ref, me_ref, z_ref, rim_ref, taps_ref, cols_ref,
                  lam_ref, full_ref, res_ref, skip_ref, u_ref, ends_ref,
                  mixed_ref, conv_ref, marks_ref, zs_ref, y_ref, st_ref):
    count, width = z_ref.shape[0], z_ref.shape[1] // 3
    poles = lam_ref.shape[0] // 2
    keep_rows(z_ref, rim_ref, zs_ref)
    joined(ends_ref, micro, full_ref, st_ref, spans_ref, me_ref[0], ends_ref.shape[0], False)

    def scan(group, _):
        @pl.when(group % (SPAN // STEP) == 0)
        def _():
            marks_ref[group // (SPAN // STEP)] = st_ref[...]

        def step(masked):
            us = [u_ref[at(group, j), :] for j in range(STEP)]
            ys = [None] * STEP
            for k in range(poles):
                lr, li = lam_ref[k], lam_ref[poles + k]
                rr, ri = res_ref[k], res_ref[poles + k]
                sr, si = st_ref[k], st_ref[poles + k]
                for j in range(STEP):
                    if masked:
                        keep = keep_ref[group * STEP + j]
                        sr, si = sr * keep, si * keep
                    sr, si = lr * sr - li * si + us[j], lr * si + li * sr
                    part = rr * sr - ri * si
                    ys[j] = part if ys[j] is None else ys[j] + part
                st_ref[k], st_ref[poles + k] = sr, si
            for j in range(STEP):
                y_ref[at(group, j), :] = ys[j]

        by_flag(flag_ref[group], step)
        return 0

    lax.fori_loop(0, count // STEP, scan, 0)

    def natural(i, _):
        rows = pl.ds(pl.multiple_of(i * ROWS, ROWS), ROWS)
        cols = chunk_cols(cols_ref, i)
        query = filtered(zs_ref, taps_ref, cols, i, 0, width)
        key = filtered(zs_ref, taps_ref, cols, i, 1, width)
        value = filtered(zs_ref, taps_ref, cols, i, 2, width)
        conv = collect(y_ref, i, width) + skip_ref[...] * (key * value * cols[:, 2:3])
        conv_ref[rows, :] = conv
        mixed_ref[rows, :] = (query * conv).astype(BF)
        return 0

    lax.fori_loop(0, count // ROWS, natural, 0)


def adjoint_kernel(keep_ref, flag_ref, z_ref, rim_ref, taps_ref, cols_ref, lam_ref, dmix_ref,
                   e_ref, end_ref, zs_ref):
    count, width = z_ref.shape[0], z_ref.shape[1] // 3
    poles = lam_ref.shape[0] // 2
    keep_rows(z_ref, rim_ref, zs_ref)

    def natural(i, _):
        rows = pl.ds(pl.multiple_of(i * ROWS, ROWS), ROWS)
        query = filtered(zs_ref, taps_ref, chunk_cols(cols_ref, i), i, 0, width)
        spread(e_ref, i, dmix_ref[rows, :].astype(F32) * query)
        return 0

    lax.fori_loop(0, count // ROWS, natural, 0)
    end_ref[...] = jnp.zeros_like(end_ref)

    def scan(order, _):
        group = count // STEP - 1 - order

        def step(masked):
            es = [e_ref[at(group, j), :] for j in range(STEP)]
            for k in range(poles):
                lr, li = lam_ref[k], lam_ref[poles + k]
                br, bi = end_ref[k], end_ref[poles + k]
                for j in reversed(range(STEP)):
                    if masked:
                        keep = keep_ref[group * STEP + j + 1]
                        br, bi = br * keep, bi * keep
                    br, bi = lr * br + li * bi + es[j], lr * bi - li * br
                end_ref[k], end_ref[poles + k] = br, bi

        by_flag(flag_ref[group] + flag_ref[group + 1], step)
        return 0

    lax.fori_loop(0, count // STEP, scan, 0)


def back_kernel(micro, keep_ref, flag_ref, spans_ref, me_ref, z_ref, rim_ref, taps_ref, cols_ref,
                lam_ref, full_ref, res_ref, skip_ref, u_ref, e_ref, dmix_ref, conv_ref,
                marks_ref, ends_ref,
                dz_ref, rimback_ref, tail_ref, dtaps_ref, dskip_ref, dres_ref, g_ref,
                zs_ref, dc_ref, di_ref, ss_ref, bt_ref):
    count, width = z_ref.shape[0], z_ref.shape[1] // 3
    poles = lam_ref.shape[0] // 2
    state_rows = 2 * poles * SUB
    keep_rows(z_ref, rim_ref, zs_ref)
    joined(ends_ref, micro, full_ref, bt_ref, spans_ref, me_ref[0], ends_ref.shape[0], True)
    bt_ref[...] = bt_ref[...] * keep_ref[count]
    for ref in (dtaps_ref, dskip_ref, dres_ref, g_ref):
        ref[...] = jnp.zeros_like(ref)

    def held(slot, k):
        return pl.ds(pl.multiple_of(slot * state_rows + k * SUB, SUB), SUB)

    def block(order, _):
        number = count // SPAN - 1 - order
        for k in range(2 * poles):
            ss_ref[held(0, k), :] = marks_ref[number, k]

        def forward(inner, _):
            group = number * (SPAN // STEP) + inner

            def step(masked):
                us = [u_ref[at(group, j), :] for j in range(STEP)]
                es = [e_ref[at(group, j), :] for j in range(STEP)]
                for k in range(poles):
                    lr, li = lam_ref[k], lam_ref[poles + k]
                    sr = ss_ref[held(inner * STEP, k), :]
                    si = ss_ref[held(inner * STEP, poles + k), :]
                    ar = ai = None
                    for j in range(STEP):
                        if masked:
                            keep = keep_ref[group * STEP + j]
                            sr, si = sr * keep, si * keep
                        sr, si = lr * sr - li * si + us[j], lr * si + li * sr
                        ss_ref[held(inner * STEP + j + 1, k), :] = sr
                        ss_ref[held(inner * STEP + j + 1, poles + k), :] = si
                        ar = es[j] * sr if ar is None else ar + es[j] * sr
                        ai = es[j] * si if ai is None else ai + es[j] * si
                    dres_ref[k] = dres_ref[k] + ar
                    dres_ref[poles + k] = dres_ref[poles + k] + ai

            by_flag(flag_ref[group], step)
            return 0

        lax.fori_loop(0, SPAN // STEP, forward, 0)

        def backward(outer, _):
            inner = SPAN // STEP - 1 - outer
            group = number * (SPAN // STEP) + inner

            def step(masked):
                es = [e_ref[at(group, j), :] for j in range(STEP)]
                ds = [None] * STEP
                for k in range(poles):
                    lr, li = lam_ref[k], lam_ref[poles + k]
                    rr, ri = res_ref[k], res_ref[poles + k]
                    tr, ti = bt_ref[k], bt_ref[poles + k]
                    gr, gi = g_ref[k], g_ref[poles + k]
                    for j in reversed(range(STEP)):
                        tr, ti = lr * tr + li * ti + es[j], lr * ti - li * tr
                        part = rr * tr + ri * ti
                        ds[j] = part if ds[j] is None else ds[j] + part
                        if masked:
                            keep = keep_ref[group * STEP + j]
                            tr, ti = tr * keep, ti * keep
                        sr = ss_ref[held(inner * STEP + j, k), :]
                        si = ss_ref[held(inner * STEP + j, poles + k), :]
                        gr = gr + (sr * tr + si * ti)
                        gi = gi + (sr * ti - si * tr)
                    bt_ref[k], bt_ref[poles + k] = tr, ti
                    g_ref[k], g_ref[poles + k] = gr, gi
                for j in range(STEP):
                    di_ref[at(group, j), :] = ds[j]

            by_flag(flag_ref[group], step)
            return 0

        lax.fori_loop(0, SPAN // STEP, backward, 0)
        return 0

    lax.fori_loop(0, count // SPAN, block, 0)

    def eighths(value):
        total = value[0:SUB]
        for start in range(SUB, ROWS, SUB):
            total = total + value[start : start + SUB]
        return total

    def natural(i, _):
        rows = pl.ds(pl.multiple_of(i * ROWS, ROWS), ROWS)
        cols = chunk_cols(cols_ref, i)
        query = filtered(zs_ref, taps_ref, cols, i, 0, width)
        key = filtered(zs_ref, taps_ref, cols, i, 1, width)
        value = filtered(zs_ref, taps_ref, cols, i, 2, width)
        mask = cols[:, 2:3]
        d_mixed = dmix_ref[rows, :].astype(F32)
        e = d_mixed * query
        dskip_ref[...] = dskip_ref[...] + eighths(e * (key * value * mask))
        d_inject = (collect(di_ref, i, width) + skip_ref[...] * e) * mask
        for stream, grad in enumerate((d_mixed * conv_ref[rows, :], d_inject * value, d_inject * key)):
            lanes = slice(stream * width, (stream + 1) * width)
            dc_ref[rows, lanes] = grad
            shifted = window(zs_ref, i, stream, width)
            for lag in range(3):
                product = grad * shifted[lag]
                if lag:
                    product = product * cols[:, lag - 1 : lag]
                slot = slice((lag * 3 + stream) * SUB, (lag * 3 + stream + 1) * SUB)
                dtaps_ref[slot, :] = dtaps_ref[slot, :] + eighths(product)
        return 0

    lax.fori_loop(0, count // ROWS, natural, 0)
    dc_ref[count : count + SUB, :] = jnp.zeros((SUB, 3 * width), F32)

    def spread_back(i, _):
        rows = pl.ds(pl.multiple_of(i * ROWS, ROWS), ROWS)
        beyond = pl.ds(pl.multiple_of(i * ROWS, ROWS), ROWS + SUB)
        cols = cols_ref[beyond, :]
        v1, v2 = cols[1 : 1 + ROWS, 0:1], cols[2 : 2 + ROWS, 1:2]
        for stream in range(3):
            lanes = slice(stream * width, (stream + 1) * width)
            wide = dc_ref[beyond, lanes]
            t0, t1, t2 = (taps_ref[lag * 3 + stream : lag * 3 + stream + 1, :] for lag in range(3))
            total = t0 * wide[0:ROWS] + (t1 * wide[1 : 1 + ROWS]) * v1 + (t2 * wide[2 : 2 + ROWS]) * v2
            dz_ref[rows, lanes] = total.astype(BF)

            @pl.when(i == count // ROWS - 1)
            def _():
                tail_ref[:, lanes] = total

        return 0

    lax.fori_loop(0, count // ROWS, spread_back, 0)
    first = cols_ref[0:SUB, :]
    for stream in range(3):
        lanes = slice(stream * width, (stream + 1) * width)
        dc = dc_ref[0:SUB, lanes]
        t1, t2 = (taps_ref[lag * 3 + stream : lag * 3 + stream + 1, :] for lag in (1, 2))
        one, two = t1 * (dc * first[:, 0:1]), t2 * (dc * first[:, 1:2])
        rimback_ref[...] = rimback_ref[...] if stream else jnp.zeros_like(rimback_ref)
        rimback_ref[0:1, lanes] = two[0:1]
        rimback_ref[1:2, lanes] = one[0:1] + two[1:2]


def call(kernel, ins, outs, scratch, smem, name, flops, after=()):
    count = len(ins)

    def without(*refs):
        kernel(*refs[:count], *refs[count + len(after) :])

    vmem = pl.BlockSpec(memory_space=pltpu.VMEM)
    scalar = pl.BlockSpec(memory_space=pltpu.SMEM)
    moved = sum(a.size * a.dtype.itemsize for a in ins) + sum(
        functools.reduce(lambda x, y: x * y, s) * jnp.dtype(d).itemsize for s, d in outs
    )
    return pl.pallas_call(
        without,
        out_shape=[jax.ShapeDtypeStruct(s, d) for s, d in outs],
        in_specs=[scalar] * smem + [vmem] * (count - smem)
        + [pl.BlockSpec(memory_space=pl.ANY)] * len(after),
        out_specs=[vmem] * len(outs),
        scratch_shapes=[pltpu.VMEM(s, d) for s, d in scratch],
        compiler_params=pltpu.CompilerParams(vmem_limit_bytes=VMEM_LIMIT),
        cost_estimate=pl.CostEstimate(flops=flops, bytes_accessed=moved, transcendentals=0),
        name=name,
    )(*ins, *after)


def segment_number(position, doc_lengths):
    starts_at = jnp.cumsum(doc_lengths) - doc_lengths
    hits = (starts_at[None, :] <= position[:, None]).astype(jnp.int32)
    return jnp.sum(hits, axis=1)


def norm_scale(values):
    return lax.rsqrt(jnp.mean(values * values, axis=-1, keepdims=True) + EPS)


def norm_back(values, scale, gain, grad):
    weighted = gain[None] * grad
    d_values = scale * weighted - values * scale**3 * jnp.mean(
        weighted * values, axis=-1, keepdims=True
    )
    return d_values, jnp.sum(grad * values * scale, axis=0)


def polar(exponent, decay_rate, pole_angle):
    magnitude = jnp.exp(-exponent * decay_rate)
    phase = exponent * pole_angle
    return magnitude * jnp.cos(phase), magnitude * jnp.sin(phase)


def packed(real, imag):
    rows = real.size // (SUB * LANE)
    return jnp.concatenate([real.reshape(rows, SUB, LANE), imag.reshape(rows, SUB, LANE)])


def unpacked(pair, shape):
    half = pair.shape[0] // 2
    return pair[:half].reshape(shape), pair[half:].reshape(shape)


def gather(block, axis, dim):
    return lax.all_gather(block, axis, axis=dim, tiled=True)


def scatter(block, axis, dim):
    return lax.psum_scatter(block, axis, scatter_dimension=dim, tiled=True)


CORE, X, Y = 1, 2, 4


def over(value, bit):
    return lax.ppermute(value, "seq", [(i, i ^ bit) for i in range(8)])


def place_kernel(plan, count, me_ref, *refs):
    pieces, whole, held, arrive_sem, leave_sem = refs[:count], refs[count], refs[count + 1 : -2], refs[-2], refs[-1]
    arrive, leave = [], []
    for n, (i, lanes, bits, there) in enumerate(plan):
        rows = pieces[i].shape[0]
        spot = pl.ds(pl.multiple_of((me_ref[0] ^ bits) * rows, 16), rows)
        arrive.append(pltpu.make_async_copy(pieces[i].at[:, lanes], held[n], arrive_sem.at[n]))
        leave.append(pltpu.make_async_copy(held[n], whole.at[spot, there], leave_sem.at[n]))
    for copy in arrive:
        copy.start()
    for come, go in zip(arrive, leave):
        come.wait()
        go.start()
    for copy in leave:
        copy.wait()


def place(pieces, spans, start, width, name):
    plan = []
    for i, (bits, low) in enumerate(spans):
        first, last = max(low, start), min(low + pieces[i].shape[1], start + width)
        if first < last:
            plan.append((i, pl.ds(first - low, last - first), bits, pl.ds(first - start, last - first)))
    used = sorted({entry[0] for entry in plan})
    plan = [(used.index(i), *entry) for i, *entry in plan]
    pieces = [pieces[i] for i in used]
    rows, count, dtype = pieces[0].shape[0], len(pieces), pieces[0].dtype
    anywhere = pl.BlockSpec(memory_space=pl.ANY)
    return pl.pallas_call(
        functools.partial(place_kernel, plan, count),
        out_shape=jax.ShapeDtypeStruct((8 * rows, width), dtype),
        in_specs=[pl.BlockSpec(memory_space=pltpu.SMEM)] + [anywhere] * count,
        out_specs=anywhere,
        scratch_shapes=[pltpu.VMEM((rows, lanes.size), dtype) for _, lanes, _, _ in plan]
        + [pltpu.SemaphoreType.DMA((len(plan),)) for _ in range(2)],
        compiler_params=pltpu.CompilerParams(vmem_limit_bytes=VMEM_LIMIT),
        cost_estimate=pl.CostEstimate(flops=0, bytes_accessed=32 * rows * width, transcendentals=0),
        name=name,
    )(lax.axis_index("seq").astype(jnp.int32).reshape(1), *pieces)


def seq_links(block, half):
    if lax.axis_size("seq") != 8:
        return (block,)
    from_x, from_y = over(block, X), over(block, Y)
    return block, from_x, from_y, over(from_x[:, :half], Y), over(from_y[:, half:], X)


def seq_gather(blocks, widths, names):
    starts = [sum(widths[:i]) for i in range(len(widths))]
    if lax.axis_size("seq") != 8:
        whole = gather(blocks[0], "seq", 0)
        return [whole[:, start : start + width] for start, width in zip(starts, widths)]
    pieces = [*blocks, *[over(block, CORE) for block in blocks]]
    half = blocks[3].shape[1]
    spans = [
        (bits + core, low)
        for core in (0, CORE)
        for bits, low in ((0, 0), (X, 0), (Y, 0), (X + Y, 0), (X + Y, half))
    ]
    return [place(pieces, spans, *cut) for cut in zip(starts, widths, names)]


def plus(*terms):
    total = terms[0].astype(F32)
    for term in terms[1:]:
        total = total + term.astype(F32)
    return total


def halves_kernel(micros, core_ref, *refs):
    lefts, rights, send_ref, keep_ref = refs[:micros], refs[micros : 2 * micros], refs[-2], refs[-1]
    total = None
    for left, right in zip(lefts, rights):
        part = lax.dot_general(left[...], right[...], (((0,), (0,)), ((), ())), preferred_element_type=F32)
        total = part if total is None else total + part

    @pl.when(pl.program_id(0) < 4)
    def _():
        send_ref[...] = total.astype(BF)

    @pl.when(pl.program_id(0) >= 4)
    def _():
        keep_ref[...] = total.astype(BF)


def grad_halves(lefts, rights, name, after=()):
    if lax.axis_size("seq") != 8:
        return (dot(jnp.concatenate(lefts), jnp.concatenate(rights), ((0,), (0,))).astype(BF),)
    count, wide = lefts[0].shape
    rows, width, n = wide // 8, rights[0].shape[1], len(lefts)
    core = (lax.axis_index("seq") & CORE).astype(jnp.int32).reshape(1)
    return pl.pallas_call(
        functools.partial(halves_kernel, n),
        out_shape=[jax.ShapeDtypeStruct((wide // 2, width), BF)] * 2,
        grid_spec=pltpu.PrefetchScalarGridSpec(
            num_scalar_prefetch=1,
            grid=(8,),
            in_specs=[
                pl.BlockSpec((count, rows), lambda i, c: (0, 2 * (i % 4) + jnp.where(i < 4, 1 - c[0], c[0])))
            ] * n
            + [pl.BlockSpec((count, width), lambda i, c: (0, 0))] * n
            + [pl.BlockSpec(memory_space=pl.ANY)] * len(after),
            out_specs=[
                pl.BlockSpec((rows, width), lambda i, c: (jnp.minimum(i, 3), 0)),
                pl.BlockSpec((rows, width), lambda i, c: (jnp.maximum(i, 4) - 4, 0)),
            ],
        ),
        compiler_params=pltpu.CompilerParams(vmem_limit_bytes=VMEM_LIMIT),
        cost_estimate=pl.CostEstimate(
            flops=2 * n * count * wide * width,
            bytes_accessed=2 * n * count * (wide + width) + 2 * wide * width,
            transcendentals=0,
        ),
        name=name,
    )(core, *lefts, *rights, *after)


def grad_chip(halves, after=()):
    if len(halves) == 1:
        return halves[0]
    send, keep = halves
    four = plus(keep, over(send, CORE), nothing_of(after)).astype(BF)
    return four.reshape(4, keep.shape[0] // 4, keep.shape[1])


def owner(four, bits):
    return lax.dynamic_index_in_dim(four, (lax.axis_index("seq") // 2) ^ (bits // 2), 0, keepdims=False)


def grad_far(four, relay, after=()):
    if four.ndim == 2:
        return four
    return over(tied(owner(four, X + Y), *after), relay)


def grad_turn(four, far, relay, after=()):
    if four.ndim == 2:
        return (four,)
    nothing = nothing_of(after)
    to_x, to_y = owner(four, X).astype(F32) + nothing, owner(four, Y).astype(F32) + nothing
    if relay == Y:
        to_x = plus(to_x, far)
    else:
        to_y = plus(to_y, far)
    return to_x.astype(BF), to_y.astype(BF)


def grad_own(four, turn, after=()):
    if four.ndim == 2:
        return scatter(four, "seq", 0).astype(F32)
    return plus(owner(four, 0), over(turn[0], X), over(turn[1], Y), nothing_of(after))


def tp_sum(block):
    count = lax.axis_size("tp")
    return plus(block, *[
        lax.ppermute(block, "tp", [(i, (i + hop) % count) for i in range(count)])
        for hop in range(1, count)
    ])


def nothing_of(others):
    return sum([other[(0,) * other.ndim].astype(F32) * 0.0 for other in others], jnp.zeros((), F32))


def tied(value, *others):
    return value + nothing_of(others).astype(value.dtype) if others else value


def dot(a, b, dims):
    return lax.dot_general(a, b, (dims, ((), ())), preferred_element_type=F32)


def shards(tokens, lengths, pad_mask, gain_in, w_in, conv_taps, log_rate, pole_angle, residues,
           skip_gain, w_out, gain_mlp, w_gu, w_down, cotangent):
    micros, count, width = tokens.shape
    n_seq, n_tp = lax.axis_size("seq"), lax.axis_size("tp")
    me = lax.axis_index("seq")
    hidden = w_gu.shape[2]
    joint = jnp.concatenate([tokens.reshape(micros * count, width), w_out.T])
    joint = gather(joint, "tp", 1)
    x_full = joint[: micros * count].reshape(micros, count, -1)
    out_lanes = joint[micros * count :]
    rows_in = w_in.shape[0]
    first_links = seq_links(jnp.concatenate([w_in.reshape(rows_in, -1), w_gu.reshape(rows_in, -1)], axis=1), 3 * width)
    in_full, gu_full = seq_gather(first_links, (3 * width, 2 * hidden), ("place_in", "place_gu"))
    cot_full = [gather(cotangent[0], "tp", 1)]
    down_full = gather(tied(w_down.T, *first_links[-2:]), "seq", 0)
    out_links = seq_links(out_lanes, out_lanes.shape[1] // 2)
    (out_full,) = seq_gather(out_links, (n_tp * width,), ("place_out",))

    rate = jnp.exp(log_rate)
    lam_real, lam_imag = polar(1.0, rate, pole_angle)
    lam = packed(lam_real, lam_imag)
    lam_all = packed(*polar(float(count), rate, pole_angle))
    res = packed(residues[0], residues[1])
    taps = conv_taps.reshape(9, width)
    skip = skip_gain.reshape(1, width)
    me_word = me.astype(jnp.int32).reshape(1)
    edges = jnp.arange(n_seq + 1) * count
    seq_shape = (count * SUB, LANE)
    st_shape = lam.shape
    work = 400 * lam.shape[0] * SUB * LANE * count

    position = me * count + jnp.arange(-2, count + 1)
    seg = jnp.stack([segment_number(position, lengths[m]) for m in range(micros)])
    valid1 = (seg[:, 2:] == seg[:, 1:-1]).astype(F32)
    valid2 = (seg[:, 2:] == seg[:, :-2]).astype(F32)
    inside = (jnp.arange(count + 1) < count) | (me < n_seq - 1)
    keeps = jnp.pad(valid1 * inside[None].astype(F32), ((0, 0), (0, SUB - 1)))
    group_flags = jnp.any(keeps.reshape(micros, -1, STEP) == 0, axis=2).astype(jnp.int32)
    columns = jnp.stack([valid1[:, :count], valid2[:, :count], pad_mask.astype(F32)], axis=2)
    columns = jnp.pad(columns, ((0, 0), (0, SUB), (0, SUB - 3)))

    x_wide = x_full.astype(F32)
    scale_in = norm_scale(x_wide)
    h_in = (x_wide * scale_in * gain_in).astype(BF)
    z_low = dot(h_in, in_full, ((2,), (0,))).astype(BF)
    rims = lax.ppermute(z_low[:, count - 2 :], "seq", [(i, i + 1) for i in range(n_seq - 1)])
    rims = jnp.pad(rims.astype(F32), ((0, 0), (SUB - 2, 0), (0, 0)))
    zs = ((count + SUB, 3 * width), F32)
    bases = [(z_low[m], rims[m], taps, columns[m], lam) for m in range(micros)]
    masks = [(keeps[m], group_flags[m]) for m in range(micros)]
    last = [segment_number(edges - 1, lengths[m]) for m in range(micros)]
    first = [segment_number(edges, lengths[m]) for m in range(micros)]
    spans = [(v[1:] == v[:-1]).astype(F32) for v in last]
    spans_back = [(v[1:] == v[:-1]).astype(F32) for v in first]
    injects, ends = zip(*[
        call(front_kernel, (*masks[m], *bases[m]), [(seq_shape, F32), (st_shape, F32)],
             [zs], 2, "mixer_front", 4 * work)
        for m in range(micros)
    ])
    ends = lax.all_gather(tied(jnp.stack(ends), *out_links[1:3]).astype(BF), "seq").astype(F32)

    kept = []
    outputs = []
    for m in range(micros):
        mixed, conv_out, marks = call(
            functools.partial(finish_kernel, m),
            (*masks[m], spans[m], me_word, *bases[m], lam_all, res, skip, injects[m], ends),
            [((count, width), BF), ((count, width), F32), ((count // SPAN, *st_shape), F32)],
            [zs, (seq_shape, F32), (st_shape, F32)], 4, "mixer_finish", 5 * work,
            (kept[0]["mixed"], down_full) if m else cot_full,
        )
        kept.append(dict(mixed=mixed, conv=conv_out, marks=marks))

    order = ()
    for m in range(micros):
        mixed_full = gather(kept[m]["mixed"], "tp", 1)
        if m + 1 < micros:
            cot_full.append(gather(tied(cotangent[m + 1], mixed_full), "tp", 1))
        x_mid = tied(x_full[m].astype(F32), *order) + dot(mixed_full, out_full, ((1,), (1,)))
        scale_mid = norm_scale(x_mid)
        h_mlp = (x_mid * scale_mid * gain_mlp[None]).astype(BF)
        gate_up = dot(h_mlp, gu_full, ((1,), (0,)))
        gate, up = gate_up[:, :hidden], gate_up[:, hidden:]
        sig = jax.nn.sigmoid(gate)
        act = (gate * sig * up).astype(BF)
        down_own = scatter(dot(act, down_full, ((1,), (1,))).astype(BF), "tp", 1)
        mid_own = lax.dynamic_slice_in_dim(x_mid, lax.axis_index("tp") * width, width, 1)
        outputs.append((mid_own, down_own))

        cot = cot_full[m]
        d_act = dot(cot, down_full, ((1,), (0,)))
        d_gu = jnp.concatenate(
            [d_act * up * sig * (1.0 + gate * (1.0 - sig)), d_act * gate * sig], axis=1
        ).astype(BF)
        d_h = dot(d_gu, gu_full, ((1,), (1,)))
        d_norm, d_gain_mlp = norm_back(x_mid, scale_mid, gain_mlp, d_h)
        d_mid = d_norm + cot.astype(F32) * (1.0 / n_tp)
        d_low = d_mid.astype(BF)
        d_mixed = dot(d_low, out_full, ((1,), (0,))).astype(BF)
        order = (d_mixed,)
        d_mixed = scatter(d_mixed, "tp", 1)
        kept[m].update(
            mixed=mixed_full, h_mlp=h_mlp, act=act, d_gu=d_gu, d_mid=d_mid, d_low=d_low,
            d_mixed=d_mixed, d_gain_mlp=d_gain_mlp,
        )

    def each(name):
        return [c[name] for c in kept]

    down_halves = grad_halves(cot_full, each("act"), "grad_down", order)
    out_halves = grad_halves(each("d_low"), each("mixed"), "grad_out", order)
    down_chip, out_chip = grad_chip(down_halves), grad_chip(out_halves)
    down_far, out_far = grad_far(down_chip, Y), grad_far(out_chip, X)
    adjoints, ends = zip(*[
        call(adjoint_kernel, (*masks[m], *bases[m], kept[m]["d_mixed"]),
             [(seq_shape, F32), (st_shape, F32)], [zs], 2, "mixer_adjoint", 4 * work,
             (down_chip, out_chip) if m else (*down_halves, *out_halves))
        for m in range(micros)
    ])
    ends = lax.all_gather(tied(jnp.stack(ends), down_far, out_far).astype(BF), "seq").astype(F32)
    gu_halves = grad_halves(each("h_mlp"), each("d_gu"), "grad_gu", (ends,))
    gu_chip = grad_chip(gu_halves)
    gu_far = grad_far(gu_chip, X)
    down_turn = grad_turn(down_chip, down_far, Y, (ends,))
    g_out = grad_own(out_chip, grad_turn(out_chip, out_far, X, (ends,)))
    g_out = scatter(tied(g_out, *gu_halves).astype(BF), "tp", 1)

    token_grads = []
    partial_grads = []
    smalls = []
    for m in range(micros):
        c = kept[m]
        d_z, rim_back, tail, d_taps, d_skip, d_res, d_lam = call(
            functools.partial(back_kernel, m),
            (*masks[m], spans_back[m], me_word, *bases[m], lam_all, res, skip, injects[m],
             adjoints[m], c["d_mixed"], c["conv"], c["marks"], ends),
            [((count, 3 * width), BF), ((SUB, 3 * width), F32), ((ROWS, 3 * width), F32),
             ((9 * SUB, width), F32), ((SUB, width), F32), (st_shape, F32), (st_shape, F32)],
            [zs, ((count + SUB, 3 * width), F32), (seq_shape, F32),
             (((SPAN + 1) * st_shape[0] * SUB, LANE), F32), (st_shape, F32)],
            4, "mixer_back", 12 * work, (*partial_grads, *gu_turn) if m else (*gu_halves, gu_chip),
        )
        rim_back = lax.ppermute(rim_back[:2], "seq", [(i + 1, i) for i in range(n_seq - 1)])
        if m == 0:
            gu_turn = grad_turn(gu_chip, gu_far, X, (rim_back,))
            g_gu = grad_own(gu_chip, gu_turn)
        tail = tied(tail, g_gu if m else gu_far)
        tail = (tail + jnp.concatenate([jnp.zeros((ROWS - 2, 3 * width), F32), rim_back])).astype(BF)
        d_z = lax.dynamic_update_slice(d_z, tail, (count - ROWS, 0))
        c["d_z"] = d_z
        gain = gain_in
        if m == micros - 1:
            in_halves = grad_halves([h_in[i] for i in range(micros)], each("d_z"), "grad_in")
            gain = tied(gain_in, in_halves[0])
        d_h_in = dot(d_z, in_full, ((1,), (1,)))
        d_norm, d_gain_in = norm_back(x_full[m].astype(F32), scale_in[m], gain, d_h_in)
        gains = [d_gain_in, c["d_gain_mlp"]] if m == 0 else [gains[0] + d_gain_in, gains[1] + c["d_gain_mlp"]]
        if m == micros - 1:
            gains = tp_sum(jnp.concatenate(gains).reshape(-1, width).astype(BF))
            d_norm = tied(d_norm, gains)
        partial_grads.append((c["d_mid"] + d_norm).astype(BF))
        token_grads.append(scatter(partial_grads[m], "tp", 1))
        smalls.append((d_taps, d_lam, d_res, d_skip))

    in_chip = grad_chip(in_halves)
    d_taps, d_lam, d_res, d_skip = (sum(parts) for parts in zip(*smalls))
    g_real, g_imag = unpacked(d_lam, log_rate.shape)
    s_real, s_imag = unpacked(d_res, log_rate.shape)
    h_real = residues[0] * g_real + residues[1] * g_imag
    h_imag = residues[0] * g_imag - residues[1] * g_real
    small = jnp.concatenate([
        jnp.sum(d_taps.reshape(9, SUB, width), axis=1),
        -rate * (lam_real * h_real + lam_imag * h_imag),
        lam_real * h_imag - lam_imag * h_real,
        s_real, -s_imag,
        jnp.sum(d_skip, axis=0, keepdims=True),
        gains,
    ])
    small = jnp.sum(lax.all_gather(small.astype(BF), "seq").astype(F32), axis=0)
    in_far = grad_far(in_chip, Y, (small,))
    g_in = grad_own(in_chip, grad_turn(in_chip, in_far, Y, (small,)))
    g_down = grad_own(down_chip, down_turn, (in_far,))
    gains = small[-gains.shape[0] :]
    n_gain = gains.shape[0]
    n_pole = log_rate.shape[0]
    cuts = [9, 9 + n_pole, 9 + 2 * n_pole, 9 + 3 * n_pole, 9 + 4 * n_pole]
    return (
        jnp.stack([(mid + tied(down.astype(F32), in_far)).astype(BF) for mid, down in outputs]),
        jnp.stack(token_grads),
        gains[: n_gain // 2].reshape(-1),
        g_in.reshape(w_in.shape),
        small[: cuts[0]].reshape(conv_taps.shape),
        small[cuts[0] : cuts[1]],
        small[cuts[1] : cuts[2]],
        small[cuts[2] : cuts[4]].reshape(residues.shape),
        small[cuts[4]],
        tied(g_out.astype(F32), in_far).T,
        gains[n_gain // 2 :].reshape(-1),
        tied(g_gu, in_far).reshape(w_gu.shape),
        g_down.T,
    )


def solution(mesh):
    wide, deep, flat = P(None, "seq", "tp"), P("seq", None, "tp"), P("tp", "seq")
    poles, taps = P(None, "tp"), P(None, None, "tp")
    return jax.shard_map(
        shards,
        mesh=mesh,
        in_specs=(wide, P(), P(None, "seq"), P(), deep, taps, poles, poles, taps, P("tp"), flat,
                  P(), deep, flat, wide),
        out_specs=(wide, wide, P(), deep, taps, poles, poles, taps, P("tp"), flat, P(), deep, flat),
        check_vma=False,
    )
```

```python
import functools

import jax
import jax.numpy as jnp
from jax import lax
from jax.experimental import pallas as pl
from jax.experimental.pallas import tpu as pltpu
from jax.sharding import PartitionSpec as P

EPS = 1e-06
SPAN = 64
STEP = 8
ROWS = 64
SUB, LANE = 8, 128
BF, F32 = jnp.bfloat16, jnp.float32
VMEM_LIMIT = 56 * 1024 * 1024


def keep_rows(z_ref, rim_ref, zs_ref, streams=(0, 3)):
    width = z_ref.shape[1] // 3
    lanes = slice(streams[0] * width, streams[1] * width)
    zs_ref[0:SUB, lanes] = rim_ref[:, lanes]

    def body(i, _):
        rows = pl.ds(pl.multiple_of(i * ROWS, ROWS), ROWS)
        zs_ref[pl.ds(pl.multiple_of(i * ROWS + SUB, SUB), ROWS), lanes] = z_ref[rows, lanes].astype(F32)
        return 0

    lax.fori_loop(0, z_ref.shape[0] // ROWS, body, 0)


def window(zs_ref, i, stream, width):
    rows = pl.ds(pl.multiple_of(i * ROWS, ROWS), ROWS + SUB)
    wide = zs_ref[rows, stream * width : (stream + 1) * width]
    return wide[8 : 8 + ROWS], wide[7 : 7 + ROWS], wide[6 : 6 + ROWS]


def filtered(zs_ref, taps_ref, cols, i, stream, width):
    z0, z1, z2 = window(zs_ref, i, stream, width)
    t0, t1, t2 = (taps_ref[lag * 3 + stream : lag * 3 + stream + 1, :] for lag in range(3))
    return t0 * z0 + (t1 * z1) * cols[:, 0:1] + (t2 * z2) * cols[:, 1:2]


def spread(ref, i, value):
    parts = value.shape[1] // LANE
    for c in range(parts):
        piece = value[:, c * LANE : (c + 1) * LANE]
        for half in range(SUB // parts):
            ref[pl.ds(i * (ROWS * SUB) + half * parts + c, ROWS, stride=SUB), :] = piece


def collect(ref, i, width):
    parts = width // LANE
    pieces = []
    for c in range(parts):
        piece = ref[pl.ds(i * (ROWS * SUB) + c, ROWS, stride=SUB), :]
        for half in range(1, SUB // parts):
            piece = piece + ref[pl.ds(i * (ROWS * SUB) + half * parts + c, ROWS, stride=SUB), :]
        pieces.append(piece)
    return jnp.concatenate(pieces, axis=1)


def chunk_cols(cols_ref, i):
    return cols_ref[pl.ds(pl.multiple_of(i * ROWS, ROWS), ROWS), :]


def at(group, j):
    return pl.ds(pl.multiple_of((group * STEP + j) * SUB, SUB), SUB)


def by_flag(flag, step):
    @pl.when(flag == 0)
    def _():
        step(False)

    @pl.when(flag != 0)
    def _():
        step(True)


def eight_steps(values, powers, real, imag):
    def join(earlier, later, n):
        pr, pi = powers[n]
        return pr * earlier[0] - pi * earlier[1] + later[0], pr * earlier[1] + pi * earlier[0] + later[1]

    pr, pi = powers[0]
    pairs = [(pr * values[j] + values[j + 1], pi * values[j]) for j in range(0, STEP, 2)]
    fours = [join(pairs[j], pairs[j + 1], 1) for j in (0, 2)]
    return join((real, imag), join(*fours, 2), 3)


def end_scan(values, keep_of, masked, pow_ref, end_ref):
    poles = end_ref.shape[0] // 2
    for k in range(poles):
        sr, si = end_ref[k], end_ref[poles + k]
        if masked:
            lr, li = pow_ref[k], pow_ref[poles + k]
            for j in range(STEP):
                keep = keep_of(j)
                sr, si = sr * keep, si * keep
                sr, si = lr * sr - li * si + values[j], lr * si + li * sr
        else:
            powers = [(pow_ref[2 * poles * n + k], pow_ref[2 * poles * n + poles + k]) for n in range(4)]
            sr, si = eight_steps(values, powers, sr, si)
        end_ref[k], end_ref[poles + k] = sr, si


def front_kernel(keep_ref, flag_ref, z_ref, rim_ref, taps_ref, cols_ref, pow_ref,
                 u_ref, end_ref, zs_ref):
    count, width = z_ref.shape[0], z_ref.shape[1] // 3
    keep_rows(z_ref, rim_ref, zs_ref, (1, 3))

    def natural(i, _):
        cols = chunk_cols(cols_ref, i)
        key = filtered(zs_ref, taps_ref, cols, i, 1, width)
        value = filtered(zs_ref, taps_ref, cols, i, 2, width)
        spread(u_ref, i, key * value * cols[:, 2:3])
        return 0

    lax.fori_loop(0, count // ROWS, natural, 0)
    end_ref[...] = jnp.zeros_like(end_ref)

    def scan(group, _):
        def step(masked):
            us = [u_ref[at(group, j), :] for j in range(STEP)]
            end_scan(us, lambda j: keep_ref[group * STEP + j], masked, pow_ref, end_ref)

        by_flag(flag_ref[group], step)
        return 0

    lax.fori_loop(0, count // STEP, scan, 0)


def joined(all_ref, micro, full_ref, carry_ref, spans_ref, me, count, conj):
    poles = full_ref.shape[0] // 2
    carry_ref[...] = jnp.zeros_like(carry_ref)

    def hop(order, _):
        j = count - 1 - order if conj else order
        span = spans_ref[j]
        for k in range(poles):
            lr, li = full_ref[k] * span, full_ref[poles + k] * (-span if conj else span)
            sr, si = carry_ref[k], carry_ref[poles + k]
            carry_ref[k] = lr * sr - li * si + all_ref[j, micro, k]
            carry_ref[poles + k] = lr * si + li * sr + all_ref[j, micro, poles + k]
        return 0

    lax.fori_loop(0, count - 1 - me if conj else me, hop, 0)


def finish_kernel(micro, keep_ref, flag_ref, spans_ref, me_ref, z_ref, rim_ref, taps_ref, cols_ref,
                  lam_ref, full_ref, res_ref, skip_ref, u_ref, ends_ref,
                  mixed_ref, conv_ref, marks_ref, zs_ref, y_ref, st_ref):
    count, width = z_ref.shape[0], z_ref.shape[1] // 3
    poles = lam_ref.shape[0] // 2
    keep_rows(z_ref, rim_ref, zs_ref)
    joined(ends_ref, micro, full_ref, st_ref, spans_ref, me_ref[0], ends_ref.shape[0], False)

    def scan(group, _):
        @pl.when(group % (SPAN // STEP) == 0)
        def _():
            marks_ref[group // (SPAN // STEP)] = st_ref[...]

        def step(masked):
            us = [u_ref[at(group, j), :] for j in range(STEP)]
            ys = [None] * STEP
            for k in range(poles):
                lr, li = lam_ref[k], lam_ref[poles + k]
                rr, ri = res_ref[k], res_ref[poles + k]
                sr, si = st_ref[k], st_ref[poles + k]
                for j in range(STEP):
                    if masked:
                        keep = keep_ref[group * STEP + j]
                        sr, si = sr * keep, si * keep
                    sr, si = lr * sr - li * si + us[j], lr * si + li * sr
                    part = rr * sr - ri * si
                    ys[j] = part if ys[j] is None else ys[j] + part
                st_ref[k], st_ref[poles + k] = sr, si
            for j in range(STEP):
                y_ref[at(group, j), :] = ys[j]

        by_flag(flag_ref[group], step)
        return 0

    lax.fori_loop(0, count // STEP, scan, 0)

    def natural(i, _):
        rows = pl.ds(pl.multiple_of(i * ROWS, ROWS), ROWS)
        cols = chunk_cols(cols_ref, i)
        query = filtered(zs_ref, taps_ref, cols, i, 0, width)
        key = filtered(zs_ref, taps_ref, cols, i, 1, width)
        value = filtered(zs_ref, taps_ref, cols, i, 2, width)
        conv = collect(y_ref, i, width) + skip_ref[...] * (key * value * cols[:, 2:3])
        conv_ref[rows, :] = conv
        mixed_ref[rows, :] = (query * conv).astype(BF)
        return 0

    lax.fori_loop(0, count // ROWS, natural, 0)


def adjoint_kernel(keep_ref, flag_ref, z_ref, rim_ref, taps_ref, cols_ref, pow_ref, dmix_ref,
                   e_ref, end_ref, zs_ref):
    count, width = z_ref.shape[0], z_ref.shape[1] // 3
    keep_rows(z_ref, rim_ref, zs_ref, (0, 1))

    def natural(i, _):
        rows = pl.ds(pl.multiple_of(i * ROWS, ROWS), ROWS)
        query = filtered(zs_ref, taps_ref, chunk_cols(cols_ref, i), i, 0, width)
        spread(e_ref, i, dmix_ref[rows, :].astype(F32) * query)
        return 0

    lax.fori_loop(0, count // ROWS, natural, 0)
    end_ref[...] = jnp.zeros_like(end_ref)

    def scan(order, _):
        group = count // STEP - 1 - order

        def step(masked):
            es = [e_ref[at(group, STEP - 1 - j), :] for j in range(STEP)]
            end_scan(es, lambda j: keep_ref[group * STEP + STEP - j], masked, pow_ref, end_ref)

        by_flag(flag_ref[group] + flag_ref[group + 1], step)
        return 0

    lax.fori_loop(0, count // STEP, scan, 0)


def back_kernel(micro, keep_ref, flag_ref, spans_ref, me_ref, z_ref, rim_ref, taps_ref, cols_ref,
                lam_ref, full_ref, res_ref, skip_ref, u_ref, e_ref, dmix_ref, conv_ref,
                marks_ref, ends_ref,
                dz_ref, rimback_ref, tail_ref, dtaps_ref, dskip_ref, dres_ref, g_ref,
                zs_ref, dc_ref, di_ref, ss_ref, bt_ref):
    count, width = z_ref.shape[0], z_ref.shape[1] // 3
    poles = lam_ref.shape[0] // 2
    state_rows = 2 * poles * SUB
    keep_rows(z_ref, rim_ref, zs_ref)
    joined(ends_ref, micro, full_ref, bt_ref, spans_ref, me_ref[0], ends_ref.shape[0], True)
    bt_ref[...] = bt_ref[...] * keep_ref[count]
    for ref in (dtaps_ref, dskip_ref, dres_ref, g_ref):
        ref[...] = jnp.zeros_like(ref)

    def held(slot, k):
        return pl.ds(pl.multiple_of(slot * state_rows + k * SUB, SUB), SUB)

    def block(order, _):
        number = count // SPAN - 1 - order
        for k in range(2 * poles):
            ss_ref[held(0, k), :] = marks_ref[number, k]

        def forward(inner, _):
            group = number * (SPAN // STEP) + inner

            def step(masked):
                us = [u_ref[at(group, j), :] for j in range(STEP)]
                es = [e_ref[at(group, j), :] for j in range(STEP)]
                for k in range(poles):
                    lr, li = lam_ref[k], lam_ref[poles + k]
                    sr = ss_ref[held(inner * STEP, k), :]
                    si = ss_ref[held(inner * STEP, poles + k), :]
                    ar = ai = None
                    for j in range(STEP):
                        if masked:
                            keep = keep_ref[group * STEP + j]
                            sr, si = sr * keep, si * keep
                        sr, si = lr * sr - li * si + us[j], lr * si + li * sr
                        ss_ref[held(inner * STEP + j + 1, k), :] = sr
                        ss_ref[held(inner * STEP + j + 1, poles + k), :] = si
                        ar = es[j] * sr if ar is None else ar + es[j] * sr
                        ai = es[j] * si if ai is None else ai + es[j] * si
                    dres_ref[k] = dres_ref[k] + ar
                    dres_ref[poles + k] = dres_ref[poles + k] + ai

            by_flag(flag_ref[group], step)
            return 0

        lax.fori_loop(0, SPAN // STEP, forward, 0)

        def backward(outer, _):
            inner = SPAN // STEP - 1 - outer
            group = number * (SPAN // STEP) + inner

            def step(masked):
                es = [e_ref[at(group, j), :] for j in range(STEP)]
                ds = [None] * STEP
                for k in range(poles):
                    lr, li = lam_ref[k], lam_ref[poles + k]
                    rr, ri = res_ref[k], res_ref[poles + k]
                    tr, ti = bt_ref[k], bt_ref[poles + k]
                    gr, gi = g_ref[k], g_ref[poles + k]
                    for j in reversed(range(STEP)):
                        tr, ti = lr * tr + li * ti + es[j], lr * ti - li * tr
                        part = rr * tr + ri * ti
                        ds[j] = part if ds[j] is None else ds[j] + part
                        if masked:
                            keep = keep_ref[group * STEP + j]
                            tr, ti = tr * keep, ti * keep
                        sr = ss_ref[held(inner * STEP + j, k), :]
                        si = ss_ref[held(inner * STEP + j, poles + k), :]
                        gr = gr + (sr * tr + si * ti)
                        gi = gi + (sr * ti - si * tr)
                    bt_ref[k], bt_ref[poles + k] = tr, ti
                    g_ref[k], g_ref[poles + k] = gr, gi
                for j in range(STEP):
                    di_ref[at(group, j), :] = ds[j]

            by_flag(flag_ref[group], step)
            return 0

        lax.fori_loop(0, SPAN // STEP, backward, 0)
        return 0

    lax.fori_loop(0, count // SPAN, block, 0)

    def eighths(value):
        total = value[0:SUB]
        for start in range(SUB, ROWS, SUB):
            total = total + value[start : start + SUB]
        return total

    def natural(i, _):
        rows = pl.ds(pl.multiple_of(i * ROWS, ROWS), ROWS)
        cols = chunk_cols(cols_ref, i)
        query = filtered(zs_ref, taps_ref, cols, i, 0, width)
        key = filtered(zs_ref, taps_ref, cols, i, 1, width)
        value = filtered(zs_ref, taps_ref, cols, i, 2, width)
        mask = cols[:, 2:3]
        d_mixed = dmix_ref[rows, :].astype(F32)
        e = d_mixed * query
        dskip_ref[...] = dskip_ref[...] + eighths(e * (key * value * mask))
        d_inject = (collect(di_ref, i, width) + skip_ref[...] * e) * mask
        for stream, grad in enumerate((d_mixed * conv_ref[rows, :], d_inject * value, d_inject * key)):
            lanes = slice(stream * width, (stream + 1) * width)
            dc_ref[rows, lanes] = grad
            shifted = window(zs_ref, i, stream, width)
            for lag in range(3):
                product = grad * shifted[lag]
                if lag:
                    product = product * cols[:, lag - 1 : lag]
                slot = slice((lag * 3 + stream) * SUB, (lag * 3 + stream + 1) * SUB)
                dtaps_ref[slot, :] = dtaps_ref[slot, :] + eighths(product)
        return 0

    lax.fori_loop(0, count // ROWS, natural, 0)
    dc_ref[count : count + SUB, :] = jnp.zeros((SUB, 3 * width), F32)

    def spread_back(i, _):
        rows = pl.ds(pl.multiple_of(i * ROWS, ROWS), ROWS)
        beyond = pl.ds(pl.multiple_of(i * ROWS, ROWS), ROWS + SUB)
        cols = cols_ref[beyond, :]
        v1, v2 = cols[1 : 1 + ROWS, 0:1], cols[2 : 2 + ROWS, 1:2]
        for stream in range(3):
            lanes = slice(stream * width, (stream + 1) * width)
            wide = dc_ref[beyond, lanes]
            t0, t1, t2 = (taps_ref[lag * 3 + stream : lag * 3 + stream + 1, :] for lag in range(3))
            total = t0 * wide[0:ROWS] + (t1 * wide[1 : 1 + ROWS]) * v1 + (t2 * wide[2 : 2 + ROWS]) * v2
            dz_ref[rows, lanes] = total.astype(BF)

            @pl.when(i == count // ROWS - 1)
            def _():
                tail_ref[:, lanes] = total

        return 0

    lax.fori_loop(0, count // ROWS, spread_back, 0)
    first = cols_ref[0:SUB, :]
    for stream in range(3):
        lanes = slice(stream * width, (stream + 1) * width)
        dc = dc_ref[0:SUB, lanes]
        t1, t2 = (taps_ref[lag * 3 + stream : lag * 3 + stream + 1, :] for lag in (1, 2))
        one, two = t1 * (dc * first[:, 0:1]), t2 * (dc * first[:, 1:2])
        rimback_ref[...] = rimback_ref[...] if stream else jnp.zeros_like(rimback_ref)
        rimback_ref[0:1, lanes] = two[0:1]
        rimback_ref[1:2, lanes] = one[0:1] + two[1:2]


def call(kernel, ins, outs, scratch, smem, name, flops, after=()):
    count = len(ins)

    def without(*refs):
        kernel(*refs[:count], *refs[count + len(after) :])

    local = pl.BlockSpec(memory_space=pltpu.VMEM)
    scalar = pl.BlockSpec(memory_space=pltpu.SMEM)
    moved = sum(a.size * a.dtype.itemsize for a in ins) + sum(
        functools.reduce(lambda x, y: x * y, s) * jnp.dtype(d).itemsize for s, d in outs
    )
    return pl.pallas_call(
        without,
        out_shape=[jax.ShapeDtypeStruct(s, d) for s, d in outs],
        in_specs=[scalar] * smem + [local] * (count - smem)
        + [pl.BlockSpec(memory_space=pl.ANY)] * len(after),
        out_specs=[local] * len(outs),
        scratch_shapes=[pltpu.VMEM(s, d) for s, d in scratch],
        compiler_params=pltpu.CompilerParams(vmem_limit_bytes=VMEM_LIMIT),
        cost_estimate=pl.CostEstimate(flops=flops, bytes_accessed=moved, transcendentals=0),
        name=name,
    )(*ins, *after)


def segment_number(position, doc_lengths):
    starts_at = jnp.cumsum(doc_lengths) - doc_lengths
    hits = (starts_at[None, :] <= position[:, None]).astype(jnp.int32)
    return jnp.sum(hits, axis=1)


def norm_scale(values):
    return lax.rsqrt(jnp.mean(values * values, axis=-1, keepdims=True) + EPS)


def norm_back(values, scale, gain, grad):
    weighted = gain[None] * grad
    d_values = scale * weighted - values * scale**3 * jnp.mean(
        weighted * values, axis=-1, keepdims=True
    )
    return d_values, jnp.sum(grad * values * scale, axis=0)


def polar(exponent, decay_rate, pole_angle):
    magnitude = jnp.exp(-exponent * decay_rate)
    phase = exponent * pole_angle
    return magnitude * jnp.cos(phase), magnitude * jnp.sin(phase)


def packed(real, imag):
    rows = real.size // (SUB * LANE)
    return jnp.concatenate([real.reshape(rows, SUB, LANE), imag.reshape(rows, SUB, LANE)])


def unpacked(pair, shape):
    half = pair.shape[0] // 2
    return pair[:half].reshape(shape), pair[half:].reshape(shape)


def gather(block, axis, dim):
    return lax.all_gather(block, axis, axis=dim, tiled=True)


def scatter(block, axis, dim):
    return lax.psum_scatter(block, axis, scatter_dimension=dim, tiled=True)


CORE, X, Y = 1, 2, 4


def over(value, bit):
    return lax.ppermute(value, "seq", [(i, i ^ bit) for i in range(8)])


def place_kernel(plan, count, me_ref, *refs):
    pieces, whole, held, arrive_sem, leave_sem = refs[:count], refs[count], refs[count + 1 : -2], refs[-2], refs[-1]
    arrive, leave = [], []
    for n, (i, lanes, bits, there) in enumerate(plan):
        rows = pieces[i].shape[0]
        spot = pl.ds(pl.multiple_of((me_ref[0] ^ bits) * rows, 16), rows)
        arrive.append(pltpu.make_async_copy(pieces[i].at[:, lanes], held[n], arrive_sem.at[n]))
        leave.append(pltpu.make_async_copy(held[n], whole.at[spot, there], leave_sem.at[n]))
    for copy in arrive:
        copy.start()
    for come, go in zip(arrive, leave):
        come.wait()
        go.start()
    for copy in leave:
        copy.wait()


def place(pieces, spans, start, width, name):
    plan = []
    for i, (bits, low) in enumerate(spans):
        first, last = max(low, start), min(low + pieces[i].shape[1], start + width)
        if first < last:
            plan.append((i, pl.ds(first - low, last - first), bits, pl.ds(first - start, last - first)))
    used = sorted({entry[0] for entry in plan})
    plan = [(used.index(i), *entry) for i, *entry in plan]
    pieces = [pieces[i] for i in used]
    rows, count, dtype = pieces[0].shape[0], len(pieces), pieces[0].dtype
    anywhere = pl.BlockSpec(memory_space=pl.ANY)
    return pl.pallas_call(
        functools.partial(place_kernel, plan, count),
        out_shape=jax.ShapeDtypeStruct((8 * rows, width), dtype),
        in_specs=[pl.BlockSpec(memory_space=pltpu.SMEM)] + [anywhere] * count,
        out_specs=anywhere,
        scratch_shapes=[pltpu.VMEM((rows, lanes.size), dtype) for _, lanes, _, _ in plan]
        + [pltpu.SemaphoreType.DMA((len(plan),)) for _ in range(2)],
        compiler_params=pltpu.CompilerParams(vmem_limit_bytes=VMEM_LIMIT),
        cost_estimate=pl.CostEstimate(flops=0, bytes_accessed=32 * rows * width, transcendentals=0),
        name=name,
    )(lax.axis_index("seq").astype(jnp.int32).reshape(1), *pieces)


def seq_links(block, half):
    if lax.axis_size("seq") != 8:
        return (block,)
    from_x, from_y = over(block, X), over(block, Y)
    return block, from_x, from_y, over(from_x[:, :half], Y), over(from_y[:, half:], X)


def seq_gather(blocks, widths, names):
    starts = [sum(widths[:i]) for i in range(len(widths))]
    if lax.axis_size("seq") != 8:
        whole = gather(blocks[0], "seq", 0)
        return [whole[:, start : start + width] for start, width in zip(starts, widths)]
    pieces = [*blocks, *[over(block, CORE) for block in blocks]]
    half = blocks[3].shape[1]
    spans = [
        (bits + core, low)
        for core in (0, CORE)
        for bits, low in ((0, 0), (X, 0), (Y, 0), (X + Y, 0), (X + Y, half))
    ]
    return [place(pieces, spans, *cut) for cut in zip(starts, widths, names)]


def plus(*terms):
    total = terms[0].astype(F32)
    for term in terms[1:]:
        total = total + term.astype(F32)
    return total


def halves_kernel(micros, core_ref, *refs):
    lefts, rights, send_ref, keep_ref = refs[:micros], refs[micros : 2 * micros], refs[-2], refs[-1]
    total = None
    for left, right in zip(lefts, rights):
        part = lax.dot_general(left[...], right[...], (((0,), (0,)), ((), ())), preferred_element_type=F32)
        total = part if total is None else total + part

    @pl.when(pl.program_id(0) < 4)
    def _():
        send_ref[...] = total.astype(BF)

    @pl.when(pl.program_id(0) >= 4)
    def _():
        keep_ref[...] = total.astype(BF)


def grad_halves(lefts, rights, name, after=()):
    if lax.axis_size("seq") != 8:
        return (dot(jnp.concatenate(lefts), jnp.concatenate(rights), ((0,), (0,))).astype(BF),)
    count, wide = lefts[0].shape
    rows, width, n = wide // 8, rights[0].shape[1], len(lefts)
    core = (lax.axis_index("seq") & CORE).astype(jnp.int32).reshape(1)
    return pl.pallas_call(
        functools.partial(halves_kernel, n),
        out_shape=[jax.ShapeDtypeStruct((wide // 2, width), BF)] * 2,
        grid_spec=pltpu.PrefetchScalarGridSpec(
            num_scalar_prefetch=1,
            grid=(8,),
            in_specs=[
                pl.BlockSpec((count, rows), lambda i, c: (0, 2 * (i % 4) + jnp.where(i < 4, 1 - c[0], c[0])))
            ] * n
            + [pl.BlockSpec((count, width), lambda i, c: (0, 0))] * n
            + [pl.BlockSpec(memory_space=pl.ANY)] * len(after),
            out_specs=[
                pl.BlockSpec((rows, width), lambda i, c: (jnp.minimum(i, 3), 0)),
                pl.BlockSpec((rows, width), lambda i, c: (jnp.maximum(i, 4) - 4, 0)),
            ],
        ),
        compiler_params=pltpu.CompilerParams(vmem_limit_bytes=VMEM_LIMIT),
        cost_estimate=pl.CostEstimate(
            flops=2 * n * count * wide * width,
            bytes_accessed=2 * n * count * (wide + width) + 2 * wide * width,
            transcendentals=0,
        ),
        name=name,
    )(core, *lefts, *rights, *after)


def grad_chip(halves, after=()):
    if len(halves) == 1:
        return halves[0]
    send, keep = halves
    four = plus(keep, over(send, CORE), nothing_of(after)).astype(BF)
    return four.reshape(4, keep.shape[0] // 4, keep.shape[1])


def owner(four, bits):
    return lax.dynamic_index_in_dim(four, (lax.axis_index("seq") // 2) ^ (bits // 2), 0, keepdims=False)


def grad_far(four, relay, after=()):
    if four.ndim == 2:
        return four
    return over(tied(owner(four, X + Y), *after), relay)


def grad_turn(four, far, relay, after=()):
    if four.ndim == 2:
        return (four,)
    nothing = nothing_of(after)
    to_x, to_y = owner(four, X).astype(F32) + nothing, owner(four, Y).astype(F32) + nothing
    if relay == Y:
        to_x = plus(to_x, far)
    else:
        to_y = plus(to_y, far)
    return to_x.astype(BF), to_y.astype(BF)


def grad_own(four, turn, after=()):
    if four.ndim == 2:
        return scatter(four, "seq", 0).astype(F32)
    return plus(owner(four, 0), over(turn[0], X), over(turn[1], Y), nothing_of(after))


def tp_sum(block):
    count = lax.axis_size("tp")
    return plus(block, *[
        lax.ppermute(block, "tp", [(i, (i + hop) % count) for i in range(count)])
        for hop in range(1, count)
    ])


def nothing_of(others):
    return sum([other[(0,) * other.ndim].astype(F32) * 0.0 for other in others], jnp.zeros((), F32))


def tied(value, *others):
    return value + nothing_of(others).astype(value.dtype) if others else value


def dot(a, b, dims):
    return lax.dot_general(a, b, (dims, ((), ())), preferred_element_type=F32)


def shards(tokens, lengths, pad_mask, gain_in, w_in, conv_taps, log_rate, pole_angle, residues,
           skip_gain, w_out, gain_mlp, w_gu, w_down, cotangent):
    micros, count, width = tokens.shape
    n_seq, n_tp = lax.axis_size("seq"), lax.axis_size("tp")
    me = lax.axis_index("seq")
    hidden = w_gu.shape[2]
    joint = jnp.concatenate([tokens.reshape(micros * count, width), w_out.T])
    joint = gather(joint, "tp", 1)
    x_full = joint[: micros * count].reshape(micros, count, -1)
    out_lanes = joint[micros * count :]
    rows_in = w_in.shape[0]
    first_links = seq_links(jnp.concatenate([w_in.reshape(rows_in, -1), w_gu.reshape(rows_in, -1)], axis=1), 3 * width)
    in_full, gu_full = seq_gather(first_links, (3 * width, 2 * hidden), ("place_in", "place_gu"))
    cot_full = [gather(cotangent[0], "tp", 1)]
    down_full = gather(tied(w_down.T, *first_links[-2:]), "seq", 0)
    out_links = seq_links(out_lanes, out_lanes.shape[1] // 2)
    (out_full,) = seq_gather(out_links, (n_tp * width,), ("place_out",))

    rate = jnp.exp(log_rate)
    lam_real, lam_imag = polar(1.0, rate, pole_angle)
    lam = packed(lam_real, lam_imag)
    powers = [(lam_real, lam_imag)] + [polar(n, rate, pole_angle) for n in (2.0, 4.0, 8.0)]
    pow_ahead = jnp.concatenate([packed(real, imag) for real, imag in powers])
    pow_back = jnp.concatenate([packed(real, -imag) for real, imag in powers])
    lam_all = packed(*polar(float(count), rate, pole_angle))
    res = packed(residues[0], residues[1])
    taps = conv_taps.reshape(9, width)
    skip = skip_gain.reshape(1, width)
    me_word = me.astype(jnp.int32).reshape(1)
    edges = jnp.arange(n_seq + 1) * count
    seq_shape = (count * SUB, LANE)
    st_shape = lam.shape
    work = 400 * lam.shape[0] * SUB * LANE * count

    position = me * count + jnp.arange(-2, count + 1)
    seg = jnp.stack([segment_number(position, lengths[m]) for m in range(micros)])
    valid1 = (seg[:, 2:] == seg[:, 1:-1]).astype(F32)
    valid2 = (seg[:, 2:] == seg[:, :-2]).astype(F32)
    inside = (jnp.arange(count + 1) < count) | (me < n_seq - 1)
    keeps = jnp.pad(valid1 * inside[None].astype(F32), ((0, 0), (0, SUB - 1)))
    group_flags = jnp.any(keeps.reshape(micros, -1, STEP) == 0, axis=2).astype(jnp.int32)
    columns = jnp.stack([valid1[:, :count], valid2[:, :count], pad_mask.astype(F32)], axis=2)
    columns = jnp.pad(columns, ((0, 0), (0, SUB), (0, SUB - 3)))

    x_wide = x_full.astype(F32)
    scale_in = norm_scale(x_wide)
    h_in = (x_wide * scale_in * gain_in).astype(BF)
    z_low = dot(h_in, in_full, ((2,), (0,))).astype(BF)
    rims = lax.ppermute(z_low[:, count - 2 :], "seq", [(i, i + 1) for i in range(n_seq - 1)])
    rims = jnp.pad(rims.astype(F32), ((0, 0), (SUB - 2, 0), (0, 0)))
    zs = ((count + SUB, 3 * width), F32)
    bases = [(z_low[m], rims[m], taps, columns[m], lam) for m in range(micros)]
    masks = [(keeps[m], group_flags[m]) for m in range(micros)]
    last = [segment_number(edges - 1, lengths[m]) for m in range(micros)]
    first = [segment_number(edges, lengths[m]) for m in range(micros)]
    spans = [(v[1:] == v[:-1]).astype(F32) for v in last]
    spans_back = [(v[1:] == v[:-1]).astype(F32) for v in first]
    injects, ends = zip(*[
        call(front_kernel, (*masks[m], *bases[m][:-1], pow_ahead), [(seq_shape, F32), (st_shape, F32)],
             [zs], 2, "mixer_front", 4 * work)
        for m in range(micros)
    ])
    ends = lax.all_gather(tied(jnp.stack(ends), *out_links[1:3]).astype(BF), "seq").astype(F32)

    kept = []
    outputs = []
    for m in range(micros):
        mixed, conv_out, marks = call(
            functools.partial(finish_kernel, m),
            (*masks[m], spans[m], me_word, *bases[m], lam_all, res, skip, injects[m], ends),
            [((count, width), BF), ((count, width), F32), ((count // SPAN, *st_shape), F32)],
            [zs, (seq_shape, F32), (st_shape, F32)], 4, "mixer_finish", 5 * work,
            (kept[0]["mixed"], down_full) if m else cot_full,
        )
        kept.append(dict(mixed=mixed, conv=conv_out, marks=marks))

    order = ()
    for m in range(micros):
        mixed_full = gather(kept[m]["mixed"], "tp", 1)
        if m + 1 < micros:
            cot_full.append(gather(tied(cotangent[m + 1], mixed_full), "tp", 1))
        x_mid = tied(x_full[m].astype(F32), *order) + dot(mixed_full, out_full, ((1,), (1,)))
        scale_mid = norm_scale(x_mid)
        h_mlp = (x_mid * scale_mid * gain_mlp[None]).astype(BF)
        gate_up = dot(h_mlp, gu_full, ((1,), (0,)))
        gate, up = gate_up[:, :hidden], gate_up[:, hidden:]
        sig = jax.nn.sigmoid(gate)
        act = (gate * sig * up).astype(BF)
        down_own = scatter(dot(act, down_full, ((1,), (1,))).astype(BF), "tp", 1)
        mid_own = lax.dynamic_slice_in_dim(x_mid, lax.axis_index("tp") * width, width, 1)
        outputs.append((mid_own, down_own))

        cot = cot_full[m]
        d_act = dot(cot, down_full, ((1,), (0,)))
        d_gu = jnp.concatenate(
            [d_act * up * sig * (1.0 + gate * (1.0 - sig)), d_act * gate * sig], axis=1
        ).astype(BF)
        d_h = dot(d_gu, gu_full, ((1,), (1,)))
        d_norm, d_gain_mlp = norm_back(x_mid, scale_mid, gain_mlp, d_h)
        d_mid = d_norm + cot.astype(F32) * (1.0 / n_tp)
        d_low = d_mid.astype(BF)
        d_mixed = dot(d_low, out_full, ((1,), (0,))).astype(BF)
        order = (d_mixed,)
        d_mixed = scatter(d_mixed, "tp", 1)
        kept[m].update(
            mixed=mixed_full, h_mlp=h_mlp, act=act, d_gu=d_gu, d_mid=d_mid, d_low=d_low,
            d_mixed=d_mixed, d_gain_mlp=d_gain_mlp,
        )

    def each(name):
        return [c[name] for c in kept]

    down_halves = grad_halves(cot_full, each("act"), "grad_down", order)
    out_halves = grad_halves(each("d_low"), each("mixed"), "grad_out", order)
    down_chip, out_chip = grad_chip(down_halves), grad_chip(out_halves)
    down_far, out_far = grad_far(down_chip, Y), grad_far(out_chip, X)
    adjoints, ends = zip(*[
        call(adjoint_kernel, (*masks[m], *bases[m][:-1], pow_back, kept[m]["d_mixed"]),
             [(seq_shape, F32), (st_shape, F32)], [zs], 2, "mixer_adjoint", 4 * work,
             (down_chip, out_chip) if m else (*down_halves, *out_halves))
        for m in range(micros)
    ])
    ends = lax.all_gather(tied(jnp.stack(ends), down_far, out_far).astype(BF), "seq").astype(F32)
    gu_halves = grad_halves(each("h_mlp"), each("d_gu"), "grad_gu", (ends,))
    gu_chip = grad_chip(gu_halves)
    gu_far = grad_far(gu_chip, X)
    down_turn = grad_turn(down_chip, down_far, Y, (ends,))
    g_out = grad_own(out_chip, grad_turn(out_chip, out_far, X, (ends,)))
    g_out = scatter(tied(g_out, *gu_halves).astype(BF), "tp", 1)

    token_grads = []
    partial_grads = []
    smalls = []
    for m in range(micros):
        c = kept[m]
        d_z, rim_back, tail, d_taps, d_skip, d_res, d_lam = call(
            functools.partial(back_kernel, m),
            (*masks[m], spans_back[m], me_word, *bases[m], lam_all, res, skip, injects[m],
             adjoints[m], c["d_mixed"], c["conv"], c["marks"], ends),
            [((count, 3 * width), BF), ((SUB, 3 * width), F32), ((ROWS, 3 * width), F32),
             ((9 * SUB, width), F32), ((SUB, width), F32), (st_shape, F32), (st_shape, F32)],
            [zs, ((count + SUB, 3 * width), F32), (seq_shape, F32),
             (((SPAN + 1) * st_shape[0] * SUB, LANE), F32), (st_shape, F32)],
            4, "mixer_back", 12 * work, (*partial_grads, *gu_turn) if m else (*gu_halves, gu_chip),
        )
        rim_back = lax.ppermute(rim_back[:2], "seq", [(i + 1, i) for i in range(n_seq - 1)])
        if m == 0:
            gu_turn = grad_turn(gu_chip, gu_far, X, (rim_back,))
            g_gu = grad_own(gu_chip, gu_turn)
        tail = tied(tail, g_gu if m else gu_far)
        tail = (tail + jnp.concatenate([jnp.zeros((ROWS - 2, 3 * width), F32), rim_back])).astype(BF)
        d_z = lax.dynamic_update_slice(d_z, tail, (count - ROWS, 0))
        c["d_z"] = d_z
        gain = gain_in
        if m == micros - 1:
            in_halves = grad_halves([h_in[i] for i in range(micros)], each("d_z"), "grad_in")
            gain = tied(gain_in, in_halves[0])
        d_h_in = dot(d_z, in_full, ((1,), (1,)))
        d_norm, d_gain_in = norm_back(x_full[m].astype(F32), scale_in[m], gain, d_h_in)
        gains = [d_gain_in, c["d_gain_mlp"]] if m == 0 else [gains[0] + d_gain_in, gains[1] + c["d_gain_mlp"]]
        if m == micros - 1:
            gains = tp_sum(jnp.concatenate(gains).reshape(-1, width).astype(BF))
            d_norm = tied(d_norm, gains)
        partial_grads.append((c["d_mid"] + d_norm).astype(BF))
        token_grads.append(scatter(partial_grads[m], "tp", 1))
        smalls.append((d_taps, d_lam, d_res, d_skip))

    in_chip = grad_chip(in_halves)
    d_taps, d_lam, d_res, d_skip = (sum(parts) for parts in zip(*smalls))
    g_real, g_imag = unpacked(d_lam, log_rate.shape)
    s_real, s_imag = unpacked(d_res, log_rate.shape)
    h_real = residues[0] * g_real + residues[1] * g_imag
    h_imag = residues[0] * g_imag - residues[1] * g_real
    small = jnp.concatenate([
        jnp.sum(d_taps.reshape(9, SUB, width), axis=1),
        -rate * (lam_real * h_real + lam_imag * h_imag),
        lam_real * h_imag - lam_imag * h_real,
        s_real, -s_imag,
        jnp.sum(d_skip, axis=0, keepdims=True),
        gains,
    ])
    small = jnp.sum(lax.all_gather(small.astype(BF), "seq").astype(F32), axis=0)
    in_far = grad_far(in_chip, Y, (small,))
    g_in = grad_own(in_chip, grad_turn(in_chip, in_far, Y, (small,)))
    g_down = grad_own(down_chip, down_turn, (in_far,))
    gains = small[-gains.shape[0] :]
    n_gain = gains.shape[0]
    n_pole = log_rate.shape[0]
    cuts = [9, 9 + n_pole, 9 + 2 * n_pole, 9 + 3 * n_pole, 9 + 4 * n_pole]
    return (
        jnp.stack([(mid + tied(down.astype(F32), in_far)).astype(BF) for mid, down in outputs]),
        jnp.stack(token_grads),
        gains[: n_gain // 2].reshape(-1),
        g_in.reshape(w_in.shape),
        small[: cuts[0]].reshape(conv_taps.shape),
        small[cuts[0] : cuts[1]],
        small[cuts[1] : cuts[2]],
        small[cuts[2] : cuts[4]].reshape(residues.shape),
        small[cuts[4]],
        tied(g_out.astype(F32), in_far).T,
        gains[n_gain // 2 :].reshape(-1),
        tied(g_gu, in_far).reshape(w_gu.shape),
        g_down.T,
    )


def solution(mesh):
    wide, deep, flat = P(None, "seq", "tp"), P("seq", None, "tp"), P("tp", "seq")
    poles, taps = P(None, "tp"), P(None, None, "tp")
    return jax.shard_map(
        shards,
        mesh=mesh,
        in_specs=(wide, P(), P(None, "seq"), P(), deep, taps, poles, poles, taps, P("tp"), flat,
                  P(), deep, flat, wide),
        out_specs=(wide, wide, P(), deep, taps, poles, poles, taps, P("tp"), flat, P(), deep, flat),
        check_vma=False,
    )
```

```python
import functools

import jax
import jax.numpy as jnp
from jax import lax
from jax.experimental import pallas as pl
from jax.experimental.pallas import tpu as pltpu
from jax.sharding import PartitionSpec as P

EPS = 1e-06
SPAN = 64
STEP = 8
ROWS = 64
SUB, LANE = 8, 128
BF, F32 = jnp.bfloat16, jnp.float32
VMEM_LIMIT = 56 * 1024 * 1024


def keep_rows(z_ref, rim_ref, zs_ref, streams=(0, 3)):
    width = z_ref.shape[1] // 3
    lanes = slice(streams[0] * width, streams[1] * width)
    zs_ref[0:SUB, lanes] = rim_ref[:, lanes]

    def body(i, _):
        rows = pl.ds(pl.multiple_of(i * ROWS, ROWS), ROWS)
        zs_ref[pl.ds(pl.multiple_of(i * ROWS + SUB, SUB), ROWS), lanes] = z_ref[rows, lanes].astype(F32)
        return 0

    lax.fori_loop(0, z_ref.shape[0] // ROWS, body, 0)


def window(zs_ref, i, stream, width):
    rows = pl.ds(pl.multiple_of(i * ROWS, ROWS), ROWS + SUB)
    wide = zs_ref[rows, stream * width : (stream + 1) * width]
    return wide[8 : 8 + ROWS], wide[7 : 7 + ROWS], wide[6 : 6 + ROWS]


def filtered(zs_ref, taps_ref, cols, i, stream, width):
    z0, z1, z2 = window(zs_ref, i, stream, width)
    t0, t1, t2 = (taps_ref[lag * 3 + stream : lag * 3 + stream + 1, :] for lag in range(3))
    return t0 * z0 + (t1 * z1) * cols[:, 0:1] + (t2 * z2) * cols[:, 1:2]


def spread(ref, i, value):
    parts = value.shape[1] // LANE
    for c in range(parts):
        piece = value[:, c * LANE : (c + 1) * LANE]
        for half in range(SUB // parts):
            ref[pl.ds(i * (ROWS * SUB) + half * parts + c, ROWS, stride=SUB), :] = piece


def collect(ref, i, width):
    parts = width // LANE
    pieces = []
    for c in range(parts):
        piece = ref[pl.ds(i * (ROWS * SUB) + c, ROWS, stride=SUB), :]
        for half in range(1, SUB // parts):
            piece = piece + ref[pl.ds(i * (ROWS * SUB) + half * parts + c, ROWS, stride=SUB), :]
        pieces.append(piece)
    return jnp.concatenate(pieces, axis=1)


def chunk_cols(cols_ref, i):
    return cols_ref[pl.ds(pl.multiple_of(i * ROWS, ROWS), ROWS), :]


def at(group, j):
    return pl.ds(pl.multiple_of((group * STEP + j) * SUB, SUB), SUB)


def by_flag(flag, step):
    @pl.when(flag == 0)
    def _():
        step(False)

    @pl.when(flag != 0)
    def _():
        step(True)


def eight_steps(values, powers, real, imag):
    def join(earlier, later, n):
        pr, pi = powers[n]
        return pr * earlier[0] - pi * earlier[1] + later[0], pr * earlier[1] + pi * earlier[0] + later[1]

    pr, pi = powers[0]
    pairs = [(pr * values[j] + values[j + 1], pi * values[j]) for j in range(0, STEP, 2)]
    fours = [join(pairs[j], pairs[j + 1], 1) for j in (0, 2)]
    return join((real, imag), join(*fours, 2), 3)


def end_scan(values, keep_of, masked, pow_ref, end_ref):
    poles = end_ref.shape[0] // 2
    for k in range(poles):
        sr, si = end_ref[k], end_ref[poles + k]
        if masked:
            lr, li = pow_ref[k], pow_ref[poles + k]
            for j in range(STEP):
                keep = keep_of(j)
                sr, si = sr * keep, si * keep
                sr, si = lr * sr - li * si + values[j], lr * si + li * sr
        else:
            powers = [(pow_ref[2 * poles * n + k], pow_ref[2 * poles * n + poles + k]) for n in range(4)]
            sr, si = eight_steps(values, powers, sr, si)
        end_ref[k], end_ref[poles + k] = sr, si


def front_kernel(keep_ref, flag_ref, z_ref, rim_ref, taps_ref, cols_ref, pow_ref,
                 u_ref, end_ref, zs_ref):
    count, width = z_ref.shape[0], z_ref.shape[1] // 3
    keep_rows(z_ref, rim_ref, zs_ref, (1, 3))

    def natural(i, _):
        cols = chunk_cols(cols_ref, i)
        key = filtered(zs_ref, taps_ref, cols, i, 1, width)
        value = filtered(zs_ref, taps_ref, cols, i, 2, width)
        spread(u_ref, i, key * value * cols[:, 2:3])
        return 0

    lax.fori_loop(0, count // ROWS, natural, 0)
    end_ref[...] = jnp.zeros_like(end_ref)

    def scan(group, _):
        def step(masked):
            us = [u_ref[at(group, j), :] for j in range(STEP)]
            end_scan(us, lambda j: keep_ref[group * STEP + j], masked, pow_ref, end_ref)

        by_flag(flag_ref[group], step)
        return 0

    lax.fori_loop(0, count // STEP, scan, 0)


def joined(all_ref, micro, full_ref, carry_ref, spans_ref, me, count, conj):
    poles = full_ref.shape[0] // 2
    carry_ref[...] = jnp.zeros_like(carry_ref)

    def hop(order, _):
        j = count - 1 - order if conj else order
        span = spans_ref[j]
        for k in range(poles):
            lr, li = full_ref[k] * span, full_ref[poles + k] * (-span if conj else span)
            sr, si = carry_ref[k], carry_ref[poles + k]
            carry_ref[k] = lr * sr - li * si + all_ref[j, micro, k]
            carry_ref[poles + k] = lr * si + li * sr + all_ref[j, micro, poles + k]
        return 0

    lax.fori_loop(0, count - 1 - me if conj else me, hop, 0)


def finish_kernel(micro, keep_ref, flag_ref, spans_ref, me_ref, z_ref, rim_ref, taps_ref, cols_ref,
                  lam_ref, full_ref, res_ref, skip_ref, u_ref, ends_ref,
                  mixed_ref, conv_ref, marks_ref, zs_ref, y_ref, st_ref):
    count, width = z_ref.shape[0], z_ref.shape[1] // 3
    poles = lam_ref.shape[0] // 2
    keep_rows(z_ref, rim_ref, zs_ref)
    joined(ends_ref, micro, full_ref, st_ref, spans_ref, me_ref[0], ends_ref.shape[0], False)

    def scan(group, _):
        @pl.when(group % (SPAN // STEP) == 0)
        def _():
            marks_ref[group // (SPAN // STEP)] = st_ref[...]

        def step(masked):
            us = [u_ref[at(group, j), :] for j in range(STEP)]
            ys = [None] * STEP
            for k in range(poles):
                lr, li = lam_ref[k], lam_ref[poles + k]
                rr, ri = res_ref[k], res_ref[poles + k]
                sr, si = st_ref[k], st_ref[poles + k]
                for j in range(STEP):
                    if masked:
                        keep = keep_ref[group * STEP + j]
                        sr, si = sr * keep, si * keep
                    sr, si = lr * sr - li * si + us[j], lr * si + li * sr
                    part = rr * sr - ri * si
                    ys[j] = part if ys[j] is None else ys[j] + part
                st_ref[k], st_ref[poles + k] = sr, si
            for j in range(STEP):
                y_ref[at(group, j), :] = ys[j]

        by_flag(flag_ref[group], step)
        return 0

    lax.fori_loop(0, count // STEP, scan, 0)

    def natural(i, _):
        rows = pl.ds(pl.multiple_of(i * ROWS, ROWS), ROWS)
        cols = chunk_cols(cols_ref, i)
        query = filtered(zs_ref, taps_ref, cols, i, 0, width)
        key = filtered(zs_ref, taps_ref, cols, i, 1, width)
        value = filtered(zs_ref, taps_ref, cols, i, 2, width)
        conv = collect(y_ref, i, width) + skip_ref[...] * (key * value * cols[:, 2:3])
        conv_ref[rows, :] = conv
        mixed_ref[rows, :] = (query * conv).astype(BF)
        return 0

    lax.fori_loop(0, count // ROWS, natural, 0)


def adjoint_kernel(keep_ref, flag_ref, z_ref, rim_ref, taps_ref, cols_ref, pow_ref, dmix_ref,
                   e_ref, end_ref, zs_ref):
    count, width = z_ref.shape[0], z_ref.shape[1] // 3
    keep_rows(z_ref, rim_ref, zs_ref, (0, 1))

    def natural(i, _):
        rows = pl.ds(pl.multiple_of(i * ROWS, ROWS), ROWS)
        query = filtered(zs_ref, taps_ref, chunk_cols(cols_ref, i), i, 0, width)
        spread(e_ref, i, dmix_ref[rows, :].astype(F32) * query)
        return 0

    lax.fori_loop(0, count // ROWS, natural, 0)
    end_ref[...] = jnp.zeros_like(end_ref)

    def scan(order, _):
        group = count // STEP - 1 - order

        def step(masked):
            es = [e_ref[at(group, STEP - 1 - j), :] for j in range(STEP)]
            end_scan(es, lambda j: keep_ref[group * STEP + STEP - j], masked, pow_ref, end_ref)

        by_flag(flag_ref[group] + flag_ref[group + 1], step)
        return 0

    lax.fori_loop(0, count // STEP, scan, 0)


def back_kernel(micro, keep_ref, flag_ref, spans_ref, me_ref, z_ref, rim_ref, taps_ref, cols_ref,
                lam_ref, full_ref, res_ref, skip_ref, u_ref, e_ref, dmix_ref, conv_ref,
                marks_ref, ends_ref,
                dz_ref, rimback_ref, tail_ref, dtaps_ref, dskip_ref, dres_ref, g_ref,
                zs_ref, dc_ref, di_ref, ss_ref, bt_ref):
    count, width = z_ref.shape[0], z_ref.shape[1] // 3
    poles = lam_ref.shape[0] // 2
    state_rows = 2 * poles * SUB
    keep_rows(z_ref, rim_ref, zs_ref)
    joined(ends_ref, micro, full_ref, bt_ref, spans_ref, me_ref[0], ends_ref.shape[0], True)
    bt_ref[...] = bt_ref[...] * keep_ref[count]
    for ref in (dtaps_ref, dskip_ref, dres_ref, g_ref):
        ref[...] = jnp.zeros_like(ref)

    def held(slot, k):
        return pl.ds(pl.multiple_of(slot * state_rows + k * SUB, SUB), SUB)

    def block(order, _):
        number = count // SPAN - 1 - order
        for k in range(2 * poles):
            ss_ref[held(0, k), :] = marks_ref[number, k]

        def forward(inner, _):
            group = number * (SPAN // STEP) + inner

            def step(masked):
                us = [u_ref[at(group, j), :] for j in range(STEP)]
                es = [e_ref[at(group, j), :] for j in range(STEP)]
                for k in range(poles):
                    lr, li = lam_ref[k], lam_ref[poles + k]
                    sr = ss_ref[held(inner * STEP, k), :]
                    si = ss_ref[held(inner * STEP, poles + k), :]
                    ar = ai = None
                    for j in range(STEP):
                        if masked:
                            keep = keep_ref[group * STEP + j]
                            sr, si = sr * keep, si * keep
                        sr, si = lr * sr - li * si + us[j], lr * si + li * sr
                        ss_ref[held(inner * STEP + j + 1, k), :] = sr
                        ss_ref[held(inner * STEP + j + 1, poles + k), :] = si
                        ar = es[j] * sr if ar is None else ar + es[j] * sr
                        ai = es[j] * si if ai is None else ai + es[j] * si
                    dres_ref[k] = dres_ref[k] + ar
                    dres_ref[poles + k] = dres_ref[poles + k] + ai

            by_flag(flag_ref[group], step)
            return 0

        lax.fori_loop(0, SPAN // STEP, forward, 0)

        def backward(outer, _):
            inner = SPAN // STEP - 1 - outer
            group = number * (SPAN // STEP) + inner

            def step(masked):
                es = [e_ref[at(group, j), :] for j in range(STEP)]
                ds = [None] * STEP
                for k in range(poles):
                    lr, li = lam_ref[k], lam_ref[poles + k]
                    rr, ri = res_ref[k], res_ref[poles + k]
                    tr, ti = bt_ref[k], bt_ref[poles + k]
                    gr, gi = g_ref[k], g_ref[poles + k]
                    for j in reversed(range(STEP)):
                        tr, ti = lr * tr + li * ti + es[j], lr * ti - li * tr
                        part = rr * tr + ri * ti
                        ds[j] = part if ds[j] is None else ds[j] + part
                        if masked:
                            keep = keep_ref[group * STEP + j]
                            tr, ti = tr * keep, ti * keep
                        sr = ss_ref[held(inner * STEP + j, k), :]
                        si = ss_ref[held(inner * STEP + j, poles + k), :]
                        gr = gr + (sr * tr + si * ti)
                        gi = gi + (sr * ti - si * tr)
                    bt_ref[k], bt_ref[poles + k] = tr, ti
                    g_ref[k], g_ref[poles + k] = gr, gi
                for j in range(STEP):
                    di_ref[at(group, j), :] = ds[j]

            by_flag(flag_ref[group], step)
            return 0

        lax.fori_loop(0, SPAN // STEP, backward, 0)
        return 0

    lax.fori_loop(0, count // SPAN, block, 0)

    def eighths(value):
        total = value[0:SUB]
        for start in range(SUB, ROWS, SUB):
            total = total + value[start : start + SUB]
        return total

    def natural(i, _):
        rows = pl.ds(pl.multiple_of(i * ROWS, ROWS), ROWS)
        cols = chunk_cols(cols_ref, i)
        query = filtered(zs_ref, taps_ref, cols, i, 0, width)
        key = filtered(zs_ref, taps_ref, cols, i, 1, width)
        value = filtered(zs_ref, taps_ref, cols, i, 2, width)
        mask = cols[:, 2:3]
        d_mixed = dmix_ref[rows, :].astype(F32)
        e = d_mixed * query
        dskip_ref[...] = dskip_ref[...] + eighths(e * (key * value * mask))
        d_inject = (collect(di_ref, i, width) + skip_ref[...] * e) * mask
        for stream, grad in enumerate((d_mixed * conv_ref[rows, :], d_inject * value, d_inject * key)):
            lanes = slice(stream * width, (stream + 1) * width)
            dc_ref[rows, lanes] = grad
            shifted = window(zs_ref, i, stream, width)
            for lag in range(3):
                product = grad * shifted[lag]
                if lag:
                    product = product * cols[:, lag - 1 : lag]
                slot = slice((lag * 3 + stream) * SUB, (lag * 3 + stream + 1) * SUB)
                dtaps_ref[slot, :] = dtaps_ref[slot, :] + eighths(product)
        return 0

    lax.fori_loop(0, count // ROWS, natural, 0)
    dc_ref[count : count + SUB, :] = jnp.zeros((SUB, 3 * width), F32)

    def spread_back(i, _):
        rows = pl.ds(pl.multiple_of(i * ROWS, ROWS), ROWS)
        beyond = pl.ds(pl.multiple_of(i * ROWS, ROWS), ROWS + SUB)
        cols = cols_ref[beyond, :]
        v1, v2 = cols[1 : 1 + ROWS, 0:1], cols[2 : 2 + ROWS, 1:2]
        for stream in range(3):
            lanes = slice(stream * width, (stream + 1) * width)
            wide = dc_ref[beyond, lanes]
            t0, t1, t2 = (taps_ref[lag * 3 + stream : lag * 3 + stream + 1, :] for lag in range(3))
            total = t0 * wide[0:ROWS] + (t1 * wide[1 : 1 + ROWS]) * v1 + (t2 * wide[2 : 2 + ROWS]) * v2
            dz_ref[rows, lanes] = total.astype(BF)

            @pl.when(i == count // ROWS - 1)
            def _():
                tail_ref[:, lanes] = total

        return 0

    lax.fori_loop(0, count // ROWS, spread_back, 0)
    first = cols_ref[0:SUB, :]
    for stream in range(3):
        lanes = slice(stream * width, (stream + 1) * width)
        dc = dc_ref[0:SUB, lanes]
        t1, t2 = (taps_ref[lag * 3 + stream : lag * 3 + stream + 1, :] for lag in (1, 2))
        one, two = t1 * (dc * first[:, 0:1]), t2 * (dc * first[:, 1:2])
        rimback_ref[...] = rimback_ref[...] if stream else jnp.zeros_like(rimback_ref)
        rimback_ref[0:1, lanes] = two[0:1]
        rimback_ref[1:2, lanes] = one[0:1] + two[1:2]


def call(kernel, ins, outs, scratch, smem, name, flops, after=()):
    count = len(ins)

    def without(*refs):
        kernel(*refs[:count], *refs[count + len(after) :])

    local = pl.BlockSpec(memory_space=pltpu.VMEM)
    scalar = pl.BlockSpec(memory_space=pltpu.SMEM)
    moved = sum(a.size * a.dtype.itemsize for a in ins) + sum(
        functools.reduce(lambda x, y: x * y, s) * jnp.dtype(d).itemsize for s, d in outs
    )
    return pl.pallas_call(
        without,
        out_shape=[jax.ShapeDtypeStruct(s, d) for s, d in outs],
        in_specs=[scalar] * smem + [local] * (count - smem)
        + [pl.BlockSpec(memory_space=pl.ANY)] * len(after),
        out_specs=[local] * len(outs),
        scratch_shapes=[pltpu.VMEM(s, d) for s, d in scratch],
        compiler_params=pltpu.CompilerParams(vmem_limit_bytes=VMEM_LIMIT),
        cost_estimate=pl.CostEstimate(flops=flops, bytes_accessed=moved, transcendentals=0),
        name=name,
    )(*ins, *after)


def segment_number(position, doc_lengths):
    starts_at = jnp.cumsum(doc_lengths) - doc_lengths
    hits = (starts_at[None, :] <= position[:, None]).astype(jnp.int32)
    return jnp.sum(hits, axis=1)


def norm_scale(values):
    return lax.rsqrt(jnp.mean(values * values, axis=-1, keepdims=True) + EPS)


def norm_back(values, scale, gain, grad):
    weighted = gain[None] * grad
    d_values = scale * weighted - values * scale**3 * jnp.mean(
        weighted * values, axis=-1, keepdims=True
    )
    return d_values, jnp.sum(grad * values * scale, axis=0)


def polar(exponent, decay_rate, pole_angle):
    magnitude = jnp.exp(-exponent * decay_rate)
    phase = exponent * pole_angle
    return magnitude * jnp.cos(phase), magnitude * jnp.sin(phase)


def packed(real, imag):
    rows = real.size // (SUB * LANE)
    return jnp.concatenate([real.reshape(rows, SUB, LANE), imag.reshape(rows, SUB, LANE)])


def unpacked(pair, shape):
    half = pair.shape[0] // 2
    return pair[:half].reshape(shape), pair[half:].reshape(shape)


def gather(block, axis, dim):
    return lax.all_gather(block, axis, axis=dim, tiled=True)


def scatter(block, axis, dim):
    return lax.psum_scatter(block, axis, scatter_dimension=dim, tiled=True)


CORE, X, Y = 1, 2, 4


def over(value, bit):
    return lax.ppermute(value, "seq", [(i, i ^ bit) for i in range(8)])


def place_kernel(plan, count, me_ref, *refs):
    pieces, whole, held, arrive_sem, leave_sem = refs[:count], refs[count], refs[count + 1 : -2], refs[-2], refs[-1]
    arrive, leave = [], []
    for n, (i, lanes, bits, there) in enumerate(plan):
        rows = pieces[i].shape[0]
        spot = pl.ds(pl.multiple_of((me_ref[0] ^ bits) * rows, 16), rows)
        arrive.append(pltpu.make_async_copy(pieces[i].at[:, lanes], held[n], arrive_sem.at[n]))
        leave.append(pltpu.make_async_copy(held[n], whole.at[spot, there], leave_sem.at[n]))
    for copy in arrive:
        copy.start()
    for come, go in zip(arrive, leave):
        come.wait()
        go.start()
    for copy in leave:
        copy.wait()


def place(pieces, spans, start, width, name):
    plan = []
    for i, (bits, low) in enumerate(spans):
        first, last = max(low, start), min(low + pieces[i].shape[1], start + width)
        if first < last:
            plan.append((i, pl.ds(first - low, last - first), bits, pl.ds(first - start, last - first)))
    used = sorted({entry[0] for entry in plan})
    plan = [(used.index(i), *entry) for i, *entry in plan]
    pieces = [pieces[i] for i in used]
    rows, count, dtype = pieces[0].shape[0], len(pieces), pieces[0].dtype
    anywhere = pl.BlockSpec(memory_space=pl.ANY)
    return pl.pallas_call(
        functools.partial(place_kernel, plan, count),
        out_shape=jax.ShapeDtypeStruct((8 * rows, width), dtype),
        in_specs=[pl.BlockSpec(memory_space=pltpu.SMEM)] + [anywhere] * count,
        out_specs=anywhere,
        scratch_shapes=[pltpu.VMEM((rows, lanes.size), dtype) for _, lanes, _, _ in plan]
        + [pltpu.SemaphoreType.DMA((len(plan),)) for _ in range(2)],
        compiler_params=pltpu.CompilerParams(vmem_limit_bytes=VMEM_LIMIT),
        cost_estimate=pl.CostEstimate(flops=0, bytes_accessed=32 * rows * width, transcendentals=0),
        name=name,
    )(lax.axis_index("seq").astype(jnp.int32).reshape(1), *pieces)


def seq_links(block, half):
    if lax.axis_size("seq") != 8:
        return (block,)
    from_x, from_y = over(block, X), over(block, Y)
    return block, from_x, from_y, over(from_x[:, :half], Y), over(from_y[:, half:], X)


def seq_gather(blocks, widths, names):
    starts = [sum(widths[:i]) for i in range(len(widths))]
    if lax.axis_size("seq") != 8:
        whole = gather(blocks[0], "seq", 0)
        return [whole[:, start : start + width] for start, width in zip(starts, widths)]
    pieces = [*blocks, *[over(block, CORE) for block in blocks]]
    half = blocks[3].shape[1]
    spans = [
        (bits + core, low)
        for core in (0, CORE)
        for bits, low in ((0, 0), (X, 0), (Y, 0), (X + Y, 0), (X + Y, half))
    ]
    return [place(pieces, spans, *cut) for cut in zip(starts, widths, names)]


def plus(*terms):
    total = terms[0].astype(F32)
    for term in terms[1:]:
        total = total + term.astype(F32)
    return total


def halves_kernel(micros, core_ref, *refs):
    lefts, rights, send_ref, keep_ref = refs[:micros], refs[micros : 2 * micros], refs[-2], refs[-1]
    rows, width = send_ref.shape

    def into(out_ref):
        for start in range(0, width, 512):
            lanes = slice(start, min(start + 512, width))
            total = None
            for left, right in zip(lefts, rights):
                part = lax.dot_general(
                    left[...], right[:, lanes], (((0,), (0,)), ((), ())), preferred_element_type=F32
                )
                total = part if total is None else total + part
            out_ref[:, lanes] = total.astype(BF)

    pl.when(pl.program_id(0) < 4)(lambda: into(send_ref))
    pl.when(pl.program_id(0) >= 4)(lambda: into(keep_ref))


def grad_halves(lefts, rights, name, after=()):
    if lax.axis_size("seq") != 8:
        return (dot(jnp.concatenate(lefts), jnp.concatenate(rights), ((0,), (0,))).astype(BF),)
    count, wide = lefts[0].shape
    rows, width, n = wide // 8, rights[0].shape[1], len(lefts)
    core = (lax.axis_index("seq") & CORE).astype(jnp.int32).reshape(1)
    return pl.pallas_call(
        functools.partial(halves_kernel, n),
        out_shape=[jax.ShapeDtypeStruct((wide // 2, width), BF)] * 2,
        grid_spec=pltpu.PrefetchScalarGridSpec(
            num_scalar_prefetch=1,
            grid=(8,),
            in_specs=[
                pl.BlockSpec((count, rows), lambda i, c: (0, 2 * (i % 4) + jnp.where(i < 4, 1 - c[0], c[0])))
            ] * n
            + [pl.BlockSpec((count, width), lambda i, c: (0, 0))] * n
            + [pl.BlockSpec(memory_space=pl.ANY)] * len(after),
            out_specs=[
                pl.BlockSpec((rows, width), lambda i, c: (jnp.minimum(i, 3), 0)),
                pl.BlockSpec((rows, width), lambda i, c: (jnp.maximum(i, 4) - 4, 0)),
            ],
        ),
        compiler_params=pltpu.CompilerParams(vmem_limit_bytes=VMEM_LIMIT),
        cost_estimate=pl.CostEstimate(
            flops=2 * n * count * wide * width,
            bytes_accessed=2 * n * count * (wide + width) + 2 * wide * width,
            transcendentals=0,
        ),
        name=name,
    )(core, *lefts, *rights, *after)


def grad_chip(halves, after=()):
    if len(halves) == 1:
        return halves[0]
    send, keep = halves
    four = plus(keep, over(send, CORE), nothing_of(after)).astype(BF)
    return four.reshape(4, keep.shape[0] // 4, keep.shape[1])


def owner(four, bits):
    return lax.dynamic_index_in_dim(four, (lax.axis_index("seq") // 2) ^ (bits // 2), 0, keepdims=False)


def grad_far(four, relay, after=()):
    if four.ndim == 2:
        return four
    return over(tied(owner(four, X + Y), *after), relay)


def grad_turn(four, far, relay, after=()):
    if four.ndim == 2:
        return (four,)
    nothing = nothing_of(after)
    to_x, to_y = owner(four, X).astype(F32) + nothing, owner(four, Y).astype(F32) + nothing
    if relay == Y:
        to_x = plus(to_x, far)
    else:
        to_y = plus(to_y, far)
    return to_x.astype(BF), to_y.astype(BF)


def grad_own(four, turn, after=()):
    if four.ndim == 2:
        return scatter(four, "seq", 0).astype(F32)
    return plus(owner(four, 0), over(turn[0], X), over(turn[1], Y), nothing_of(after))


def tp_sum(block):
    count = lax.axis_size("tp")
    return plus(block, *[
        lax.ppermute(block, "tp", [(i, (i + hop) % count) for i in range(count)])
        for hop in range(1, count)
    ])


def nothing_of(others):
    return sum([other[(0,) * other.ndim].astype(F32) * 0.0 for other in others], jnp.zeros((), F32))


def tied(value, *others):
    return value + nothing_of(others).astype(value.dtype) if others else value


def dot(a, b, dims):
    return lax.dot_general(a, b, (dims, ((), ())), preferred_element_type=F32)


def shards(tokens, lengths, pad_mask, gain_in, w_in, conv_taps, log_rate, pole_angle, residues,
           skip_gain, w_out, gain_mlp, w_gu, w_down, cotangent):
    micros, count, width = tokens.shape
    n_seq, n_tp = lax.axis_size("seq"), lax.axis_size("tp")
    me = lax.axis_index("seq")
    hidden = w_gu.shape[2]
    joint = jnp.concatenate([tokens.reshape(micros * count, width), w_out.T])
    joint = gather(joint, "tp", 1)
    x_full = joint[: micros * count].reshape(micros, count, -1)
    out_lanes = joint[micros * count :]
    rows_in = w_in.shape[0]
    first_links = seq_links(jnp.concatenate([w_in.reshape(rows_in, -1), w_gu.reshape(rows_in, -1)], axis=1), 3 * width)
    in_full, gu_full = seq_gather(first_links, (3 * width, 2 * hidden), ("place_in", "place_gu"))
    cot_full = [gather(cotangent[0], "tp", 1)]
    down_full = gather(tied(w_down.T, *first_links[-2:]), "seq", 0)
    out_links = seq_links(out_lanes, out_lanes.shape[1] // 2)
    (out_full,) = seq_gather(out_links, (n_tp * width,), ("place_out",))

    rate = jnp.exp(log_rate)
    lam_real, lam_imag = polar(1.0, rate, pole_angle)
    lam = packed(lam_real, lam_imag)
    powers = [(lam_real, lam_imag)] + [polar(n, rate, pole_angle) for n in (2.0, 4.0, 8.0)]
    pow_ahead = jnp.concatenate([packed(real, imag) for real, imag in powers])
    pow_back = jnp.concatenate([packed(real, -imag) for real, imag in powers])
    lam_all = packed(*polar(float(count), rate, pole_angle))
    res = packed(residues[0], residues[1])
    taps = conv_taps.reshape(9, width)
    skip = skip_gain.reshape(1, width)
    me_word = me.astype(jnp.int32).reshape(1)
    edges = jnp.arange(n_seq + 1) * count
    seq_shape = (count * SUB, LANE)
    st_shape = lam.shape
    work = 400 * lam.shape[0] * SUB * LANE * count

    position = me * count + jnp.arange(-2, count + 1)
    seg = jnp.stack([segment_number(position, lengths[m]) for m in range(micros)])
    valid1 = (seg[:, 2:] == seg[:, 1:-1]).astype(F32)
    valid2 = (seg[:, 2:] == seg[:, :-2]).astype(F32)
    inside = (jnp.arange(count + 1) < count) | (me < n_seq - 1)
    keeps = jnp.pad(valid1 * inside[None].astype(F32), ((0, 0), (0, SUB - 1)))
    group_flags = jnp.any(keeps.reshape(micros, -1, STEP) == 0, axis=2).astype(jnp.int32)
    columns = jnp.stack([valid1[:, :count], valid2[:, :count], pad_mask.astype(F32)], axis=2)
    columns = jnp.pad(columns, ((0, 0), (0, SUB), (0, SUB - 3)))

    x_wide = x_full.astype(F32)
    scale_in = norm_scale(x_wide)
    h_in = (x_wide * scale_in * gain_in).astype(BF)
    z_low = dot(h_in, in_full, ((2,), (0,))).astype(BF)
    rims = lax.ppermute(z_low[:, count - 2 :], "seq", [(i, i + 1) for i in range(n_seq - 1)])
    rims = jnp.pad(rims.astype(F32), ((0, 0), (SUB - 2, 0), (0, 0)))
    zs = ((count + SUB, 3 * width), F32)
    bases = [(z_low[m], rims[m], taps, columns[m], lam) for m in range(micros)]
    masks = [(keeps[m], group_flags[m]) for m in range(micros)]
    last = [segment_number(edges - 1, lengths[m]) for m in range(micros)]
    first = [segment_number(edges, lengths[m]) for m in range(micros)]
    spans = [(v[1:] == v[:-1]).astype(F32) for v in last]
    spans_back = [(v[1:] == v[:-1]).astype(F32) for v in first]
    injects, ends = zip(*[
        call(front_kernel, (*masks[m], *bases[m][:-1], pow_ahead), [(seq_shape, F32), (st_shape, F32)],
             [zs], 2, "mixer_front", 4 * work)
        for m in range(micros)
    ])
    ends = lax.all_gather(tied(jnp.stack(ends), *out_links[1:3]).astype(BF), "seq").astype(F32)

    kept = []
    outputs = []
    for m in range(micros):
        mixed, conv_out, marks = call(
            functools.partial(finish_kernel, m),
            (*masks[m], spans[m], me_word, *bases[m], lam_all, res, skip, injects[m], ends),
            [((count, width), BF), ((count, width), F32), ((count // SPAN, *st_shape), F32)],
            [zs, (seq_shape, F32), (st_shape, F32)], 4, "mixer_finish", 5 * work,
            (kept[0]["mixed"], down_full) if m else cot_full,
        )
        kept.append(dict(mixed=mixed, conv=conv_out, marks=marks))

    order = ()
    for m in range(micros):
        mixed_full = gather(kept[m]["mixed"], "tp", 1)
        if m + 1 < micros:
            cot_full.append(gather(tied(cotangent[m + 1], mixed_full), "tp", 1))
        x_mid = tied(x_full[m].astype(F32), *order) + dot(mixed_full, out_full, ((1,), (1,)))
        scale_mid = norm_scale(x_mid)
        h_mlp = (x_mid * scale_mid * gain_mlp[None]).astype(BF)
        gate_up = dot(h_mlp, gu_full, ((1,), (0,)))
        gate, up = gate_up[:, :hidden], gate_up[:, hidden:]
        sig = jax.nn.sigmoid(gate)
        act = (gate * sig * up).astype(BF)
        down_own = scatter(dot(act, down_full, ((1,), (1,))).astype(BF), "tp", 1)
        mid_own = lax.dynamic_slice_in_dim(x_mid, lax.axis_index("tp") * width, width, 1)
        outputs.append((mid_own, down_own))

        cot = cot_full[m]
        d_act = dot(cot, down_full, ((1,), (0,)))
        d_gu = jnp.concatenate(
            [d_act * up * sig * (1.0 + gate * (1.0 - sig)), d_act * gate * sig], axis=1
        ).astype(BF)
        d_h = dot(d_gu, gu_full, ((1,), (1,)))
        d_norm, d_gain_mlp = norm_back(x_mid, scale_mid, gain_mlp, d_h)
        d_mid = d_norm + cot.astype(F32) * (1.0 / n_tp)
        d_low = d_mid.astype(BF)
        d_mixed = dot(d_low, out_full, ((1,), (0,))).astype(BF)
        order = (d_mixed,)
        d_mixed = scatter(d_mixed, "tp", 1)
        kept[m].update(
            mixed=mixed_full, h_mlp=h_mlp, act=act, d_gu=d_gu, d_mid=d_mid, d_low=d_low,
            d_mixed=d_mixed, d_gain_mlp=d_gain_mlp,
        )

    def each(name):
        return [c[name] for c in kept]

    out_halves = grad_halves(each("d_low"), each("mixed"), "grad_out", order)
    down_halves = grad_halves(cot_full, each("act"), "grad_down", out_halves)
    down_chip, out_chip = grad_chip(down_halves), grad_chip(out_halves)
    down_far, out_far = grad_far(down_chip, Y), grad_far(out_chip, X)
    adjoints, ends = zip(*[
        call(adjoint_kernel, (*masks[m], *bases[m][:-1], pow_back, kept[m]["d_mixed"]),
             [(seq_shape, F32), (st_shape, F32)], [zs], 2, "mixer_adjoint", 4 * work,
             (down_chip, out_chip) if m else (*down_halves, *out_halves))
        for m in range(micros)
    ])
    ends = lax.all_gather(tied(jnp.stack(ends), down_far).astype(BF), "seq").astype(F32)
    gu_halves = grad_halves(each("h_mlp"), each("d_gu"), "grad_gu", (ends,))
    gu_chip = grad_chip(gu_halves)
    gu_far = grad_far(gu_chip, X)
    down_turn = grad_turn(down_chip, down_far, Y, (ends,))
    g_out = grad_own(out_chip, grad_turn(out_chip, out_far, X, (ends,)))
    g_out = scatter(tied(g_out, *gu_halves).astype(BF), "tp", 1)

    token_grads = []
    partial_grads = []
    smalls = []
    for m in range(micros):
        c = kept[m]
        d_z, rim_back, tail, d_taps, d_skip, d_res, d_lam = call(
            functools.partial(back_kernel, m),
            (*masks[m], spans_back[m], me_word, *bases[m], lam_all, res, skip, injects[m],
             adjoints[m], c["d_mixed"], c["conv"], c["marks"], ends),
            [((count, 3 * width), BF), ((SUB, 3 * width), F32), ((ROWS, 3 * width), F32),
             ((9 * SUB, width), F32), ((SUB, width), F32), (st_shape, F32), (st_shape, F32)],
            [zs, ((count + SUB, 3 * width), F32), (seq_shape, F32),
             (((SPAN + 1) * st_shape[0] * SUB, LANE), F32), (st_shape, F32)],
            4, "mixer_back", 12 * work, (*partial_grads, *gu_turn) if m else (*gu_halves, gu_chip),
        )
        rim_back = lax.ppermute(rim_back[:2], "seq", [(i + 1, i) for i in range(n_seq - 1)])
        if m == 0:
            gu_turn = grad_turn(gu_chip, gu_far, X, (rim_back,))
            g_gu = grad_own(gu_chip, gu_turn)
        tail = tied(tail, g_gu if m else gu_far)
        tail = (tail + jnp.concatenate([jnp.zeros((ROWS - 2, 3 * width), F32), rim_back])).astype(BF)
        d_z = lax.dynamic_update_slice(d_z, tail, (count - ROWS, 0))
        c["d_z"] = d_z
        gain = gain_in
        if m == micros - 1:
            in_halves = grad_halves([h_in[i] for i in range(micros)], each("d_z"), "grad_in")
            gain = tied(gain_in, in_halves[0])
        d_h_in = dot(d_z, in_full, ((1,), (1,)))
        d_norm, d_gain_in = norm_back(x_full[m].astype(F32), scale_in[m], gain, d_h_in)
        gains = [d_gain_in, c["d_gain_mlp"]] if m == 0 else [gains[0] + d_gain_in, gains[1] + c["d_gain_mlp"]]
        if m == micros - 1:
            gains = tp_sum(jnp.concatenate(gains).reshape(-1, width).astype(BF))
            d_norm = tied(d_norm, gains)
        partial_grads.append((c["d_mid"] + d_norm).astype(BF))
        token_grads.append(scatter(partial_grads[m], "tp", 1))
        smalls.append((d_taps, d_lam, d_res, d_skip))

    in_chip = grad_chip(in_halves)
    d_taps, d_lam, d_res, d_skip = (sum(parts) for parts in zip(*smalls))
    g_real, g_imag = unpacked(d_lam, log_rate.shape)
    s_real, s_imag = unpacked(d_res, log_rate.shape)
    h_real = residues[0] * g_real + residues[1] * g_imag
    h_imag = residues[0] * g_imag - residues[1] * g_real
    small = jnp.concatenate([
        jnp.sum(d_taps.reshape(9, SUB, width), axis=1),
        -rate * (lam_real * h_real + lam_imag * h_imag),
        lam_real * h_imag - lam_imag * h_real,
        s_real, -s_imag,
        jnp.sum(d_skip, axis=0, keepdims=True),
        gains,
    ])
    small = jnp.sum(lax.all_gather(small.astype(BF), "seq").astype(F32), axis=0)
    in_far = grad_far(in_chip, Y, (small,))
    g_in = grad_own(in_chip, grad_turn(in_chip, in_far, Y, (small,)))
    g_down = grad_own(down_chip, down_turn, (in_far,))
    gains = small[-gains.shape[0] :]
    n_gain = gains.shape[0]
    n_pole = log_rate.shape[0]
    cuts = [9, 9 + n_pole, 9 + 2 * n_pole, 9 + 3 * n_pole, 9 + 4 * n_pole]
    return (
        jnp.stack([(mid + tied(down.astype(F32), in_far)).astype(BF) for mid, down in outputs]),
        jnp.stack(token_grads),
        gains[: n_gain // 2].reshape(-1),
        g_in.reshape(w_in.shape),
        small[: cuts[0]].reshape(conv_taps.shape),
        small[cuts[0] : cuts[1]],
        small[cuts[1] : cuts[2]],
        small[cuts[2] : cuts[4]].reshape(residues.shape),
        small[cuts[4]],
        tied(g_out.astype(F32), in_far).T,
        gains[n_gain // 2 :].reshape(-1),
        tied(g_gu, in_far).reshape(w_gu.shape),
        g_down.T,
    )


def solution(mesh):
    wide, deep, flat = P(None, "seq", "tp"), P("seq", None, "tp"), P("tp", "seq")
    poles, taps = P(None, "tp"), P(None, None, "tp")
    return jax.shard_map(
        shards,
        mesh=mesh,
        in_specs=(wide, P(), P(None, "seq"), P(), deep, taps, poles, poles, taps, P("tp"), flat,
                  P(), deep, flat, wide),
        out_specs=(wide, wide, P(), deep, taps, poles, poles, taps, P("tp"), flat, P(), deep, flat),
        check_vma=False,
    )
```

```python
import functools

import jax
import jax.numpy as jnp
from jax import lax
from jax.experimental import pallas as pl
from jax.experimental.pallas import tpu as pltpu
from jax.sharding import PartitionSpec as P

EPS = 1e-06
SPAN = 64
STEP = 8
ROWS = 64
SUB, LANE = 8, 128
BF, F32 = jnp.bfloat16, jnp.float32
VMEM_LIMIT = 56 * 1024 * 1024


def keep_rows(z_ref, rim_ref, zs_ref, streams=(0, 3)):
    width = z_ref.shape[1] // 3
    lanes = slice(streams[0] * width, streams[1] * width)
    zs_ref[0:SUB, lanes] = rim_ref[:, lanes]

    def body(i, _):
        rows = pl.ds(pl.multiple_of(i * ROWS, ROWS), ROWS)
        zs_ref[pl.ds(pl.multiple_of(i * ROWS + SUB, SUB), ROWS), lanes] = z_ref[rows, lanes].astype(F32)
        return 0

    lax.fori_loop(0, z_ref.shape[0] // ROWS, body, 0)


def window(zs_ref, i, stream, width):
    rows = pl.ds(pl.multiple_of(i * ROWS, ROWS), ROWS + SUB)
    wide = zs_ref[rows, stream * width : (stream + 1) * width]
    return wide[8 : 8 + ROWS], wide[7 : 7 + ROWS], wide[6 : 6 + ROWS]


def filtered(zs_ref, taps_ref, cols, i, stream, width):
    z0, z1, z2 = window(zs_ref, i, stream, width)
    t0, t1, t2 = (taps_ref[lag * 3 + stream : lag * 3 + stream + 1, :] for lag in range(3))
    return t0 * z0 + (t1 * z1) * cols[:, 0:1] + (t2 * z2) * cols[:, 1:2]


def spread(ref, i, value):
    parts = value.shape[1] // LANE
    for c in range(parts):
        piece = value[:, c * LANE : (c + 1) * LANE]
        for half in range(SUB // parts):
            ref[pl.ds(i * (ROWS * SUB) + half * parts + c, ROWS, stride=SUB), :] = piece


def collect(ref, i, width):
    parts = width // LANE
    pieces = []
    for c in range(parts):
        piece = ref[pl.ds(i * (ROWS * SUB) + c, ROWS, stride=SUB), :]
        for half in range(1, SUB // parts):
            piece = piece + ref[pl.ds(i * (ROWS * SUB) + half * parts + c, ROWS, stride=SUB), :]
        pieces.append(piece)
    return jnp.concatenate(pieces, axis=1)


def chunk_cols(cols_ref, i):
    return cols_ref[pl.ds(pl.multiple_of(i * ROWS, ROWS), ROWS), :]


def at(group, j):
    return pl.ds(pl.multiple_of((group * STEP + j) * SUB, SUB), SUB)


def by_flag(flag, step):
    @pl.when(flag == 0)
    def _():
        step(False)

    @pl.when(flag != 0)
    def _():
        step(True)


def eight_steps(values, powers, real, imag):
    def join(earlier, later, n):
        pr, pi = powers[n]
        return pr * earlier[0] - pi * earlier[1] + later[0], pr * earlier[1] + pi * earlier[0] + later[1]

    pr, pi = powers[0]
    pairs = [(pr * values[j] + values[j + 1], pi * values[j]) for j in range(0, STEP, 2)]
    fours = [join(pairs[j], pairs[j + 1], 1) for j in (0, 2)]
    return join((real, imag), join(*fours, 2), 3)


def end_scan(values, keep_of, masked, pow_ref, end_ref):
    poles = end_ref.shape[0] // 2
    for k in range(poles):
        sr, si = end_ref[k], end_ref[poles + k]
        if masked:
            lr, li = pow_ref[k], pow_ref[poles + k]
            for j in range(STEP):
                keep = keep_of(j)
                sr, si = sr * keep, si * keep
                sr, si = lr * sr - li * si + values[j], lr * si + li * sr
        else:
            powers = [(pow_ref[2 * poles * n + k], pow_ref[2 * poles * n + poles + k]) for n in range(4)]
            sr, si = eight_steps(values, powers, sr, si)
        end_ref[k], end_ref[poles + k] = sr, si


def front_kernel(keep_ref, flag_ref, z_ref, rim_ref, taps_ref, cols_ref, pow_ref,
                 u_ref, end_ref, zs_ref):
    count, width = z_ref.shape[0], z_ref.shape[1] // 3
    keep_rows(z_ref, rim_ref, zs_ref, (1, 3))

    def natural(i, _):
        cols = chunk_cols(cols_ref, i)
        key = filtered(zs_ref, taps_ref, cols, i, 1, width)
        value = filtered(zs_ref, taps_ref, cols, i, 2, width)
        spread(u_ref, i, key * value * cols[:, 2:3])
        return 0

    lax.fori_loop(0, count // ROWS, natural, 0)
    end_ref[...] = jnp.zeros_like(end_ref)

    def scan(group, _):
        def step(masked):
            us = [u_ref[at(group, j), :] for j in range(STEP)]
            end_scan(us, lambda j: keep_ref[group * STEP + j], masked, pow_ref, end_ref)

        by_flag(flag_ref[group], step)
        return 0

    lax.fori_loop(0, count // STEP, scan, 0)


def joined(all_ref, micro, full_ref, carry_ref, spans_ref, me, count, conj):
    poles = full_ref.shape[0] // 2
    carry_ref[...] = jnp.zeros_like(carry_ref)

    def hop(order, _):
        j = count - 1 - order if conj else order
        span = spans_ref[j]
        for k in range(poles):
            lr, li = full_ref[k] * span, full_ref[poles + k] * (-span if conj else span)
            sr, si = carry_ref[k], carry_ref[poles + k]
            carry_ref[k] = lr * sr - li * si + all_ref[j, micro, k]
            carry_ref[poles + k] = lr * si + li * sr + all_ref[j, micro, poles + k]
        return 0

    lax.fori_loop(0, count - 1 - me if conj else me, hop, 0)


def finish_kernel(micro, keep_ref, flag_ref, spans_ref, me_ref, z_ref, rim_ref, taps_ref, cols_ref,
                  lam_ref, full_ref, res_ref, skip_ref, u_ref, ends_ref,
                  mixed_ref, conv_ref, marks_ref, zs_ref, y_ref, st_ref):
    count, width = z_ref.shape[0], z_ref.shape[1] // 3
    poles = lam_ref.shape[0] // 2
    keep_rows(z_ref, rim_ref, zs_ref)
    joined(ends_ref, micro, full_ref, st_ref, spans_ref, me_ref[0], ends_ref.shape[0], False)

    def scan(group, _):
        @pl.when(group % (SPAN // STEP) == 0)
        def _():
            marks_ref[group // (SPAN // STEP)] = st_ref[...]

        def step(masked):
            us = [u_ref[at(group, j), :] for j in range(STEP)]
            ys = [None] * STEP
            for k in range(poles):
                lr, li = lam_ref[k], lam_ref[poles + k]
                rr, ri = res_ref[k], res_ref[poles + k]
                sr, si = st_ref[k], st_ref[poles + k]
                for j in range(STEP):
                    if masked:
                        keep = keep_ref[group * STEP + j]
                        sr, si = sr * keep, si * keep
                    sr, si = lr * sr - li * si + us[j], lr * si + li * sr
                    part = rr * sr - ri * si
                    ys[j] = part if ys[j] is None else ys[j] + part
                st_ref[k], st_ref[poles + k] = sr, si
            for j in range(STEP):
                y_ref[at(group, j), :] = ys[j]

        by_flag(flag_ref[group], step)
        return 0

    lax.fori_loop(0, count // STEP, scan, 0)

    def natural(i, _):
        rows = pl.ds(pl.multiple_of(i * ROWS, ROWS), ROWS)
        cols = chunk_cols(cols_ref, i)
        query = filtered(zs_ref, taps_ref, cols, i, 0, width)
        key = filtered(zs_ref, taps_ref, cols, i, 1, width)
        value = filtered(zs_ref, taps_ref, cols, i, 2, width)
        conv = collect(y_ref, i, width) + skip_ref[...] * (key * value * cols[:, 2:3])
        conv_ref[rows, :] = conv
        mixed_ref[rows, :] = (query * conv).astype(BF)
        return 0

    lax.fori_loop(0, count // ROWS, natural, 0)


def adjoint_kernel(keep_ref, flag_ref, z_ref, rim_ref, taps_ref, cols_ref, pow_ref, dmix_ref,
                   e_ref, end_ref, zs_ref):
    count, width = z_ref.shape[0], z_ref.shape[1] // 3
    keep_rows(z_ref, rim_ref, zs_ref, (0, 1))

    def natural(i, _):
        rows = pl.ds(pl.multiple_of(i * ROWS, ROWS), ROWS)
        query = filtered(zs_ref, taps_ref, chunk_cols(cols_ref, i), i, 0, width)
        spread(e_ref, i, dmix_ref[rows, :].astype(F32) * query)
        return 0

    lax.fori_loop(0, count // ROWS, natural, 0)
    end_ref[...] = jnp.zeros_like(end_ref)

    def scan(order, _):
        group = count // STEP - 1 - order

        def step(masked):
            es = [e_ref[at(group, STEP - 1 - j), :] for j in range(STEP)]
            end_scan(es, lambda j: keep_ref[group * STEP + STEP - j], masked, pow_ref, end_ref)

        by_flag(flag_ref[group] + flag_ref[group + 1], step)
        return 0

    lax.fori_loop(0, count // STEP, scan, 0)


def back_kernel(micro, keep_ref, flag_ref, spans_ref, me_ref, z_ref, rim_ref, taps_ref, cols_ref,
                lam_ref, full_ref, res_ref, skip_ref, u_ref, e_ref, dmix_ref, conv_ref,
                marks_ref, ends_ref,
                dz_ref, rimback_ref, tail_ref, dtaps_ref, dskip_ref, dres_ref, g_ref,
                zs_ref, dc_ref, di_ref, ss_ref, bt_ref):
    count, width = z_ref.shape[0], z_ref.shape[1] // 3
    poles = lam_ref.shape[0] // 2
    state_rows = 2 * poles * SUB
    keep_rows(z_ref, rim_ref, zs_ref)
    joined(ends_ref, micro, full_ref, bt_ref, spans_ref, me_ref[0], ends_ref.shape[0], True)
    bt_ref[...] = bt_ref[...] * keep_ref[count]
    for ref in (dtaps_ref, dskip_ref, dres_ref, g_ref):
        ref[...] = jnp.zeros_like(ref)

    def held(slot, k):
        return pl.ds(pl.multiple_of(slot * state_rows + k * SUB, SUB), SUB)

    def block(order, _):
        number = count // SPAN - 1 - order
        for k in range(2 * poles):
            ss_ref[held(0, k), :] = marks_ref[number, k]

        def forward(inner, _):
            group = number * (SPAN // STEP) + inner

            def step(masked):
                us = [u_ref[at(group, j), :] for j in range(STEP)]
                es = [e_ref[at(group, j), :] for j in range(STEP)]
                for k in range(poles):
                    lr, li = lam_ref[k], lam_ref[poles + k]
                    sr = ss_ref[held(inner * STEP, k), :]
                    si = ss_ref[held(inner * STEP, poles + k), :]
                    ar = ai = None
                    for j in range(STEP):
                        if masked:
                            keep = keep_ref[group * STEP + j]
                            sr, si = sr * keep, si * keep
                        sr, si = lr * sr - li * si + us[j], lr * si + li * sr
                        ss_ref[held(inner * STEP + j + 1, k), :] = sr
                        ss_ref[held(inner * STEP + j + 1, poles + k), :] = si
                        ar = es[j] * sr if ar is None else ar + es[j] * sr
                        ai = es[j] * si if ai is None else ai + es[j] * si
                    dres_ref[k] = dres_ref[k] + ar
                    dres_ref[poles + k] = dres_ref[poles + k] + ai

            by_flag(flag_ref[group], step)
            return 0

        lax.fori_loop(0, SPAN // STEP, forward, 0)

        def backward(outer, _):
            inner = SPAN // STEP - 1 - outer
            group = number * (SPAN // STEP) + inner

            def step(masked):
                es = [e_ref[at(group, j), :] for j in range(STEP)]
                ds = [None] * STEP
                for k in range(poles):
                    lr, li = lam_ref[k], lam_ref[poles + k]
                    rr, ri = res_ref[k], res_ref[poles + k]
                    tr, ti = bt_ref[k], bt_ref[poles + k]
                    gr, gi = g_ref[k], g_ref[poles + k]
                    for j in reversed(range(STEP)):
                        tr, ti = lr * tr + li * ti + es[j], lr * ti - li * tr
                        part = rr * tr + ri * ti
                        ds[j] = part if ds[j] is None else ds[j] + part
                        if masked:
                            keep = keep_ref[group * STEP + j]
                            tr, ti = tr * keep, ti * keep
                        sr = ss_ref[held(inner * STEP + j, k), :]
                        si = ss_ref[held(inner * STEP + j, poles + k), :]
                        gr = gr + (sr * tr + si * ti)
                        gi = gi + (sr * ti - si * tr)
                    bt_ref[k], bt_ref[poles + k] = tr, ti
                    g_ref[k], g_ref[poles + k] = gr, gi
                for j in range(STEP):
                    di_ref[at(group, j), :] = ds[j]

            by_flag(flag_ref[group], step)
            return 0

        lax.fori_loop(0, SPAN // STEP, backward, 0)
        return 0

    lax.fori_loop(0, count // SPAN, block, 0)

    def eighths(value):
        total = value[0:SUB]
        for start in range(SUB, ROWS, SUB):
            total = total + value[start : start + SUB]
        return total

    def natural(i, _):
        rows = pl.ds(pl.multiple_of(i * ROWS, ROWS), ROWS)
        cols = chunk_cols(cols_ref, i)
        query = filtered(zs_ref, taps_ref, cols, i, 0, width)
        key = filtered(zs_ref, taps_ref, cols, i, 1, width)
        value = filtered(zs_ref, taps_ref, cols, i, 2, width)
        mask = cols[:, 2:3]
        d_mixed = dmix_ref[rows, :].astype(F32)
        e = d_mixed * query
        dskip_ref[...] = dskip_ref[...] + eighths(e * (key * value * mask))
        d_inject = (collect(di_ref, i, width) + skip_ref[...] * e) * mask
        for stream, grad in enumerate((d_mixed * conv_ref[rows, :], d_inject * value, d_inject * key)):
            lanes = slice(stream * width, (stream + 1) * width)
            dc_ref[rows, lanes] = grad
            shifted = window(zs_ref, i, stream, width)
            for lag in range(3):
                product = grad * shifted[lag]
                if lag:
                    product = product * cols[:, lag - 1 : lag]
                slot = slice((lag * 3 + stream) * SUB, (lag * 3 + stream + 1) * SUB)
                dtaps_ref[slot, :] = dtaps_ref[slot, :] + eighths(product)
        return 0

    lax.fori_loop(0, count // ROWS, natural, 0)
    dc_ref[count : count + SUB, :] = jnp.zeros((SUB, 3 * width), F32)

    def spread_back(i, _):
        rows = pl.ds(pl.multiple_of(i * ROWS, ROWS), ROWS)
        beyond = pl.ds(pl.multiple_of(i * ROWS, ROWS), ROWS + SUB)
        cols = cols_ref[beyond, :]
        v1, v2 = cols[1 : 1 + ROWS, 0:1], cols[2 : 2 + ROWS, 1:2]
        for stream in range(3):
            lanes = slice(stream * width, (stream + 1) * width)
            wide = dc_ref[beyond, lanes]
            t0, t1, t2 = (taps_ref[lag * 3 + stream : lag * 3 + stream + 1, :] for lag in range(3))
            total = t0 * wide[0:ROWS] + (t1 * wide[1 : 1 + ROWS]) * v1 + (t2 * wide[2 : 2 + ROWS]) * v2
            dz_ref[rows, lanes] = total.astype(BF)

            @pl.when(i == count // ROWS - 1)
            def _():
                tail_ref[:, lanes] = total

        return 0

    lax.fori_loop(0, count // ROWS, spread_back, 0)
    first = cols_ref[0:SUB, :]
    for stream in range(3):
        lanes = slice(stream * width, (stream + 1) * width)
        dc = dc_ref[0:SUB, lanes]
        t1, t2 = (taps_ref[lag * 3 + stream : lag * 3 + stream + 1, :] for lag in (1, 2))
        one, two = t1 * (dc * first[:, 0:1]), t2 * (dc * first[:, 1:2])
        rimback_ref[...] = rimback_ref[...] if stream else jnp.zeros_like(rimback_ref)
        rimback_ref[0:1, lanes] = two[0:1]
        rimback_ref[1:2, lanes] = one[0:1] + two[1:2]


def call(kernel, ins, outs, scratch, smem, name, flops, after=()):
    count = len(ins)

    def without(*refs):
        kernel(*refs[:count], *refs[count + len(after) :])

    local = pl.BlockSpec(memory_space=pltpu.VMEM)
    scalar = pl.BlockSpec(memory_space=pltpu.SMEM)
    moved = sum(a.size * a.dtype.itemsize for a in ins) + sum(
        functools.reduce(lambda x, y: x * y, s) * jnp.dtype(d).itemsize for s, d in outs
    )
    return pl.pallas_call(
        without,
        out_shape=[jax.ShapeDtypeStruct(s, d) for s, d in outs],
        in_specs=[scalar] * smem + [local] * (count - smem)
        + [pl.BlockSpec(memory_space=pl.ANY)] * len(after),
        out_specs=[local] * len(outs),
        scratch_shapes=[pltpu.VMEM(s, d) for s, d in scratch],
        compiler_params=pltpu.CompilerParams(vmem_limit_bytes=VMEM_LIMIT),
        cost_estimate=pl.CostEstimate(flops=flops, bytes_accessed=moved, transcendentals=0),
        name=name,
    )(*ins, *after)


def segment_number(position, doc_lengths):
    starts_at = jnp.cumsum(doc_lengths) - doc_lengths
    hits = (starts_at[None, :] <= position[:, None]).astype(jnp.int32)
    return jnp.sum(hits, axis=1)


def norm_scale(values):
    return lax.rsqrt(jnp.mean(values * values, axis=-1, keepdims=True) + EPS)


def norm_back(values, scale, gain, grad):
    weighted = gain[None] * grad
    d_values = scale * weighted - values * scale**3 * jnp.mean(
        weighted * values, axis=-1, keepdims=True
    )
    return d_values, jnp.sum(grad * values * scale, axis=0)


def polar(exponent, decay_rate, pole_angle):
    magnitude = jnp.exp(-exponent * decay_rate)
    phase = exponent * pole_angle
    return magnitude * jnp.cos(phase), magnitude * jnp.sin(phase)


def packed(real, imag):
    rows = real.size // (SUB * LANE)
    return jnp.concatenate([real.reshape(rows, SUB, LANE), imag.reshape(rows, SUB, LANE)])


def unpacked(pair, shape):
    half = pair.shape[0] // 2
    return pair[:half].reshape(shape), pair[half:].reshape(shape)


def gather(block, axis, dim):
    return lax.all_gather(block, axis, axis=dim, tiled=True)


def scatter(block, axis, dim):
    return lax.psum_scatter(block, axis, scatter_dimension=dim, tiled=True)


CORE, X, Y = 1, 2, 4


def over(value, bit):
    return lax.ppermute(value, "seq", [(i, i ^ bit) for i in range(8)])


def place_kernel(plan, count, me_ref, *refs):
    pieces, whole, held, arrive_sem, leave_sem = refs[:count], refs[count], refs[count + 1 : -2], refs[-2], refs[-1]
    arrive, leave = [], []
    for n, (i, lanes, bits, there) in enumerate(plan):
        rows = pieces[i].shape[0]
        spot = pl.ds(pl.multiple_of((me_ref[0] ^ bits) * rows, 16), rows)
        arrive.append(pltpu.make_async_copy(pieces[i].at[:, lanes], held[n], arrive_sem.at[n]))
        leave.append(pltpu.make_async_copy(held[n], whole.at[spot, there], leave_sem.at[n]))
    for copy in arrive:
        copy.start()
    for come, go in zip(arrive, leave):
        come.wait()
        go.start()
    for copy in leave:
        copy.wait()


def place(pieces, spans, start, width, name):
    plan = []
    for i, (bits, low) in enumerate(spans):
        first, last = max(low, start), min(low + pieces[i].shape[1], start + width)
        if first < last:
            plan.append((i, pl.ds(first - low, last - first), bits, pl.ds(first - start, last - first)))
    used = sorted({entry[0] for entry in plan})
    plan = [(used.index(i), *entry) for i, *entry in plan]
    pieces = [pieces[i] for i in used]
    rows, count, dtype = pieces[0].shape[0], len(pieces), pieces[0].dtype
    anywhere = pl.BlockSpec(memory_space=pl.ANY)
    return pl.pallas_call(
        functools.partial(place_kernel, plan, count),
        out_shape=jax.ShapeDtypeStruct((8 * rows, width), dtype),
        in_specs=[pl.BlockSpec(memory_space=pltpu.SMEM)] + [anywhere] * count,
        out_specs=anywhere,
        scratch_shapes=[pltpu.VMEM((rows, lanes.size), dtype) for _, lanes, _, _ in plan]
        + [pltpu.SemaphoreType.DMA((len(plan),)) for _ in range(2)],
        compiler_params=pltpu.CompilerParams(vmem_limit_bytes=VMEM_LIMIT),
        cost_estimate=pl.CostEstimate(flops=0, bytes_accessed=32 * rows * width, transcendentals=0),
        name=name,
    )(lax.axis_index("seq").astype(jnp.int32).reshape(1), *pieces)


def seq_links(block, half):
    if lax.axis_size("seq") != 8:
        return (block,)
    from_x, from_y = over(block, X), over(block, Y)
    return block, from_x, from_y, over(from_x[:, :half], Y), over(from_y[:, half:], X)


def seq_gather(blocks, widths, names):
    starts = [sum(widths[:i]) for i in range(len(widths))]
    if lax.axis_size("seq") != 8:
        whole = gather(blocks[0], "seq", 0)
        return [whole[:, start : start + width] for start, width in zip(starts, widths)]
    pieces = [*blocks, *[over(block, CORE) for block in blocks]]
    half = blocks[3].shape[1]
    spans = [
        (bits + core, low)
        for core in (0, CORE)
        for bits, low in ((0, 0), (X, 0), (Y, 0), (X + Y, 0), (X + Y, half))
    ]
    return [place(pieces, spans, *cut) for cut in zip(starts, widths, names)]


def plus(*terms):
    total = terms[0].astype(F32)
    for term in terms[1:]:
        total = total + term.astype(F32)
    return total


def halves_kernel(micros, core_ref, *refs):
    lefts, rights, send_ref, keep_ref = refs[:micros], refs[micros : 2 * micros], refs[-2], refs[-1]
    rows, width = send_ref.shape

    def into(out_ref):
        for start in range(0, width, 512):
            lanes = slice(start, min(start + 512, width))
            total = None
            for left, right in zip(lefts, rights):
                part = lax.dot_general(
                    left[...], right[:, lanes], (((0,), (0,)), ((), ())), preferred_element_type=F32
                )
                total = part if total is None else total + part
            out_ref[:, lanes] = total.astype(BF)

    pl.when(pl.program_id(0) < 4)(lambda: into(send_ref))
    pl.when(pl.program_id(0) >= 4)(lambda: into(keep_ref))


def grad_halves(lefts, rights, name, after=()):
    if lax.axis_size("seq") != 8:
        return (dot(jnp.concatenate(lefts), jnp.concatenate(rights), ((0,), (0,))).astype(BF),)
    count, wide = lefts[0].shape
    rows, width, n = wide // 8, rights[0].shape[1], len(lefts)
    core = (lax.axis_index("seq") & CORE).astype(jnp.int32).reshape(1)
    return pl.pallas_call(
        functools.partial(halves_kernel, n),
        out_shape=[jax.ShapeDtypeStruct((wide // 2, width), BF)] * 2,
        grid_spec=pltpu.PrefetchScalarGridSpec(
            num_scalar_prefetch=1,
            grid=(8,),
            in_specs=[
                pl.BlockSpec((count, rows), lambda i, c: (0, 2 * (i % 4) + jnp.where(i < 4, 1 - c[0], c[0])))
            ] * n
            + [pl.BlockSpec((count, width), lambda i, c: (0, 0))] * n
            + [pl.BlockSpec(memory_space=pl.ANY)] * len(after),
            out_specs=[
                pl.BlockSpec((rows, width), lambda i, c: (jnp.minimum(i, 3), 0)),
                pl.BlockSpec((rows, width), lambda i, c: (jnp.maximum(i, 4) - 4, 0)),
            ],
        ),
        compiler_params=pltpu.CompilerParams(vmem_limit_bytes=VMEM_LIMIT),
        cost_estimate=pl.CostEstimate(
            flops=2 * n * count * wide * width,
            bytes_accessed=2 * n * count * (wide + width) + 2 * wide * width,
            transcendentals=0,
        ),
        name=name,
    )(core, *lefts, *rights, *after)


def grad_chip(halves, after=()):
    if len(halves) == 1:
        return halves[0]
    send, keep = halves
    four = plus(keep, over(send, CORE), nothing_of(after)).astype(BF)
    return four.reshape(4, keep.shape[0] // 4, keep.shape[1])


def owner(four, bits):
    return lax.dynamic_index_in_dim(four, (lax.axis_index("seq") // 2) ^ (bits // 2), 0, keepdims=False)


def grad_far(four, relay, after=()):
    if four.ndim == 2:
        return four
    return over(tied(owner(four, X + Y), *after), relay)


def grad_turn(four, far, relay, after=()):
    if four.ndim == 2:
        return (four,)
    nothing = nothing_of(after)
    to_x, to_y = owner(four, X).astype(F32) + nothing, owner(four, Y).astype(F32) + nothing
    if relay == Y:
        to_x = plus(to_x, far)
    else:
        to_y = plus(to_y, far)
    return to_x.astype(BF), to_y.astype(BF)


def grad_own(four, turn, after=()):
    if four.ndim == 2:
        return scatter(four, "seq", 0).astype(F32)
    return plus(owner(four, 0), over(turn[0], X), over(turn[1], Y), nothing_of(after))


def tp_sum(block):
    count = lax.axis_size("tp")
    return plus(block, *[
        lax.ppermute(block, "tp", [(i, (i + hop) % count) for i in range(count)])
        for hop in range(1, count)
    ])


def nothing_of(others):
    return sum([other[(0,) * other.ndim].astype(F32) * 0.0 for other in others], jnp.zeros((), F32))


def tied(value, *others):
    return value + nothing_of(others).astype(value.dtype) if others else value


def dot(a, b, dims):
    return lax.dot_general(a, b, (dims, ((), ())), preferred_element_type=F32)


def shards(tokens, lengths, pad_mask, gain_in, w_in, conv_taps, log_rate, pole_angle, residues,
           skip_gain, w_out, gain_mlp, w_gu, w_down, cotangent):
    micros, count, width = tokens.shape
    n_seq, n_tp = lax.axis_size("seq"), lax.axis_size("tp")
    me = lax.axis_index("seq")
    hidden = w_gu.shape[2]
    joint = jnp.concatenate([tokens.reshape(micros * count, width), w_out.T])
    joint = gather(joint, "tp", 1)
    x_full = joint[: micros * count].reshape(micros, count, -1)
    out_lanes = joint[micros * count :]
    rows_in = w_in.shape[0]
    first_links = seq_links(jnp.concatenate([w_in.reshape(rows_in, -1), w_gu.reshape(rows_in, -1)], axis=1), 3 * width)
    in_full, gu_full = seq_gather(first_links, (3 * width, 2 * hidden), ("place_in", "place_gu"))
    cot_full = [gather(cotangent[0], "tp", 1)]
    down_full = gather(tied(w_down.T, *first_links[-2:]), "seq", 0)
    out_links = seq_links(out_lanes, out_lanes.shape[1] // 2)
    (out_full,) = seq_gather(out_links, (n_tp * width,), ("place_out",))

    rate = jnp.exp(log_rate)
    lam_real, lam_imag = polar(1.0, rate, pole_angle)
    lam = packed(lam_real, lam_imag)
    powers = [(lam_real, lam_imag)] + [polar(n, rate, pole_angle) for n in (2.0, 4.0, 8.0)]
    pow_ahead = jnp.concatenate([packed(real, imag) for real, imag in powers])
    pow_back = jnp.concatenate([packed(real, -imag) for real, imag in powers])
    lam_all = packed(*polar(float(count), rate, pole_angle))
    res = packed(residues[0], residues[1])
    taps = conv_taps.reshape(9, width)
    skip = skip_gain.reshape(1, width)
    me_word = me.astype(jnp.int32).reshape(1)
    edges = jnp.arange(n_seq + 1) * count
    seq_shape = (count * SUB, LANE)
    st_shape = lam.shape
    work = 400 * lam.shape[0] * SUB * LANE * count

    position = me * count + jnp.arange(-2, count + 1)
    seg = jnp.stack([segment_number(position, lengths[m]) for m in range(micros)])
    valid1 = (seg[:, 2:] == seg[:, 1:-1]).astype(F32)
    valid2 = (seg[:, 2:] == seg[:, :-2]).astype(F32)
    inside = (jnp.arange(count + 1) < count) | (me < n_seq - 1)
    keeps = jnp.pad(valid1 * inside[None].astype(F32), ((0, 0), (0, SUB - 1)))
    group_flags = jnp.any(keeps.reshape(micros, -1, STEP) == 0, axis=2).astype(jnp.int32)
    columns = jnp.stack([valid1[:, :count], valid2[:, :count], pad_mask.astype(F32)], axis=2)
    columns = jnp.pad(columns, ((0, 0), (0, SUB), (0, SUB - 3)))

    x_wide = x_full.astype(F32)
    scale_in = norm_scale(x_wide)
    h_in = (x_wide * scale_in * gain_in).astype(BF)
    z_low = dot(h_in, in_full, ((2,), (0,))).astype(BF)
    rims = lax.ppermute(z_low[:, count - 2 :], "seq", [(i, i + 1) for i in range(n_seq - 1)])
    rims = jnp.pad(rims.astype(F32), ((0, 0), (SUB - 2, 0), (0, 0)))
    zs = ((count + SUB, 3 * width), F32)
    bases = [(z_low[m], rims[m], taps, columns[m], lam) for m in range(micros)]
    masks = [(keeps[m], group_flags[m]) for m in range(micros)]
    last = [segment_number(edges - 1, lengths[m]) for m in range(micros)]
    first = [segment_number(edges, lengths[m]) for m in range(micros)]
    spans = [(v[1:] == v[:-1]).astype(F32) for v in last]
    spans_back = [(v[1:] == v[:-1]).astype(F32) for v in first]
    injects, ends = zip(*[
        call(front_kernel, (*masks[m], *bases[m][:-1], pow_ahead), [(seq_shape, F32), (st_shape, F32)],
             [zs], 2, "mixer_front", 4 * work)
        for m in range(micros)
    ])
    ends = lax.all_gather(tied(jnp.stack(ends), *out_links[1:3]).astype(BF), "seq").astype(F32)

    kept = []
    outputs = []
    for m in range(micros):
        mixed, conv_out, marks = call(
            functools.partial(finish_kernel, m),
            (*masks[m], spans[m], me_word, *bases[m], lam_all, res, skip, injects[m], ends),
            [((count, width), BF), ((count, width), F32), ((count // SPAN, *st_shape), F32)],
            [zs, (seq_shape, F32), (st_shape, F32)], 4, "mixer_finish", 5 * work,
            (kept[0]["mixed"], down_full) if m else cot_full,
        )
        kept.append(dict(mixed=mixed, conv=conv_out, marks=marks))

    order = ()
    for m in range(micros):
        mixed_full = gather(kept[m]["mixed"], "tp", 1)
        if m + 1 < micros:
            cot_full.append(gather(tied(cotangent[m + 1], mixed_full), "tp", 1))
        x_mid = tied(x_full[m].astype(F32), *order) + dot(mixed_full, out_full, ((1,), (1,)))
        scale_mid = norm_scale(x_mid)
        h_mlp = (x_mid * scale_mid * gain_mlp[None]).astype(BF)
        gate_up = dot(h_mlp, gu_full, ((1,), (0,)))
        gate, up = gate_up[:, :hidden], gate_up[:, hidden:]
        sig = jax.nn.sigmoid(gate)
        act = (gate * sig * up).astype(BF)
        down_own = scatter(dot(act, down_full, ((1,), (1,))).astype(BF), "tp", 1)
        mid_own = lax.dynamic_slice_in_dim(x_mid, lax.axis_index("tp") * width, width, 1)
        outputs.append((mid_own, down_own))

        cot = cot_full[m]
        d_act = dot(cot, down_full, ((1,), (0,)))
        d_gu = jnp.concatenate(
            [d_act * up * sig * (1.0 + gate * (1.0 - sig)), d_act * gate * sig], axis=1
        ).astype(BF)
        d_h = dot(d_gu, gu_full, ((1,), (1,)))
        d_norm, d_gain_mlp = norm_back(x_mid, scale_mid, gain_mlp, d_h)
        d_mid = d_norm + cot.astype(F32) * (1.0 / n_tp)
        d_low = d_mid.astype(BF)
        d_mixed = dot(d_low, out_full, ((1,), (0,))).astype(BF)
        order = (d_mixed,)
        d_mixed = scatter(d_mixed, "tp", 1)
        kept[m].update(
            mixed=mixed_full, h_mlp=h_mlp, act=act, d_gu=d_gu, d_mid=d_mid, d_low=d_low,
            d_mixed=d_mixed, d_gain_mlp=d_gain_mlp,
        )

    def each(name):
        return [c[name] for c in kept]

    out_halves = grad_halves(each("d_low"), each("mixed"), "grad_out", order)
    down_halves = grad_halves(cot_full, each("act"), "grad_down", out_halves)
    down_chip, out_chip = grad_chip(down_halves), grad_chip(out_halves)
    down_far, out_far = grad_far(down_chip, Y), grad_far(out_chip, X)
    adjoints, ends = zip(*[
        call(adjoint_kernel, (*masks[m], *bases[m][:-1], pow_back, kept[m]["d_mixed"]),
             [(seq_shape, F32), (st_shape, F32)], [zs], 2, "mixer_adjoint", 4 * work,
             (down_chip, out_chip) if m else (*down_halves, *out_halves))
        for m in range(micros)
    ])
    ends = lax.all_gather(tied(jnp.stack(ends), down_far).astype(BF), "seq").astype(F32)
    gu_halves = grad_halves(each("h_mlp"), each("d_gu"), "grad_gu", (ends,))
    gu_chip = grad_chip(gu_halves)
    gu_far = grad_far(gu_chip, X)
    down_turn = grad_turn(down_chip, down_far, Y, (ends,))
    g_out = grad_own(out_chip, grad_turn(out_chip, out_far, X, (ends,)))
    g_out = scatter(tied(g_out, *gu_halves).astype(BF), "tp", 1)

    token_grads = []
    partial_grads = []
    smalls = []
    for m in range(micros):
        c = kept[m]
        d_z, rim_back, tail, d_taps, d_skip, d_res, d_lam = call(
            functools.partial(back_kernel, m),
            (*masks[m], spans_back[m], me_word, *bases[m], lam_all, res, skip, injects[m],
             adjoints[m], c["d_mixed"], c["conv"], c["marks"], ends),
            [((count, 3 * width), BF), ((SUB, 3 * width), F32), ((ROWS, 3 * width), F32),
             ((9 * SUB, width), F32), ((SUB, width), F32), (st_shape, F32), (st_shape, F32)],
            [zs, ((count + SUB, 3 * width), F32), (seq_shape, F32),
             (((SPAN + 1) * st_shape[0] * SUB, LANE), F32), (st_shape, F32)],
            4, "mixer_back", 12 * work, (*partial_grads, *gu_turn) if m else (*gu_halves, gu_chip),
        )
        rim_back = lax.ppermute(rim_back[:2], "seq", [(i + 1, i) for i in range(n_seq - 1)])
        if m == 0:
            gu_turn = grad_turn(gu_chip, gu_far, X, (rim_back,))
            g_gu = grad_own(gu_chip, gu_turn)
        tail = tied(tail, g_gu if m else gu_far)
        tail = (tail + jnp.concatenate([jnp.zeros((ROWS - 2, 3 * width), F32), rim_back])).astype(BF)
        d_z = lax.dynamic_update_slice(d_z, tail, (count - ROWS, 0))
        c["d_z"] = d_z
        gain = gain_in
        if m == micros - 1:
            in_halves = grad_halves([h_in[i] for i in range(micros)], each("d_z"), "grad_in")
            gain = tied(gain_in, in_halves[0])
        d_h_in = dot(d_z, in_full, ((1,), (1,)))
        d_norm, d_gain_in = norm_back(x_full[m].astype(F32), scale_in[m], gain, d_h_in)
        smalls.append((d_taps, d_lam, d_res, d_skip))
        gains = [d_gain_in, c["d_gain_mlp"]] if m == 0 else [gains[0] + d_gain_in, gains[1] + c["d_gain_mlp"]]
        if m == micros - 1:
            gains = tp_sum(jnp.concatenate(gains).reshape(-1, width).astype(BF))
            d_taps, d_lam, d_res, d_skip = (sum(parts) for parts in zip(*smalls))
            g_real, g_imag = unpacked(d_lam, log_rate.shape)
            s_real, s_imag = unpacked(d_res, log_rate.shape)
            h_real = residues[0] * g_real + residues[1] * g_imag
            h_imag = residues[0] * g_imag - residues[1] * g_real
            small = jnp.concatenate([
                jnp.sum(d_taps.reshape(9, SUB, width), axis=1),
                -rate * (lam_real * h_real + lam_imag * h_imag),
                lam_real * h_imag - lam_imag * h_real,
                s_real, -s_imag,
                jnp.sum(d_skip, axis=0, keepdims=True),
                gains,
            ])
            small = jnp.sum(lax.all_gather(small.astype(BF), "seq").astype(F32), axis=0)
            d_norm = tied(d_norm, small)
        partial_grads.append((c["d_mid"] + d_norm).astype(BF))
        token_grads.append(scatter(partial_grads[m], "tp", 1))

    in_chip = grad_chip(in_halves)
    in_far = grad_far(in_chip, Y, (small,))
    g_in = grad_own(in_chip, grad_turn(in_chip, in_far, Y, (small,)))
    g_down = grad_own(down_chip, down_turn, (in_far,))
    gains = small[-gains.shape[0] :]
    n_gain = gains.shape[0]
    n_pole = log_rate.shape[0]
    cuts = [9, 9 + n_pole, 9 + 2 * n_pole, 9 + 3 * n_pole, 9 + 4 * n_pole]
    return (
        jnp.stack([(mid + tied(down.astype(F32), in_far)).astype(BF) for mid, down in outputs]),
        jnp.stack(token_grads),
        gains[: n_gain // 2].reshape(-1),
        g_in.reshape(w_in.shape),
        small[: cuts[0]].reshape(conv_taps.shape),
        small[cuts[0] : cuts[1]],
        small[cuts[1] : cuts[2]],
        small[cuts[2] : cuts[4]].reshape(residues.shape),
        small[cuts[4]],
        tied(g_out.astype(F32), in_far).T,
        gains[n_gain // 2 :].reshape(-1),
        tied(g_gu, in_far).reshape(w_gu.shape),
        g_down.T,
    )


def solution(mesh):
    wide, deep, flat = P(None, "seq", "tp"), P("seq", None, "tp"), P("tp", "seq")
    poles, taps = P(None, "tp"), P(None, None, "tp")
    return jax.shard_map(
        shards,
        mesh=mesh,
        in_specs=(wide, P(), P(None, "seq"), P(), deep, taps, poles, poles, taps, P("tp"), flat,
                  P(), deep, flat, wide),
        out_specs=(wide, wide, P(), deep, taps, poles, poles, taps, P("tp"), flat, P(), deep, flat),
        check_vma=False,
    )
```
